32 devices in a mesh: rows: 4 (over x, core), heads: 8 (over z, y).
Axes of the slice: x: 2, y: 2, z: 4, core: 2. Of those that a mesh axis runs over, the one named last changes fastest.
Arguments:
- tokens: bfloat16 [24576, 1024], P(('rows', 'heads')), may hold values from -6 to 6
- cotangent: bfloat16 [24576, 1024], P(('rows', 'heads')), may hold values from -6 to 6
- domain: int32 [12], P('rows'), may hold values from 0 to 3
- group_weight: float32 [4], replicated, may hold values from 0.25 to 4
- gain_attn: bfloat16 [1024], replicated, may hold values from 0.5 to 1.5
- w_query: bfloat16 [1024, 1024], P(None, 'heads'), may hold values from -0.25 to 0.25
- w_query_rope: bfloat16 [1024, 512], P(None, 'heads'), may hold values from -0.25 to 0.25
- w_latent: bfloat16 [1024, 512], replicated, may hold values from -0.1875 to 0.1875
- w_key_rope: bfloat16 [1024, 32], replicated, may hold values from -0.1875 to 0.1875
- w_key_up: bfloat16 [256, 1024], P(None, 'heads'), may hold values from -0.375 to 0.375
- w_value_up: bfloat16 [256, 1024], P(None, 'heads'), may hold values from -0.375 to 0.375
- w_out: bfloat16 [1024, 1024], P('heads'), may hold values from -0.75 to 0.75
- gain_mlp: bfloat16 [1024], replicated, may hold values from 0.5 to 1.5
- w_gate: bfloat16 [1024, 2816], P(None, 'heads'), may hold values from -0.1875 to 0.1875
- w_up: bfloat16 [1024, 2816], P(None, 'heads'), may hold values from -0.1875 to 0.1875
- w_down: bfloat16 [2816, 1024], P('heads'), may hold values from -0.109375 to 0.109375
Outputs:
- block_output: bfloat16 [24576, 1024], P(('rows', 'heads'))
- grad_tokens: float32 [24576, 1024], P(('rows', 'heads'))
- grad_gain_attn: float32 [1024], P(('rows', 'heads'))
- grad_query: float32 [1024, 1024], P('rows', 'heads')
- grad_query_rope: float32 [1024, 512], P('rows', 'heads')
- grad_latent: float32 [1024, 512], P(('rows', 'heads'))
- grad_key_rope: float32 [1024, 32], P(('rows', 'heads'))
- grad_key_up: float32 [256, 1024], P('rows', 'heads')
- grad_value_up: float32 [256, 1024], P('rows', 'heads')
- grad_out: float32 [1024, 1024], P('heads', 'rows')
- grad_gain_mlp: float32 [1024], P(('rows', 'heads'))
- grad_gate: float32 [1024, 2816], P('rows', 'heads')
- grad_up: float32 [1024, 2816], P('rows', 'heads')
- grad_down: float32 [2816, 1024], P('heads', 'rows')
The draws below stay inside these ranges and needn't reach their ends.
All inputs are finite; a program needn't handle non-finite values.
Results may differ from the reference program's by a relative error of at most 0.018.
Values may be sent and summed in bfloat16 or wider, within the bound.
A program may use at most 256 MiB of HBM per device.

```python
import math
import jax
import jax.numpy as jnp
from jax import lax

D = 1024
HEADS = 16
HD = 64
LGROUPS = 2
LAT = 256
RD = 32
FF = 2816
GROUPS = 4
LEN = 2048
SEQS = 12
TOKENS = 24576


def place_ends(result, stream_key, least, high):
    index_at = [jax.random.randint(jax.random.fold_in(stream_key, axis), (), 0, length) for axis, length in enumerate(result.shape)]
    widest = result.shape.index(max(result.shape))
    neighbour = index_at[:widest] + [(index_at[widest] + 1) % result.shape[widest]] + index_at[widest + 1:]
    return result.at[tuple(index_at)].set(least).at[tuple(neighbour)].set(high)


def shard_levels(own_key, shape, pieces, smallest, top_value):
    gain = 1.0
    for axis_at, blocks in pieces:
        steps = jax.random.uniform(jax.random.fold_in(jax.random.fold_in(own_key, 6), axis_at), (blocks,), jnp.float32, smallest / len(pieces), top_value / len(pieces))
        gain = gain * jnp.repeat(jnp.exp(steps), shape[axis_at] // blocks).reshape((-1,) + (1,) * (len(shape) - 1 - axis_at))
    return gain


def bell_draw(rng, dims, deviation, most, shards=(), held_as=jnp.bfloat16):
    result = jax.random.normal(rng, dims, jnp.float32) * deviation
    if len(shards) > 0:
        result = shard_levels(rng, dims, shards, -0.22, 0.18) * result
    return jnp.clip(result, min=-most, max=most).astype(held_as)


def setup_inputs(seed: int = 0) -> dict:
    key_of = jax.random.split(jax.random.key(seed), 17)
    return {
        "tokens": bell_draw(key_of[0], (TOKENS, D), 1.0, 6.0, ((0, 32),)),
        "cotangent": bell_draw(key_of[1], (TOKENS, D), 1.0, 6.0, ((0, 32),)),
        "domain": place_ends(jax.random.randint(key_of[2], (SEQS,), 0, GROUPS), jax.random.fold_in(key_of[2], 1), 0, GROUPS - 1).astype(jnp.int32),
        "group_weight": jnp.clip(jnp.exp(jax.random.uniform(key_of[3], (GROUPS,), jnp.float32, math.log(0.25), math.log(4.0))), 0.25, 4.0),
        "gain_attn": jnp.clip(1.0 + 0.1 * jax.random.normal(key_of[4], (D,), jnp.float32), 0.5, 1.5).astype(jnp.bfloat16),
        "w_query": bell_draw(key_of[5], (D, HEADS * HD), (D // 2) ** -0.5, 0.25, ((1, 8),)),
        "w_query_rope": bell_draw(key_of[6], (D, HEADS * RD), (D // 2) ** -0.5, 0.25, ((1, 8),)),
        "w_latent": bell_draw(key_of[7], (D, LGROUPS * LAT), D ** -0.5, 0.1875),
        "w_key_rope": bell_draw(key_of[8], (D, RD), D ** -0.5, 0.1875),
        "w_key_up": bell_draw(key_of[9], (LAT, HEADS * HD), LAT ** -0.5, 0.375, ((1, 8),)),
        "w_value_up": bell_draw(key_of[10], (LAT, HEADS * HD), LAT ** -0.5, 0.375, ((1, 8),)),
        "w_out": bell_draw(key_of[11], (HEADS * HD, D), HD ** -0.5, 0.75, ((0, 8),)),
        "gain_mlp": jnp.clip(1.0 + 0.1 * jax.random.normal(key_of[12], (D,), jnp.float32), 0.5, 1.5).astype(jnp.bfloat16),
        "w_gate": bell_draw(key_of[13], (D, FF), D ** -0.5, 0.1875, ((1, 8),)),
        "w_up": bell_draw(key_of[14], (D, FF), D ** -0.5, 0.1875, ((1, 8),)),
        "w_down": bell_draw(key_of[15], (FF, D), FF ** -0.5, 0.109375, ((0, 8),)),
    }


EPS = 1e-05
THETA = 10000.0
NEG_LARGE = -1e+30

@jax.custom_vjp
def low(v):
    return lax.optimization_barrier(v.astype(jnp.bfloat16)).astype(jnp.float32)

@jax.custom_vjp
def low_back(v):
    return v

def low_keep(v):
    return (low(v), None)

def low_pass(kept, grad):
    return (grad,)

def back_keep(v):
    return (v, None)

def back_low(kept, grad):
    return (low(grad),)
low.defvjp(low_keep, low_pass)
low_back.defvjp(back_keep, back_low)

def both_ways(value):
    return low_back(low(value))

def matmul(left, right):
    return jnp.dot(left, right, precision=lax.Precision.HIGHEST)

def rms_scale(values):
    return lax.rsqrt(lax.optimization_barrier(jnp.mean(values * values, axis=-1, keepdims=True)) + EPS)

def rotary(seq_len, half_dim):
    positions = jnp.arange(seq_len).astype(jnp.float32)
    frequency = THETA ** (-jnp.arange(half_dim).astype(jnp.float32) / half_dim)
    angles = positions[:, None] * frequency[None, :]
    return (jnp.cos(angles), jnp.sin(angles))

def rotate(values, cosine, sine_table):
    half_dim = values.shape[-1] // 2
    front_half = values[..., :half_dim]
    back_half = values[..., half_dim:]
    return jnp.concatenate([front_half * cosine - back_half * sine_table, back_half * cosine + front_half * sine_table], axis=-1)

def attend_block(query_block, rope_block, key_heads, key_rope, value_heads, offset):
    scores = jnp.einsum('qhd,khd->hqk', query_block, key_heads, precision=lax.Precision.HIGHEST)
    scores = scores + jnp.einsum('qhr,khr->hqk', rope_block, key_rope, precision=lax.Precision.HIGHEST)
    scores = low_back(scores * (HD + RD) ** (-0.5))
    rows_at = offset + jnp.arange(query_block.shape[0]).astype(jnp.int32)
    cols_at = jnp.arange(key_heads.shape[0]).astype(jnp.int32)
    scores = jnp.where((cols_at[None, :] <= rows_at[:, None])[None], scores, NEG_LARGE)
    row_max = lax.optimization_barrier(jnp.max(scores, axis=-1, keepdims=True))
    exp_terms = jnp.exp(scores - row_max)
    attention = exp_terms / lax.optimization_barrier(jnp.sum(exp_terms, axis=-1, keepdims=True))
    return jnp.einsum('hqk,khd->qhd', low(attention), value_heads, precision=lax.Precision.HIGHEST)

def block_layer(params, tokens_seq):
    gain_attn, w_query, w_query_rope, w_latent, w_key_rope, w_key_up, w_value_up, w_out, gain_mlp, w_gate, w_up, w_down = params
    seq_len = tokens_seq.shape[0]
    cosine, sine_table = rotary(seq_len, RD // 2)
    cosine = cosine[:, None, :]
    sine_table = sine_table[:, None, :]
    normed = low(tokens_seq * rms_scale(tokens_seq) * gain_attn)
    query_heads = both_ways(matmul(normed, w_query)).reshape(seq_len, HEADS, HD)
    query_raw = low_back(matmul(normed, w_query_rope)).reshape(seq_len, HEADS, RD)
    query_rope = both_ways(rotate(query_raw, cosine, sine_table))
    latent = matmul(normed, w_latent).reshape(seq_len, LGROUPS, LAT)
    group_of = (jnp.arange(HEADS) // (HEADS // LGROUPS)).astype(jnp.int32)
    latent_heads = both_ways(latent[:, group_of, :])
    key_raw = matmul(normed, w_key_rope)
    key_copies = low_back(jnp.broadcast_to(key_raw[:, None, :], (seq_len, HEADS, RD)))
    key_rope = both_ways(rotate(key_copies, cosine, sine_table))
    key_heads = both_ways(jnp.einsum('lhc,chd->lhd', latent_heads, w_key_up.reshape(LAT, HEADS, HD), precision=lax.Precision.HIGHEST))
    value_heads = both_ways(jnp.einsum('lhc,chd->lhd', latent_heads, w_value_up.reshape(LAT, HEADS, HD), precision=lax.Precision.HIGHEST))
    block_rows = min(512, seq_len)
    starts = (jnp.arange(seq_len // block_rows) * block_rows).astype(jnp.int32)

    def one_block(offset):
        query_block = lax.dynamic_slice_in_dim(query_heads, offset, block_rows, 0)
        rope_block = lax.dynamic_slice_in_dim(query_rope, offset, block_rows, 0)
        return attend_block(query_block, rope_block, key_heads, key_rope, value_heads, offset)
    mixed_heads = lax.map(jax.checkpoint(one_block), starts).reshape(seq_len, HEADS * HD)
    hidden = tokens_seq + low_back(matmul(both_ways(mixed_heads), w_out))
    normed_mlp = low(hidden * rms_scale(hidden) * gain_mlp)
    gate_act = low_back(matmul(normed_mlp, w_gate))
    up_act = low_back(matmul(normed_mlp, w_up))
    inner_act = low(jax.nn.silu(gate_act) * up_act)
    return hidden + low_back(matmul(inner_act, w_down))

def reference(tokens, cotangent, domain, group_weight, gain_attn, w_query, w_query_rope, w_latent, w_key_rope, w_key_up, w_value_up, w_out, gain_mlp, w_gate, w_up, w_down):
    params = tuple((weight.astype(jnp.float32) for weight in (gain_attn, w_query, w_query_rope, w_latent, w_key_rope, w_key_up, w_value_up, w_out, gain_mlp, w_gate, w_up, w_down)))
    seq_weight = lax.optimization_barrier(jnp.sum((domain[:, None] == jnp.arange(GROUPS).astype(jnp.int32)[None, :]).astype(jnp.float32) * group_weight.astype(jnp.float32)[None, :], axis=1))
    tokens_all = tokens.astype(jnp.float32).reshape(SEQS, LEN, D)
    cotangent_all = cotangent.astype(jnp.float32).reshape(SEQS, LEN, D)

    def per_seq(totals, inputs):
        tokens_seq, cotangent_seq, weight_seq = inputs
        output, pullback = jax.vjp(block_layer, params, tokens_seq)
        grad_params, grad_seq = pullback(cotangent_seq * weight_seq)
        totals = jax.tree.map(lambda summed, addend: summed + addend, totals, grad_params)
        return (totals, (output.astype(jnp.bfloat16), grad_seq))
    initial = jax.tree.map(jnp.zeros_like, params)
    totals, (outputs, grads_in) = lax.scan(per_seq, initial, (tokens_all, cotangent_all, seq_weight))
    return (outputs.reshape(TOKENS, D), grads_in.reshape(TOKENS, D), totals[0], totals[1], totals[2], totals[3], totals[4], totals[5], totals[6], totals[7], totals[8], totals[9], totals[10], totals[11])
```

```python
import functools
import math

import jax
import jax.numpy as jnp
from jax import lax
from jax.experimental import pallas as pl
from jax.experimental.pallas import tpu as pltpu
from jax.sharding import PartitionSpec as P

D = 1024
HEADS = 16
HD = 64
LGROUPS = 2
LAT = 256
RD = 32
LEN = 2048
EPS = 1e-05
THETA = 10000.0
NEG_LARGE = -1e30
LANES = 128
PAIR = 2
LOG2E = math.log2(math.e)
LN2 = math.log(2.0)
SCALE = (HD + RD) ** (-0.5)

bf16 = jnp.bfloat16
f32 = jnp.float32


def dot_nn(a, b):
    return jnp.dot(a, b, preferred_element_type=f32)


def dot_nt(a, b):
    return lax.dot_general(a, b, (((1,), (1,)), ((), ())), preferred_element_type=f32)


def dot_tn(a, b):
    return lax.dot_general(a, b, (((0,), (0,)), ((), ())), preferred_element_type=f32)


def rms_scale(values):
    return lax.rsqrt(jnp.mean(values * values, axis=-1, keepdims=True) + EPS)


def norm_backward(source, scale_rows, gain, grad_normed):
    scaled = source * scale_rows
    weighted = grad_normed * gain
    grad_source = scale_rows * (
        weighted - scaled * jnp.mean(weighted * scaled, axis=-1, keepdims=True)
    )
    return (grad_source, jnp.sum(grad_normed * scaled, axis=0))


def attend_forward_kernel(
    block, own, halo, place_ref, q_ref, latent_ref, rope_ref, up_ref, mixed_ref, log_ref, key_s, value_s
):
    total = halo + own

    def prepare(index, _):
        rows = pl.ds(pl.multiple_of(index * block, block), block)
        latent = latent_ref[rows, :]
        lane = lax.broadcasted_iota(jnp.int32, (block, LANES), 1)
        for e in range(PAIR):
            both = dot_nn(latent, up_ref[:, e * LANES : (e + 1) * LANES]).astype(bf16)
            key_s[e, rows, :] = jnp.where(lane < HD, both, rope_ref[rows, :])
            value_s[e, index] = both[:, HD:].T
        return 0

    lax.fori_loop(halo - place_ref[0], total, prepare, 0)
    keep = lax.broadcasted_iota(jnp.int32, (block, block), 0) <= lax.broadcasted_iota(
        jnp.int32, (block, block), 1
    )
    for j in range(own):
        at = halo + j
        cols = slice(j * block, (j + 1) * block)
        queries = [q_ref[cols, e * LANES : (e + 1) * LANES].T for e in range(PAIR)]
        state = []
        for e in range(PAIR):
            scores = dot_nn(key_s[e, at * block : (at + 1) * block, :], queries[e])
            scores = jnp.where(keep, scores, NEG_LARGE)
            top = jnp.max(scores, axis=0, keepdims=True)
            terms = jnp.exp2(scores - top)
            sums = jnp.sum(terms, axis=0, keepdims=True)
            state += [top, sums, dot_nn(value_s[e, at], terms.astype(bf16))]

        def step(index, held):
            rows = pl.ds(pl.multiple_of(index * block, block), block)
            out = []
            for e in range(PAIR):
                top, sums, mixed = held[3 * e : 3 * e + 3]
                scores = dot_nn(key_s[e, rows, :], queries[e])
                higher = jnp.maximum(top, jnp.max(scores, axis=0, keepdims=True))
                shrink = jnp.exp2(top - higher)
                terms = jnp.exp2(scores - higher)
                sums = sums * shrink + jnp.sum(terms, axis=0, keepdims=True)
                mixed = mixed * shrink + dot_nn(value_s[e, index], terms.astype(bf16))
                out += [higher, sums, mixed]
            return tuple(out)

        state = lax.fori_loop(at - place_ref[j], at, step, tuple(state))
        for e in range(PAIR):
            top, sums, mixed = state[3 * e : 3 * e + 3]
            mixed_ref[e * HD : (e + 1) * HD, cols] = (mixed / sums).astype(bf16)
            log_ref[e, :, cols] = top + jnp.log2(sums)


def attend_forward(places, queries, window, up_weight, block, own, halo):
    rows, wide = own * block, (halo + own) * block
    steps = HEADS // LGROUPS // PAIR
    return pl.pallas_call(
        functools.partial(attend_forward_kernel, block, own, halo),
        grid_spec=pltpu.PrefetchScalarGridSpec(
            num_scalar_prefetch=1,
            grid=(HEADS // PAIR,),
            in_specs=[
                pl.BlockSpec((rows, PAIR * LANES), lambda h, p: (0, h)),
                pl.BlockSpec((wide, LAT), lambda h, p: (0, h // steps)),
                pl.BlockSpec((wide, LANES), lambda h, p: (0, LGROUPS * LAT // LANES)),
                pl.BlockSpec((LAT, PAIR * LANES), lambda h, p: (0, h)),
            ],
            out_specs=[
                pl.BlockSpec((PAIR * HD, rows), lambda h, p: (h, 0)),
                pl.BlockSpec((PAIR, 1, rows), lambda h, p: (h, 0, 0)),
            ],
            scratch_shapes=[
                pltpu.VMEM((PAIR, wide, LANES), bf16),
                pltpu.VMEM((PAIR, halo + own, HD, block), bf16),
            ],
        ),
        out_shape=[
            jax.ShapeDtypeStruct((HEADS * HD, rows), bf16),
            jax.ShapeDtypeStruct((HEADS, 1, rows), f32),
        ],
        compiler_params=pltpu.CompilerParams(vmem_limit_bytes=48 << 20),
        name="attend_forward",
    )(places, queries, window, window, up_weight)


def attend_backward_kernel(
    block, own, halo, steps, place_ref, q_ref, latent_ref, rope_ref, up_ref, mixed_ref, log_ref,
    grad_ref, cos_ref, low_ref, high_ref, dq_ref, dlatent_ref, drope_ref, dup_ref,
    key_s, key_t_s, value_s, dkey_s, dvalue_s,
):
    h = pl.program_id(0)
    total = halo + own
    first = halo - place_ref[0]

    @pl.when(h == 0)
    def _():
        drope_ref[...] = jnp.zeros_like(drope_ref)

    @pl.when(h % steps == 0)
    def _():
        dlatent_ref[...] = jnp.zeros_like(dlatent_ref)

    lane = lax.broadcasted_iota(jnp.int32, (block, LANES), 1)

    def prepare(index, _):
        rows = pl.ds(pl.multiple_of(index * block, block), block)
        latent = latent_ref[rows, :]
        for e in range(PAIR):
            both = dot_nn(latent, up_ref[:, e * LANES : (e + 1) * LANES]).astype(bf16)
            keys = jnp.where(lane < HD, both, rope_ref[rows, :])
            key_s[e, rows, :] = keys
            key_t_s[e, index] = keys.T
            value_s[e, rows, :] = both[:, HD:]
            dkey_s[e, rows, :] = jnp.zeros((block, LANES), f32)
            dvalue_s[e, rows, :] = jnp.zeros((block, LANES), f32)
        return 0

    lax.fori_loop(first, total, prepare, 0)
    keep = lax.broadcasted_iota(jnp.int32, (block, block), 0) <= lax.broadcasted_iota(
        jnp.int32, (block, block), 1
    )
    for j in range(own):
        at = halo + j
        cols = slice(j * block, (j + 1) * block)
        queries = [q_ref[cols, e * LANES : (e + 1) * LANES] for e in range(PAIR)]
        queries_t = [q.T for q in queries]
        grads_t = [grad_ref[e * HD : (e + 1) * HD, cols] for e in range(PAIR)]
        grads = [jnp.concatenate([jnp.zeros((block, HD), bf16), g.T], axis=1) for g in grads_t]
        logs = [log_ref[e, :, cols] for e in range(PAIR)]
        inner = [
            jnp.sum(
                grads_t[e].astype(f32) * mixed_ref[e * HD : (e + 1) * HD, cols].astype(f32),
                axis=0,
                keepdims=True,
            )
            for e in range(PAIR)
        ]

        def tile(index, held, masked):
            rows = pl.ds(pl.multiple_of(index * block, block), block)
            out = []
            for e in range(PAIR):
                scores = dot_nn(key_s[e, rows, :], queries_t[e])
                if masked:
                    scores = jnp.where(keep, scores, NEG_LARGE)
                probs = jnp.exp2(scores - logs[e])
                grad_probs = dot_nn(value_s[e, rows, :], grads_t[e])
                grad_scores = (probs * (grad_probs - inner[e])).astype(bf16)
                dvalue_s[e, rows, :] += dot_nn(probs.astype(bf16), grads[e])
                dkey_s[e, rows, :] += dot_nn(grad_scores, queries[e])
                out.append(held[e] + dot_nn(key_t_s[e, index], grad_scores))
            return tuple(out)

        held = tile(at, tuple(jnp.zeros((LANES, block), f32) for _ in range(PAIR)), True)
        held = lax.fori_loop(
            at - place_ref[j], at, lambda index, held: tile(index, held, False), held
        )
        for e in range(PAIR):
            grad = held[e].T * SCALE
            grad = (
                grad * cos_ref[cols, :]
                + pltpu.roll(grad, RD // 2, 1) * low_ref[cols, :]
                + pltpu.roll(grad, LANES - RD // 2, 1) * high_ref[cols, :]
            )
            dq_ref[cols, e * LANES : (e + 1) * LANES] = grad.astype(bf16)
    dup_ref[...] = jnp.zeros_like(dup_ref)

    def finish(index, _):
        rows = pl.ds(pl.multiple_of(index * block, block), block)
        latent_t = latent_ref[rows, :].T
        grad_latent = None
        grad_rope = None
        for e in range(PAIR):
            grad_key = dkey_s[e, rows, :] * LN2
            both = jnp.where(lane < HD, grad_key, dvalue_s[e, rows, :]).astype(bf16)
            part = dot_nt(both, up_ref[:, e * LANES : (e + 1) * LANES])
            grad_latent = part if grad_latent is None else grad_latent + part
            grad_rope = grad_key if grad_rope is None else grad_rope + grad_key
            dup_ref[:, e * LANES : (e + 1) * LANES] += dot_nn(latent_t, both)
        dlatent_ref[rows, :] += grad_latent
        drope_ref[rows, :] += grad_rope
        return 0

    lax.fori_loop(first, total, finish, 0)


def attend_backward(
    places, queries, window, up_weight, mixed, logs, grad_mixed, cos_t, low_t, high_t, block, own, halo
):
    rows, wide = own * block, (halo + own) * block
    steps = HEADS // LGROUPS // PAIR
    table = pl.BlockSpec((rows, LANES), lambda h, p: (0, 0))
    return pl.pallas_call(
        functools.partial(attend_backward_kernel, block, own, halo, steps),
        grid_spec=pltpu.PrefetchScalarGridSpec(
            num_scalar_prefetch=1,
            grid=(HEADS // PAIR,),
            in_specs=[
                pl.BlockSpec((rows, PAIR * LANES), lambda h, p: (0, h)),
                pl.BlockSpec((wide, LAT), lambda h, p: (0, h // steps)),
                pl.BlockSpec((wide, LANES), lambda h, p: (0, LGROUPS * LAT // LANES)),
                pl.BlockSpec((LAT, PAIR * LANES), lambda h, p: (0, h)),
                pl.BlockSpec((PAIR * HD, rows), lambda h, p: (h, 0)),
                pl.BlockSpec((PAIR, 1, rows), lambda h, p: (h, 0, 0)),
                pl.BlockSpec((PAIR * HD, rows), lambda h, p: (h, 0)),
                table,
                table,
                table,
            ],
            out_specs=[
                pl.BlockSpec((rows, PAIR * LANES), lambda h, p: (0, h)),
                pl.BlockSpec((wide, LAT), lambda h, p: (0, h // steps)),
                pl.BlockSpec((wide, LANES), lambda h, p: (0, 0)),
                pl.BlockSpec((LAT, PAIR * LANES), lambda h, p: (0, h)),
            ],
            scratch_shapes=[
                pltpu.VMEM((PAIR, wide, LANES), bf16),
                pltpu.VMEM((PAIR, halo + own, LANES, block), bf16),
                pltpu.VMEM((PAIR, wide, HD), bf16),
                pltpu.VMEM((PAIR, wide, LANES), f32),
                pltpu.VMEM((PAIR, wide, LANES), f32),
            ],
        ),
        out_shape=[
            jax.ShapeDtypeStruct((rows, HEADS * LANES), bf16),
            jax.ShapeDtypeStruct((wide, LGROUPS * LAT), f32),
            jax.ShapeDtypeStruct((wide, LANES), f32),
            jax.ShapeDtypeStruct((LAT, HEADS * LANES), f32),
        ],
        compiler_params=pltpu.CompilerParams(vmem_limit_bytes=56 << 20),
        name="attend_backward",
    )(places, queries, window, window, up_weight, mixed, logs, grad_mixed, cos_t, low_t, high_t)


def project_kernel(normed_ref, weight_ref, cos_ref, sin_ref, out_ref):
    raw = dot_nn(normed_ref[...], weight_ref[...])
    for e in range(PAIR):
        part = raw[:, e * LANES : (e + 1) * LANES]
        part = part * cos_ref[...] + pltpu.roll(part, LANES - RD, 1) * sin_ref[...]
        out_ref[:, e * LANES : (e + 1) * LANES] = part.astype(bf16)


def project_queries(normed, weight, cos_t, sin_t):
    rows = normed.shape[0]
    table = pl.BlockSpec((rows, LANES), lambda h: (0, 0))
    return pl.pallas_call(
        project_kernel,
        grid=(HEADS // PAIR,),
        in_specs=[
            pl.BlockSpec((rows, D), lambda h: (0, 0)),
            pl.BlockSpec((D, PAIR * LANES), lambda h: (0, h)),
            table,
            table,
        ],
        out_specs=pl.BlockSpec((rows, PAIR * LANES), lambda h: (0, h)),
        out_shape=jax.ShapeDtypeStruct((rows, HEADS * LANES), bf16),
        compiler_params=pltpu.CompilerParams(vmem_limit_bytes=40 << 20),
        name="project_queries",
    )(normed, weight, cos_t, sin_t)


def feed_kernel(cuts, shards, units, normed_ref, grad_ref, weight_ref, out_ref, dnormed_ref, dweight_ref):
    def whole(which):
        return jnp.concatenate(
            [
                jnp.concatenate(
                    [weight_ref[q, t, which * units : (which + 1) * units, :] for q in range(cuts)],
                    axis=1,
                )
                for t in range(shards)
            ],
            axis=0,
        )

    def put(which, grad):
        wide = D // cuts
        for t in range(shards):
            for q in range(cuts):
                dweight_ref[q, t, which * units : (which + 1) * units, :] = grad[
                    t * units : (t + 1) * units, q * wide : (q + 1) * wide
                ].astype(bf16)

    @pl.when(pl.program_id(0) == 0)
    def _():
        out_ref[...] = jnp.zeros_like(out_ref)
        dnormed_ref[...] = jnp.zeros_like(dnormed_ref)

    normed = normed_ref[...]
    grad = grad_ref[...]
    w_gate, w_up, w_down = whole(0), whole(1), whole(2)
    gate = dot_nt(w_gate, normed)
    upper = dot_nt(w_up, normed)
    grad_inner = dot_nt(w_down, grad)
    sig = jax.nn.sigmoid(gate)
    silu = gate * sig
    inner = (silu * upper).astype(bf16)
    grad_gate = (grad_inner * upper * sig * (1.0 + gate * (1.0 - sig))).astype(bf16)
    grad_upper = (grad_inner * silu).astype(bf16)
    out_ref[...] += dot_tn(inner, w_down)
    dnormed_ref[...] += dot_tn(grad_gate, w_gate)
    dnormed_ref[...] += dot_tn(grad_upper, w_up)
    put(0, dot_nn(grad_gate, normed))
    put(1, dot_nn(grad_upper, normed))
    put(2, dot_nn(inner, grad))


def feed_forward_both(normed, grad, weights, units):
    rows = normed.shape[0]
    cuts, pieces, tall, wide = weights.shape
    shards = max(1, min(pieces, 704 // units))
    once = pl.Buffered(1)
    return pl.pallas_call(
        functools.partial(feed_kernel, cuts, shards, units),
        grid=(pieces // shards,),
        in_specs=[
            pl.BlockSpec((rows, D), lambda f: (0, 0), pipeline_mode=once),
            pl.BlockSpec((rows, D), lambda f: (0, 0), pipeline_mode=once),
            pl.BlockSpec((cuts, shards, tall, wide), lambda f: (0, f, 0, 0)),
        ],
        out_specs=[
            pl.BlockSpec((rows, D), lambda f: (0, 0), pipeline_mode=once),
            pl.BlockSpec((rows, D), lambda f: (0, 0), pipeline_mode=once),
            pl.BlockSpec((cuts, shards, 3 * units, wide), lambda f: (0, f, 0, 0)),
        ],
        out_shape=[
            jax.ShapeDtypeStruct((rows, D), f32),
            jax.ShapeDtypeStruct((rows, D), f32),
            jax.ShapeDtypeStruct((cuts, pieces, 3 * units, wide), bf16),
        ],
        compiler_params=pltpu.CompilerParams(vmem_limit_bytes=60 << 20),
        name="feed_forward_both",
    )(normed, grad, weights)


def bits_of(size):
    return size.bit_length() - 1


def bit_pairs(size, bit):
    return [(i, i ^ (1 << bit)) for i in range(size)]


def gather_all(piece, shape):
    lead = []
    for axis in ("heads", "rows"):
        for bit in range(bits_of(shape[axis])):
            other = lax.ppermute(piece, axis, bit_pairs(shape[axis], bit))
            upper = (lax.axis_index(axis) >> bit) & 1
            piece = jnp.stack(
                [jnp.where(upper == 1, other, piece), jnp.where(upper == 1, piece, other)]
            )
            lead.append((axis, bit))
    tail = len(piece.shape) - len(lead)
    lead = lead[::-1]
    wanted = [("rows", b) for b in reversed(range(bits_of(shape["rows"])))]
    wanted += [("heads", b) for b in reversed(range(bits_of(shape["heads"])))]
    order = [lead.index(w) for w in wanted] + [len(lead) + i for i in range(tail)]
    whole = piece.transpose(order)
    return whole.reshape((shape["rows"], shape["heads"]) + whole.shape[len(lead) :])


def scatter_all(parts, shape):
    row_bits, head_bits = bits_of(shape["rows"]), bits_of(shape["heads"])
    tails = [part.shape[2:] for part in parts]
    lead = [("rows", b) for b in reversed(range(row_bits))]
    lead += [("heads", b) for b in reversed(range(head_bits))]
    parts = [part.reshape((2,) * len(lead) + tail) for part, tail in zip(parts, tails)]
    for axis, count in (("rows", row_bits), ("heads", head_bits)):
        for bit in range(count):
            at = lead.index((axis, bit))
            upper = (lax.axis_index(axis) >> bit) & 1
            sent = [lax.dynamic_index_in_dim(part, 1 - upper, at, keepdims=False) for part in parts]
            kept = [lax.dynamic_index_in_dim(part, upper, at, keepdims=False) for part in parts]
            got = [lax.ppermute(part, axis, bit_pairs(shape[axis], bit)) for part in sent]
            parts = [
                (a.astype(f32) + b.astype(f32)).astype(part.dtype)
                for a, b, part in zip(kept, got, parts)
            ]
            lead.pop(at)
    return parts


def lane_table(rows, entries):
    columns = []
    for width, value in entries:
        columns.append(
            jnp.full((rows, width), value, f32) if isinstance(value, float) else value
        )
    return jnp.concatenate(columns, axis=1)


def on_device(
    shape,
    tokens,
    cotangent,
    domain,
    group_weight,
    gain_attn,
    w_query,
    w_query_rope,
    w_latent,
    w_key_rope,
    w_key_up,
    w_value_up,
    w_out,
    gain_mlp,
    w_gate,
    w_up,
    w_down,
):
    n_rows, n_heads = shape["rows"], shape["heads"]
    row_at, head_at = lax.axis_index("rows"), lax.axis_index("heads")
    local = tokens.shape[0]
    block = math.gcd(local, LEN)
    own, halo = local // block, LEN // block - 1
    heads_here = w_query.shape[1] // HD
    units = w_gate.shape[1]
    cut = D // n_rows

    half = RD // 2
    rope_here = w_query_rope.reshape(D, heads_here, RD)
    query_here = jnp.concatenate(
        [
            w_query.reshape(D, heads_here, HD),
            rope_here,
            -rope_here[:, :, half:],
            rope_here[:, :, :half],
        ],
        axis=2,
    ).reshape(D, heads_here * LANES)
    up_here = jnp.concatenate(
        [w_key_up.reshape(LAT, heads_here, HD), w_value_up.reshape(LAT, heads_here, HD)], axis=2
    ).reshape(LAT, heads_here * LANES)
    small = jnp.concatenate([query_here, up_here], axis=0)
    tall = small.shape[0]
    small_piece = lax.dynamic_slice_in_dim(small, row_at * (tall // n_rows), tall // n_rows, 0)
    small_all = gather_all(small_piece, shape).transpose(0, 2, 1, 3).reshape(tall, HEADS * LANES)
    query_weight, up_weight = small_all[:D], small_all[D:]

    def part_of(weight):
        return lax.dynamic_slice_in_dim(weight, row_at * cut, cut, 1)

    large = jnp.concatenate(
        [part_of(w_gate.T), part_of(w_up.T), part_of(w_down), part_of(w_out)], axis=0
    )
    large_all = lax.all_gather(large, ("rows", "heads"), axis=0, tiled=True)
    large_all = large_all.reshape(n_rows, n_heads, large.shape[0], cut)
    out_weight = large_all[:, :, 3 * units :].transpose(1, 2, 0, 3).reshape(HEADS * HD, D)

    start = head_at * local
    positions = ((start + jnp.arange(local)) % LEN).astype(f32)
    frequency = THETA ** (-jnp.arange(half).astype(f32) / half)
    angles = positions[:, None] * frequency[None, :]
    cos, sin = jnp.cos(angles), jnp.sin(angles)
    places = ((start // block + jnp.arange(own)) % (LEN // block)).astype(jnp.int32)
    front = SCALE * LOG2E
    query_cos = lane_table(local, [(HD, front), (0, front * cos), (0, front * cos), (RD, 0.0)])
    query_sin = lane_table(local, [(HD, 0.0), (0, front * sin), (0, front * sin), (RD, 0.0)])
    key_cos = lane_table(local, [(HD, 0.0), (0, cos), (0, cos), (RD, 0.0)])
    key_sin = lane_table(local, [(HD, 0.0), (0, sin), (0, sin), (RD, 0.0)])
    back_cos = lane_table(local, [(HD, 1.0), (0, cos), (0, cos), (RD, 0.0)])
    back_low = lane_table(local, [(HD + half, 0.0), (0, -sin), (RD, 0.0)])
    back_high = lane_table(local, [(HD, 0.0), (0, sin), (half + RD, 0.0)])

    source = tokens.astype(f32)
    scale_attn = rms_scale(source)
    gain_one = gain_attn.astype(f32)
    normed = (source * scale_attn * gain_one).astype(bf16)
    blank = jnp.zeros((D, HD), bf16)
    latent_weight = jnp.concatenate(
        [w_latent, blank, w_key_rope, -w_key_rope[:, half:], w_key_rope[:, :half]], axis=1
    )
    raw = dot_nn(normed, latent_weight)
    raw_rope = raw[:, LGROUPS * LAT :]
    key_rope = raw_rope * key_cos + jnp.roll(raw_rope, -RD, axis=1) * key_sin
    latent = jnp.concatenate([raw[:, : LGROUPS * LAT], key_rope], axis=1).astype(bf16)

    def halo_pairs(k):
        back = -(-k // own)
        needs = [i for i in range(n_heads) if (i * local % LEN) // block >= k]
        return [(i - back, i) for i in needs]

    def halo_rows(k):
        at = own - 1 - (k - 1) % own
        return slice(at * block, (at + 1) * block)

    pieces = [
        lax.ppermute(latent[halo_rows(k)], "heads", halo_pairs(k)) for k in range(halo, 0, -1)
    ]
    window = jnp.concatenate(pieces + [latent], axis=0)
    queries = project_queries(normed, query_weight, query_cos, query_sin)
    mixed, logs = attend_forward(places, queries, window, up_weight, block, own, halo)

    hidden = source + dot_tn(mixed, out_weight)
    scale_mlp = rms_scale(hidden)
    gain_two = gain_mlp.astype(f32)
    normed_mlp = (hidden * scale_mlp * gain_two).astype(bf16)
    seq_weights = jnp.sum(
        (domain[:, None] == jnp.arange(group_weight.shape[0])[None, :]).astype(f32)
        * group_weight[None, :],
        axis=1,
    )
    token_seq = (start + jnp.arange(local)) // LEN
    token_weight = jnp.sum(
        (token_seq[:, None] == jnp.arange(domain.shape[0])[None, :]).astype(f32)
        * seq_weights[None, :],
        axis=1,
    )
    grad_output = cotangent.astype(f32) * token_weight[:, None]
    direct = cut % LANES == 0
    feed_weights = large_all
    if not direct:
        feed_weights = large_all[:, :, : 3 * units].transpose(1, 2, 0, 3)
        feed_weights = feed_weights.reshape(1, n_heads, 3 * units, D)
    feed_out, grad_normed_mlp, grad_feed = feed_forward_both(
        normed_mlp, grad_output.astype(bf16), feed_weights, units
    )
    if not direct:
        grad_feed = grad_feed.reshape(n_heads, 3 * units, n_rows, cut).transpose(2, 0, 1, 3)
    block_output = (hidden + feed_out).astype(bf16)
    grad_hidden_part, grad_gain_two = norm_backward(hidden, scale_mlp, gain_two, grad_normed_mlp)
    grad_hidden = grad_output + grad_hidden_part
    grad_hidden_low = grad_hidden.astype(bf16)
    own_feed = lax.psum_scatter(
        grad_feed.reshape((n_rows * n_heads,) + grad_feed.shape[2:]),
        ("rows", "heads"),
        scatter_dimension=0,
        tiled=True,
    )[0].astype(f32)

    grad_mixed = dot_nt(out_weight, grad_hidden_low).astype(bf16)
    grad_out_weight = dot_nn(mixed, grad_hidden_low).astype(bf16)
    own_out = lax.psum_scatter(
        grad_out_weight.reshape(n_heads, HEADS * HD // n_heads, n_rows, cut)
        .transpose(2, 0, 1, 3)
        .reshape(n_rows * n_heads, HEADS * HD // n_heads, cut),
        ("rows", "heads"),
        scatter_dimension=0,
        tiled=True,
    )[0].astype(f32)
    grad_query, grad_latent, grad_rope, grad_up_weight = attend_backward(
        places, queries, window, up_weight, mixed, logs, grad_mixed, back_cos, back_low, back_high,
        block, own, halo,
    )
    grad_window = jnp.concatenate([grad_latent, grad_rope], axis=1).astype(bf16)
    own_blocks = [
        grad_window[(halo + j) * block : (halo + j + 1) * block].astype(f32) for j in range(own)
    ]
    for k in range(1, halo + 1):
        got = lax.ppermute(
            grad_window[(halo - k) * block : (halo - k + 1) * block],
            "heads",
            [(b, a) for a, b in halo_pairs(k)],
        )
        at = own - 1 - (k - 1) % own
        own_blocks[at] = own_blocks[at] + got.astype(f32)
    grad_own = jnp.concatenate(own_blocks, axis=0)
    grad_rope_own = grad_own[:, LGROUPS * LAT :]
    grad_rope_own = (
        grad_rope_own * (key_cos)
        + jnp.roll(grad_rope_own, half, axis=1) * back_low
        + jnp.roll(grad_rope_own, -half, axis=1) * back_high
    )
    grad_own = jnp.concatenate([grad_own[:, : LGROUPS * LAT], grad_rope_own], axis=1).astype(bf16)

    grad_normed = dot_nt(grad_query, query_weight) + dot_nt(grad_own, latent_weight)
    grad_source_part, grad_gain_one = norm_backward(source, scale_attn, gain_one, grad_normed)
    grad_tokens = grad_hidden + grad_source_part
    grad_query_weight = dot_tn(normed, grad_query)
    grad_latent_weight = dot_tn(normed, grad_own)
    grad_small = jnp.concatenate([grad_query_weight, grad_up_weight], axis=0).astype(bf16)
    grad_small = jnp.concatenate(
        [
            grad_query_weight.astype(bf16).reshape(n_rows, D // n_rows, n_heads, heads_here * LANES),
            grad_up_weight.astype(bf16).reshape(n_rows, LAT // n_rows, n_heads, heads_here * LANES),
        ],
        axis=1,
    ).transpose(0, 2, 1, 3)
    at = LGROUPS * LAT
    grad_latent_weight = jnp.concatenate(
        [
            grad_latent_weight[:, :at],
            grad_gain_one[:, None],
            grad_gain_two[:, None],
            jnp.zeros((D, HD - 2), f32),
            grad_latent_weight[:, at + HD :],
        ],
        axis=1,
    ).astype(bf16)
    own_small, own_latent = scatter_all(
        [grad_small, grad_latent_weight.reshape(n_rows, n_heads, D // (n_rows * n_heads), at + LANES)],
        shape,
    )
    own_small = own_small.astype(f32)
    own_latent = own_latent.astype(f32)
    own_query = own_small[: D // n_rows].reshape(D // n_rows, heads_here, LANES)
    own_up = own_small[D // n_rows :].reshape(LAT // n_rows, heads_here, LANES)
    return (
        block_output,
        grad_tokens,
        own_latent[:, at],
        own_query[:, :, :HD].reshape(D // n_rows, heads_here * HD),
        own_query[:, :, HD : HD + RD].reshape(D // n_rows, heads_here * RD),
        own_latent[:, :at],
        own_latent[:, at + HD : at + HD + RD],
        own_up[:, :, :HD].reshape(LAT // n_rows, heads_here * HD),
        own_up[:, :, HD:].reshape(LAT // n_rows, heads_here * HD),
        own_out,
        own_latent[:, at + 1],
        own_feed[:units].T,
        own_feed[units : 2 * units].T,
        own_feed[2 * units :],
    )


def solution(mesh):
    in_specs = (
        P(("rows", "heads"), None),
        P(("rows", "heads"), None),
        P("rows"),
        P(),
        P(),
        P(None, "heads"),
        P(None, "heads"),
        P(),
        P(),
        P(None, "heads"),
        P(None, "heads"),
        P("heads", None),
        P(),
        P(None, "heads"),
        P(None, "heads"),
        P("heads", None),
    )
    out_specs = (
        P(("rows", "heads"), None),
        P(("rows", "heads"), None),
        P(("rows", "heads")),
        P("rows", "heads"),
        P("rows", "heads"),
        P(("rows", "heads"), None),
        P(("rows", "heads"), None),
        P("rows", "heads"),
        P("rows", "heads"),
        P("heads", "rows"),
        P(("rows", "heads")),
        P("rows", "heads"),
        P("rows", "heads"),
        P("heads", "rows"),
    )
    return jax.shard_map(
        functools.partial(on_device, dict(mesh.shape)),
        mesh=mesh,
        in_specs=in_specs,
        out_specs=out_specs,
        check_vma=False,
    )
```

```python
import functools
import math

import jax
import jax.numpy as jnp
from jax import lax
from jax.experimental import pallas as pl
from jax.experimental.pallas import tpu as pltpu
from jax.sharding import PartitionSpec as P

D = 1024
HEADS = 16
HD = 64
LGROUPS = 2
LAT = 256
RD = 32
LEN = 2048
EPS = 1e-05
THETA = 10000.0
NEG_LARGE = -1e30
LANES = 128
PAIR = 2
GROUP = HEADS // LGROUPS
TALL = 80
CHUNKS = 4
SHARES = (2, 2, 1)
LOG2E = math.log2(math.e)
LN2 = math.log(2.0)
SCALE = (HD + RD) ** (-0.5)

bf16 = jnp.bfloat16
f32 = jnp.float32


def dot_nn(a, b):
    return jnp.dot(a, b, preferred_element_type=f32)


def dot_nt(a, b):
    return lax.dot_general(a, b, (((1,), (1,)), ((), ())), preferred_element_type=f32)


def dot_tn(a, b):
    return lax.dot_general(a, b, (((0,), (0,)), ((), ())), preferred_element_type=f32)


def rms_scale(values):
    return lax.rsqrt(jnp.mean(values * values, axis=-1, keepdims=True) + EPS)


def norm_backward(source, scale_rows, gain, grad_normed):
    scaled = source * scale_rows
    weighted = grad_normed * gain
    grad_source = scale_rows * (
        weighted - scaled * jnp.mean(weighted * scaled, axis=-1, keepdims=True)
    )
    return (grad_source, jnp.sum(grad_normed * scaled, axis=0))


def keys_values(groups, latent_ref, rope_ref, up_ref, rows, count):
    rope = rope_ref[rows, :]
    lane = lax.broadcasted_iota(jnp.int32, (count, LANES), 1)
    keys, values = [], []
    for e in range(0, GROUP, PAIR):
        latent = latent_ref[rows, groups[e] * LAT : (groups[e] + 1) * LAT]
        up = [up_ref[:, e + i].reshape(LAT, LANES) for i in range(PAIR)]
        up = jnp.concatenate(up, axis=1)
        wide = dot_nn(latent, up).astype(bf16)
        for i in range(PAIR):
            both = wide[:, i * LANES : (i + 1) * LANES]
            keys.append(jnp.where(lane < HD, both, rope))
            values.append(both)
    return keys, values


def values_ones(value):
    count = value.shape[0]
    return jnp.concatenate([value.T[HD:], jnp.ones((TALL - HD, count), bf16)], axis=0)


def attend_forward_kernel(
    groups, block, own, halo, place_ref, q_ref, latent_ref, rope_ref, up_ref, mixed_ref, log_ref,
    query_s, top_s, sum_s,
):
    rows = own * block
    ahead, until = place_ref[0], place_ref[1]
    for e in range(GROUP):
        query_s[e] = q_ref[:, e * LANES : (e + 1) * LANES].T
    keys, values = keys_values(
        groups, latent_ref, rope_ref, up_ref, slice(halo * block, (halo + own) * block), rows
    )
    values = [values_ones(value) for value in values]
    for j in range(own):
        count = (j + 1) * block
        key_at = lax.broadcasted_iota(jnp.int32, (count, block), 0)
        query_at = lax.broadcasted_iota(jnp.int32, (count, block), 1) + j * block
        keep = (key_at <= query_at) & (key_at >= jnp.where(j >= until, until * block, 0))
        cols = slice(j * block, count)
        scores = [
            jnp.where(keep, dot_nn(keys[e][:count], query_s[e, :, cols]), NEG_LARGE)
            for e in range(GROUP)
        ]
        for e in range(GROUP):
            top = jnp.max(scores[e], axis=0, keepdims=True)
            terms = jnp.exp2(scores[e] - top).astype(bf16)
            top_s[e, :, cols] = top
            sum_s[e, :, cols] = dot_nn(values[e][:, :count], terms)
    for blocks in range(1, own + 1):
        wide = blocks * block

        def step(index, _):
            at = pl.ds(pl.multiple_of(index * block, block), block)
            keys, values = keys_values(groups, latent_ref, rope_ref, up_ref, at, block)
            values = [values_ones(value) for value in values]
            scores = [dot_nn(keys[e], query_s[e, :, :wide]) for e in range(GROUP)]
            for e in range(GROUP):
                top = top_s[e, :, :wide]
                higher = jnp.maximum(top, jnp.max(scores[e], axis=0, keepdims=True))
                shrink = jnp.exp2(top - higher)
                terms = jnp.exp2(scores[e] - higher).astype(bf16)
                top_s[e, :, :wide] = higher
                sum_s[e, :, :wide] = sum_s[e, :, :wide] * shrink + dot_nn(values[e], terms)
            return 0

        lax.fori_loop(jnp.where(until == blocks, halo - ahead, halo), halo, step, 0)
    for e in range(GROUP):
        total = sum_s[e]
        sums = total[HD : HD + 1]
        mixed_ref[e * HD : (e + 1) * HD, :] = (total[:HD] * (1.0 / sums)).astype(bf16)
        log_ref[e] = top_s[e] + jnp.log2(sums)


def attend_forward(part, groups, places, queries, window, up_weight, block, own, halo):
    rows, wide = own * block, (halo + own) * block
    cuts, shards, once = up_weight.shape[0], up_weight.shape[1], pl.Buffered(1)
    return pl.pallas_call(
        functools.partial(attend_forward_kernel, groups, block, own, halo),
        grid_spec=pltpu.PrefetchScalarGridSpec(
            num_scalar_prefetch=1,
            grid=(1,),
            in_specs=[
                pl.BlockSpec(
                    (None, rows, GROUP * LANES),
                    lambda g, p: (part * GROUP // shards, 0, part * GROUP % shards // GROUP),
                    pipeline_mode=once,
                ),
                pl.BlockSpec((wide, LGROUPS * LAT), lambda g, p: (0, 0)),
                pl.BlockSpec((wide, LANES), lambda g, p: (0, LGROUPS * LAT // LANES)),
                pl.BlockSpec(
                    (cuts, GROUP, LAT // cuts, LANES),
                    lambda g, p: (0, part * GROUP % shards // GROUP, D // LAT, part * GROUP // shards),
                    pipeline_mode=once,
                ),
            ],
            out_specs=[
                pl.BlockSpec((GROUP * HD, rows), lambda g, p: (0, 0)),
                pl.BlockSpec((GROUP, 1, rows), lambda g, p: (0, 0, 0)),
            ],
            scratch_shapes=[
                pltpu.VMEM((GROUP, LANES, rows), bf16),
                pltpu.VMEM((GROUP, 1, rows), f32),
                pltpu.VMEM((GROUP, TALL, rows), f32),
            ],
        ),
        out_shape=[
            jax.ShapeDtypeStruct((GROUP * HD, rows), bf16),
            jax.ShapeDtypeStruct((GROUP, 1, rows), f32),
        ],
        compiler_params=pltpu.CompilerParams(vmem_limit_bytes=56 << 20),
        cost_estimate=pl.CostEstimate(
            flops=40 * 10**9, bytes_accessed=30 * 10**6, transcendentals=0
        ),
        name="attend_forward",
    )(places, queries, window, window, up_weight)


def attend_backward_kernel(
    groups, block, own, halo, place_ref, q_ref, latent_ref, rope_ref, up_ref, mixed_ref, log_ref,
    grad_ref, cos_ref, low_ref, high_ref, dq_ref, dlatent_ref, drope_ref, dup_ref,
    query_s, grad_s, inner_s, dquery_s, both_s,
):
    rows = own * block
    ahead, until = place_ref[0], place_ref[1]
    first = halo - ahead
    drope_ref[...] = jnp.zeros_like(drope_ref)

    def clear(index, _):
        at = pl.ds(pl.multiple_of(index * block, block), block)
        both_s[at, :] = jnp.zeros((block, GROUP * LANES), bf16)
        return 0

    lax.fori_loop(0, first, clear, 0)
    for e in range(GROUP):
        query_s[e] = q_ref[:, e * LANES : (e + 1) * LANES].T
        grad = grad_ref[e * HD : (e + 1) * HD, :]
        grad_s[e] = jnp.concatenate([jnp.zeros((rows, HD), bf16), grad.T], axis=1)
        inner_s[e] = jnp.sum(
            grad.astype(f32) * mixed_ref[e * HD : (e + 1) * HD, :].astype(f32),
            axis=0,
            keepdims=True,
        )
        dquery_s[e] = jnp.zeros((LANES, rows), f32)
    lane = lax.broadcasted_iota(jnp.int32, (block, LANES), 1)

    def strip(at, low, high, keep):
        cols = slice(low, high)
        keys, values = keys_values(groups, latent_ref, rope_ref, up_ref, at, block)
        scores = [dot_nn(keys[e], query_s[e, :, cols]) for e in range(GROUP)]
        grads = [
            dot_nn(values[e][:, HD:], grad_ref[e * HD : (e + 1) * HD, cols]) for e in range(GROUP)
        ]
        grad_rope = None
        for e in range(GROUP):
            score = scores[e] if keep is None else jnp.where(keep, scores[e], NEG_LARGE)
            probs = jnp.exp2(score - log_ref[e, :, cols])
            grad_scores = (probs * (grads[e] - inner_s[e, :, cols])).astype(bf16)
            grad_value = dot_nn(probs.astype(bf16), grad_s[e, cols, :])
            grad_key = dot_nn(grad_scores, q_ref[cols, e * LANES : (e + 1) * LANES]) * LN2
            dquery_s[e, :, cols] += dot_nn(keys[e].T, grad_scores)
            both_s[at, e * LANES : (e + 1) * LANES] = jnp.where(
                lane < HD, grad_key, grad_value
            ).astype(bf16)
            grad_rope = grad_key if grad_rope is None else grad_rope + grad_key
        drope_ref[at, :] = grad_rope

    for i in range(own):
        count = rows - i * block
        key_at = lax.broadcasted_iota(jnp.int32, (block, count), 0)
        query_at = lax.broadcasted_iota(jnp.int32, (block, count), 1)
        keep = (key_at <= query_at) & (query_at < jnp.where(i < until, (until - i) * block, rows))
        strip(slice((halo + i) * block, (halo + i + 1) * block), i * block, rows, keep)
    for blocks in range(1, own + 1):

        def step(index, _):
            strip(pl.ds(pl.multiple_of(index * block, block), block), 0, blocks * block, None)
            return 0

        lax.fori_loop(jnp.where(until == blocks, first, halo), halo, step, 0)
    for e in range(GROUP):
        grad = dquery_s[e].T * SCALE
        grad = (
            grad * cos_ref[...]
            + pltpu.roll(grad, RD // 2, 1) * low_ref[...]
            + pltpu.roll(grad, LANES - RD // 2, 1) * high_ref[...]
        )
        dq_ref[:, e * LANES : (e + 1) * LANES] = grad.astype(bf16)
    for group in range(LGROUPS):
        at = slice(group * LAT, (group + 1) * LAT)
        heads = [e for e in range(GROUP) if groups[e] == group]
        if not heads:
            dlatent_ref[:, at] = jnp.zeros((dlatent_ref.shape[0], LAT), bf16)
            continue
        lanes = slice(heads[0] * LANES, (heads[-1] + 1) * LANES)
        up = jnp.concatenate([up_ref[:, e].reshape(LAT, LANES) for e in heads], axis=1)
        dlatent_ref[:, at] = dot_nt(both_s[:, lanes], up).astype(bf16)
        dup_ref[:, lanes] = dot_nn(latent_ref[:, at].T, both_s[:, lanes]).astype(bf16)


def attend_backward(
    part, groups, places, queries, window, up_weight, mixed, logs, grad_mixed, tables, block, own, halo
):
    rows, wide = own * block, (halo + own) * block
    cuts, shards, once = up_weight.shape[0], up_weight.shape[1], pl.Buffered(1)
    table = pl.BlockSpec((rows, LANES), lambda g, p: (0, 0), pipeline_mode=once)
    return pl.pallas_call(
        functools.partial(attend_backward_kernel, groups, block, own, halo),
        grid_spec=pltpu.PrefetchScalarGridSpec(
            num_scalar_prefetch=1,
            grid=(1,),
            in_specs=[
                pl.BlockSpec(
                    (None, rows, GROUP * LANES),
                    lambda g, p: (part * GROUP // shards, 0, part * GROUP % shards // GROUP),
                    pipeline_mode=once,
                ),
                pl.BlockSpec((wide, LGROUPS * LAT), lambda g, p: (0, 0), pipeline_mode=once),
                pl.BlockSpec(
                    (wide, LANES), lambda g, p: (0, LGROUPS * LAT // LANES), pipeline_mode=once
                ),
                pl.BlockSpec(
                    (cuts, GROUP, LAT // cuts, LANES),
                    lambda g, p: (0, part * GROUP % shards // GROUP, D // LAT, part * GROUP // shards),
                    pipeline_mode=once,
                ),
                pl.BlockSpec((GROUP * HD, rows), lambda g, p: (0, 0), pipeline_mode=once),
                pl.BlockSpec((GROUP, 1, rows), lambda g, p: (0, 0, 0), pipeline_mode=once),
                pl.BlockSpec((GROUP * HD, rows), lambda g, p: (0, 0), pipeline_mode=once),
                table,
                table,
                table,
            ],
            out_specs=[
                pl.BlockSpec((rows, GROUP * LANES), lambda g, p: (0, 0), pipeline_mode=once),
                pl.BlockSpec((wide, LGROUPS * LAT), lambda g, p: (0, 0), pipeline_mode=once),
                pl.BlockSpec((wide, LANES), lambda g, p: (0, 0), pipeline_mode=once),
                pl.BlockSpec((LAT, GROUP * LANES), lambda g, p: (0, 0), pipeline_mode=once),
            ],
            scratch_shapes=[
                pltpu.VMEM((GROUP, LANES, rows), bf16),
                pltpu.VMEM((GROUP, rows, LANES), bf16),
                pltpu.VMEM((GROUP, 1, rows), f32),
                pltpu.VMEM((GROUP, LANES, rows), f32),
                pltpu.VMEM((wide, GROUP * LANES), bf16),
            ],
        ),
        out_shape=[
            jax.ShapeDtypeStruct((rows, GROUP * LANES), bf16),
            jax.ShapeDtypeStruct((wide, LGROUPS * LAT), bf16),
            jax.ShapeDtypeStruct((wide, LANES), f32),
            jax.ShapeDtypeStruct((LAT, GROUP * LANES), bf16),
        ],
        compiler_params=pltpu.CompilerParams(vmem_limit_bytes=56 << 20),
        cost_estimate=pl.CostEstimate(
            flops=40 * 10**9, bytes_accessed=30 * 10**6, transcendentals=0
        ),
        name="attend_backward",
    )(places, queries, window, window, up_weight, mixed, logs, grad_mixed, *tables)


def bits_of(size):
    return size.bit_length() - 1


def bit_pairs(size, bit):
    return [(i, i ^ (1 << bit)) for i in range(size)]


def upper_bit(axis, bit):
    return (lax.axis_index(axis) >> bit) & 1


def leading(shape):
    lead = [("rows", b) for b in reversed(range(bits_of(shape["rows"])))]
    return lead + [("heads", b) for b in reversed(range(bits_of(shape["heads"])))]


def gather_orders(shape):
    rows = [("rows", b) for b in reversed(range(1, bits_of(shape["rows"])))]
    heads = [("heads", b) for b in reversed(range(bits_of(shape["heads"])))]
    last = [("rows", 0)]
    return [
        heads + rows + last,
        heads[:1] + rows + heads[1:] + last,
        heads[-1:] + rows + heads[:-1] + last,
    ]


def flip(index, bit):
    size = 1 << bit
    return index + size * (1 - 2 * (index // size % 2))


def start_barrier(shape):
    barrier = pltpu.get_barrier_semaphore()
    for axis in ("rows", "heads"):
        for away in range(1, shape[axis]):
            pl.semaphore_signal(
                barrier,
                inc=1,
                device_id={axis: lax.rem(lax.axis_index(axis) + away, shape[axis])},
                device_id_type=pl.DeviceIdType.MESH,
            )
    pl.semaphore_wait(barrier, shape["rows"] + shape["heads"] - 2)


def exchange_index(lead, done, bits):
    return tuple(pl.ds(0, 2) if item in done else bits[item] for item in lead)


def gather_kernel(
    shape, orders, plan, block, own, halo, latent_ref, near_ref, large_ref, window_ref, near_all, large_all,
    zero_s, local_sem, halo_send, halo_recv, send_sem, recv_sem,
):
    row, head = lax.axis_index("rows"), lax.axis_index("heads")
    lead = leading(shape)
    index = {"rows": row, "heads": head}
    bits = {(axis, bit): lax.rem(index[axis] // (1 << bit), 2) for axis, bit in lead}
    zero_s[...] = jnp.zeros_like(zero_s)
    mine = exchange_index(lead, (), bits)
    local = [
        pltpu.make_async_copy(near_ref, near_all.at[mine], local_sem.at[0]),
        pltpu.make_async_copy(large_ref, large_all.at[mine], local_sem.at[1]),
        pltpu.make_async_copy(
            latent_ref, window_ref.at[pl.ds(halo * block, own * block), :], local_sem.at[2]
        ),
    ]
    for copy in local:
        copy.start()
    start_barrier(shape)

    ahead = lax.rem(head * own, halo + 1)
    passed = []
    for k in range(1, halo + 1):
        back = -(-k // own)
        at = own - 1 - (k - 1) % own
        there = lax.rem(head + back, shape["heads"])
        copy = pltpu.make_async_remote_copy(
            src_ref=latent_ref.at[pl.ds(at * block, block), :],
            dst_ref=window_ref.at[pl.ds((halo - k) * block, block), :],
            send_sem=halo_send.at[k - 1],
            recv_sem=halo_recv.at[k - 1],
            device_id={"heads": there},
            device_id_type=pl.DeviceIdType.MESH,
        )
        blank = pltpu.make_async_copy(
            zero_s, window_ref.at[pl.ds((halo - k) * block, block), :], local_sem.at[2 + k]
        )
        goes = (head + back < shape["heads"]) & (lax.rem((head + back) * own, halo + 1) >= k)
        passed.append((copy, blank, goes, ahead >= k))

    for copy, blank, goes, comes in passed:

        @pl.when(goes)
        def _():
            copy.start()

        @pl.when(jnp.logical_not(comes))
        def _():
            blank.start()

    for copy in local:
        copy.wait()
    stages = len(orders[0])
    flying = [None] * len(plan)
    for time in range(max(item[0] for item in plan) + stages):
        for i, (delay, which, order, begin, count) in enumerate(plan):
            stage = time - delay
            if not 0 <= stage < stages:
                continue
            if flying[i] is not None:
                flying[i].wait()
            axis, bit = orders[order][stage]
            target = (near_all, large_all)[which]
            held = exchange_index(lead, orders[order][:stage], bits)
            piece = target.at[held + (pl.ds(begin, count), slice(None))]
            flying[i] = pltpu.make_async_remote_copy(
                src_ref=piece,
                dst_ref=piece,
                send_sem=send_sem.at[i * stages + stage],
                recv_sem=recv_sem.at[i * stages + stage],
                device_id={axis: flip(index[axis], bit)},
                device_id_type=pl.DeviceIdType.MESH,
            )
            flying[i].start()
    for copy in flying:
        copy.wait()
    for copy, blank, goes, comes in passed:

        @pl.when(goes)
        def _():
            copy.wait_send()

        @pl.when(comes)
        def _():
            copy.wait_recv()

        @pl.when(jnp.logical_not(comes))
        def _():
            blank.wait()


def gather_weights(shape, latent, near, large, block, own, halo):
    orders = gather_orders(shape)
    stages = len(orders[0])
    plan = []
    for which, (piece, cuts) in enumerate(((near, 1), (large, CHUNKS))):
        units, total, passed = piece.shape[0] // 16, cuts * sum(SHARES), 0
        for i in range(cuts):
            for order, share in enumerate(SHARES):
                begin = 16 * (units * passed // total)
                passed += share
                count = 16 * (units * passed // total) - begin
                plan.append((i, which, order, begin, count))
    anywhere = pl.BlockSpec(memory_space=pl.ANY)
    twos = (2,) * stages
    window, near_all, large_all = pl.pallas_call(
        functools.partial(gather_kernel, shape, orders, plan, block, own, halo),
        in_specs=[anywhere] * 3,
        out_specs=[anywhere] * 3,
        out_shape=[
            jax.ShapeDtypeStruct(((halo + own) * block, latent.shape[1]), bf16),
            jax.ShapeDtypeStruct(twos + near.shape, bf16),
            jax.ShapeDtypeStruct(twos + large.shape, bf16),
        ],
        scratch_shapes=[
            pltpu.VMEM((block, latent.shape[1]), bf16),
            pltpu.SemaphoreType.DMA((3 + halo,)),
            pltpu.SemaphoreType.DMA((halo,)),
            pltpu.SemaphoreType.DMA((halo,)),
            pltpu.SemaphoreType.DMA((len(plan) * stages,)),
            pltpu.SemaphoreType.DMA((len(plan) * stages,)),
        ],
        compiler_params=pltpu.CompilerParams(
            collective_id=0, has_side_effects=True, vmem_limit_bytes=16 << 20
        ),
        name="gather_weights",
    )(latent, near, large)
    full = (shape["rows"], shape["heads"])
    return window, near_all.reshape(full + near.shape), large_all.reshape(full + large.shape)


def project_kernel(here, normed_ref, weight_ref, cos_ref, sin_ref, out_ref):
    raw = dot_nn(normed_ref[...], weight_ref[...].reshape(D, here * LANES))
    for e in range(here):
        part = raw[:, e * LANES : (e + 1) * LANES]
        part = part * cos_ref[...] + pltpu.roll(part, LANES - RD, 1) * sin_ref[...]
        out_ref[e] = part.astype(bf16)


def project_queries(normed, weights, cos_t, sin_t):
    rows = normed.shape[0]
    cuts, shards, here = weights.shape[0], weights.shape[1], weights.shape[3] // LANES
    table = pl.BlockSpec((rows, LANES), lambda h: (0, 0))
    return pl.pallas_call(
        functools.partial(project_kernel, here),
        grid=(shards,),
        in_specs=[
            pl.BlockSpec((rows, D), lambda h: (0, 0)),
            pl.BlockSpec((cuts, None, D // cuts, here * LANES), lambda h: (0, h, 0, 0)),
            table,
            table,
        ],
        out_specs=pl.BlockSpec((here, rows, LANES), lambda h: (0, 0, h)),
        out_shape=jax.ShapeDtypeStruct((here, rows, shards * LANES), bf16),
        compiler_params=pltpu.CompilerParams(vmem_limit_bytes=40 << 20),
        name="project_queries",
    )(normed, weights, cos_t, sin_t)


def feed_kernel(
    cuts, shards, units, side_ref, normed_ref, grad_ref, weight_ref, out_ref, dnormed_ref, kept_ref, sent_ref
):
    def whole(which):
        return jnp.concatenate(
            [
                jnp.concatenate(
                    [weight_ref[q, t, which * units : (which + 1) * units, :] for q in range(cuts)],
                    axis=1,
                )
                for t in range(shards)
            ],
            axis=0,
        )

    wide = D // cuts
    side = side_ref[0]

    def put(which, grad):
        at = slice(which * units, (which + 1) * units)
        for t in range(shards):
            rows = slice(t * units, (t + 1) * units)
            for q in range(cuts // 2):
                even = grad[rows, 2 * q * wide : (2 * q + 1) * wide].astype(bf16)
                odd = grad[rows, (2 * q + 1) * wide : (2 * q + 2) * wide].astype(bf16)
                kept_ref[q, t, at, :] = jnp.where(side == 0, even, odd)
                sent_ref[q, t, at, :] = jnp.where(side == 0, odd, even)

    @pl.when(pl.program_id(0) == 0)
    def _():
        out_ref[...] = jnp.zeros_like(out_ref)
        dnormed_ref[...] = jnp.zeros_like(dnormed_ref)

    normed = normed_ref[...]
    grad = grad_ref[...]
    w_gate, w_up, w_down = whole(0), whole(1), whole(2)
    gate = dot_nt(w_gate, normed)
    upper = dot_nt(w_up, normed)
    grad_inner = dot_nt(w_down, grad)
    sig = jax.nn.sigmoid(gate)
    silu = gate * sig
    inner = (silu * upper).astype(bf16)
    grad_gate = (grad_inner * upper * sig * (1.0 + gate * (1.0 - sig))).astype(bf16)
    grad_upper = (grad_inner * silu).astype(bf16)
    out_ref[...] += dot_tn(inner, w_down)
    dnormed_ref[...] += dot_tn(grad_gate, w_gate)
    dnormed_ref[...] += dot_tn(grad_upper, w_up)
    put(0, dot_nn(grad_gate, normed))
    put(1, dot_nn(grad_upper, normed))
    put(2, dot_nn(inner, grad))


def feed_forward_both(side, normed, grad, weights, units):
    rows = normed.shape[0]
    cuts, pieces, _, wide = weights.shape
    shards = max(1, min(pieces, 704 // units))
    once = pl.Buffered(1)
    half = (cuts // 2, shards, 3 * units, wide)
    whole = pl.BlockSpec((rows, D), lambda f, s: (0, 0), pipeline_mode=once)
    return pl.pallas_call(
        functools.partial(feed_kernel, cuts, shards, units),
        grid_spec=pltpu.PrefetchScalarGridSpec(
            num_scalar_prefetch=1,
            grid=(pieces // shards,),
            in_specs=[
                whole,
                whole,
                pl.BlockSpec((cuts, shards, 3 * units, wide), lambda f, s: (0, f, 0, 0)),
            ],
            out_specs=[
                whole,
                whole,
                pl.BlockSpec(half, lambda f, s: (0, f, 0, 0)),
                pl.BlockSpec(half, lambda f, s: (0, f, 0, 0)),
            ],
        ),
        out_shape=[
            jax.ShapeDtypeStruct((rows, D), f32),
            jax.ShapeDtypeStruct((rows, D), f32),
            jax.ShapeDtypeStruct((cuts // 2, pieces, 3 * units, wide), bf16),
            jax.ShapeDtypeStruct((cuts // 2, pieces, 3 * units, wide), bf16),
        ],
        compiler_params=pltpu.CompilerParams(vmem_limit_bytes=60 << 20),
        cost_estimate=pl.CostEstimate(
            flops=40 * 10**9, bytes_accessed=50 * 10**6, transcendentals=0
        ),
        name="feed_forward_both",
    )(side, normed, grad, weights)


def scatter_orders(shape):
    return [order[::-1] for order in gather_orders(shape)]


class Scatter:

    def __init__(self, shape, order, array, started=None):
        self.shape = shape
        self.order = list(scatter_orders(shape)[order])
        self.lead = leading(shape)
        self.terms = [array]
        if started is not None:
            self.order.pop(0)
            self.lead.remove(("rows", 0))
            self.terms = [array, started]
        self.terms = [t.reshape((2,) * len(self.lead) + t.shape[2:]) for t in self.terms]

    def total(self, terms):
        if len(terms) == 1:
            return terms[0]
        return sum(t.astype(f32) for t in terms).astype(bf16)

    def halves(self):
        axis, bit = self.order[0]
        at = self.lead.index((axis, bit))
        upper = upper_bit(axis, bit)

        def half(which):
            return self.total(
                [lax.dynamic_index_in_dim(t, which, at, keepdims=False) for t in self.terms]
            )

        return half(upper), half(1 - upper)

    def send(self, kept, sent):
        axis, bit = self.order.pop(0)
        self.lead.remove((axis, bit))
        self.terms = [kept, lax.ppermute(sent, axis, bit_pairs(self.shape[axis], bit))]

    def left(self):
        perm = [self.lead.index(item) for item in self.order]
        array = self.total(self.terms)
        array = array.transpose(perm + list(range(len(perm), array.ndim)))
        return array.reshape((2 ** len(perm),) + array.shape[len(perm) :])


def step_all(scatters, tied):
    halves = [scatter.halves() for scatter in scatters]
    sent, tied = lax.optimization_barrier(([half[1] for half in halves], tied))
    for scatter, half, out in zip(scatters, halves, sent):
        scatter.send(half[0], out)
    return tied


def scatter_kernel(shape, orders, *refs):
    count = len(orders)
    arrays, outs = refs[:count], refs[count : 2 * count]
    scratch, (send_sem, recv_sem) = list(refs[2 * count : -2]), refs[-2:]
    index = {"rows": lax.axis_index("rows"), "heads": lax.axis_index("heads")}
    start_barrier(shape)
    held, flying = list(arrays), [None] * count
    semaphore = 0
    for stage in range(max(len(order) for order in orders) + 1):
        for i, order in enumerate(orders):
            if flying[i] is not None:
                copy, kept, landed, begin, half = flying[i]
                copy.wait()
                flying[i] = None
                if stage < len(order):
                    summed = scratch.pop(0)

                    def add(at, _):
                        both = kept[begin + at].astype(f32) + landed[at].astype(f32)
                        summed[at] = both.astype(bf16)
                        return 0

                    lax.fori_loop(0, half, add, 0)
                    held[i] = summed
                else:
                    outs[i][...] = kept[begin].astype(f32) + landed[0].astype(f32)
            if stage < len(order):
                axis, bit = order[stage]
                upper = lax.rem(index[axis] // (1 << bit), 2)
                half = held[i].shape[0] // 2
                landed = scratch.pop(0)
                copy = pltpu.make_async_remote_copy(
                    src_ref=held[i].at[pl.ds((1 - upper) * half, half)],
                    dst_ref=landed,
                    send_sem=send_sem.at[semaphore],
                    recv_sem=recv_sem.at[semaphore],
                    device_id={axis: flip(index[axis], bit)},
                    device_id_type=pl.DeviceIdType.MESH,
                )
                copy.start()
                flying[i] = (copy, held[i], landed, upper * half, half)
                semaphore += 1


def scatter_rest(shape, scatters):
    orders = [tuple(scatter.order) for scatter in scatters]
    arrays = [scatter.left() for scatter in scatters]
    scratch = []
    for stage in range(max(len(order) for order in orders) + 1):
        for order, array in zip(orders, arrays):
            tail = array.shape[1:]
            if 0 < stage < len(order):
                scratch.append(pltpu.VMEM((array.shape[0] >> stage,) + tail, bf16))
            if stage < len(order):
                scratch.append(pltpu.VMEM((array.shape[0] >> (stage + 1),) + tail, bf16))
    total = sum(len(order) for order in orders)
    inside = pl.BlockSpec(memory_space=pltpu.VMEM)
    return pl.pallas_call(
        functools.partial(scatter_kernel, shape, orders),
        in_specs=[inside] * len(arrays),
        out_specs=[inside] * len(arrays),
        out_shape=[jax.ShapeDtypeStruct(array.shape[1:], f32) for array in arrays],
        scratch_shapes=scratch
        + [pltpu.SemaphoreType.DMA((total,)), pltpu.SemaphoreType.DMA((total,))],
        compiler_params=pltpu.CompilerParams(
            collective_id=1, has_side_effects=True, vmem_limit_bytes=48 << 20
        ),
        name="scatter_rest",
    )(*arrays)


def lane_table(rows, entries):
    columns = []
    for width, value in entries:
        columns.append(
            jnp.full((rows, width), value, f32) if isinstance(value, float) else value
        )
    return jnp.concatenate(columns, axis=1)


def on_device(
    shape,
    tokens,
    cotangent,
    domain,
    group_weight,
    gain_attn,
    w_query,
    w_query_rope,
    w_latent,
    w_key_rope,
    w_key_up,
    w_value_up,
    w_out,
    gain_mlp,
    w_gate,
    w_up,
    w_down,
):
    n_rows, n_heads = shape["rows"], shape["heads"]
    row_at, head_at = lax.axis_index("rows"), lax.axis_index("heads")
    local = tokens.shape[0]
    block = math.gcd(local, LEN)
    own, halo = local // block, LEN // block - 1
    here = w_query.shape[1] // HD
    units = w_gate.shape[1]
    cut = D // n_rows
    half = RD // 2

    head_of = [(i % n_heads) * here + i // n_heads for i in range(HEADS)]
    group_of = [head // GROUP for head in head_of]
    parts = [tuple(group_of[p * GROUP : (p + 1) * GROUP]) for p in range(HEADS // GROUP)]

    def part_of(weight):
        return lax.dynamic_slice_in_dim(weight, row_at * cut, cut, 1)

    start = head_at * local
    positions = ((start + jnp.arange(local)) % LEN).astype(f32)
    frequency = THETA ** (-jnp.arange(half).astype(f32) / half)
    angles = positions[:, None] * frequency[None, :]
    cos, sin = jnp.cos(angles), jnp.sin(angles)
    ahead = start // block % (LEN // block)
    places = jnp.stack([ahead, jnp.minimum(LEN // block - ahead, own)]).astype(jnp.int32)
    front = SCALE * LOG2E
    query_cos = lane_table(local, [(HD, front), (0, front * cos), (0, front * cos), (RD, 0.0)])
    query_sin = lane_table(local, [(HD, 0.0), (0, front * sin), (0, front * sin), (RD, 0.0)])
    key_cos = lane_table(local, [(HD, 0.0), (0, cos), (0, cos), (RD, 0.0)])
    key_sin = lane_table(local, [(HD, 0.0), (0, sin), (0, sin), (RD, 0.0)])
    back_cos = lane_table(local, [(HD, 1.0), (0, cos), (0, cos), (RD, 0.0)])
    back_low = lane_table(local, [(HD + half, 0.0), (0, -sin), (RD, 0.0)])
    back_high = lane_table(local, [(HD, 0.0), (0, sin), (half + RD, 0.0)])

    source = tokens.astype(f32)
    scale_attn = rms_scale(source)
    gain_one = gain_attn.astype(f32)
    normed = (source * scale_attn * gain_one).astype(bf16)
    blank = jnp.zeros((D, HD), bf16)
    latent_weight = jnp.concatenate(
        [w_latent, blank, w_key_rope, -w_key_rope[:, half:], w_key_rope[:, :half]], axis=1
    )
    raw = dot_nn(normed, latent_weight)
    raw_rope = raw[:, LGROUPS * LAT :]
    key_rope = raw_rope * key_cos + jnp.roll(raw_rope, -RD, axis=1) * key_sin
    latent = jnp.concatenate([raw[:, : LGROUPS * LAT], key_rope], axis=1).astype(bf16)

    def halo_pairs(k):
        back = -(-k // own)
        needs = [i for i in range(n_heads) if (i * local % LEN) // block >= k]
        return [(i - back, i) for i in needs]

    def halo_rows(k):
        at = own - 1 - (k - 1) % own
        return slice(at * block, (at + 1) * block)

    rope_here = w_query_rope.reshape(D, here, RD)
    query_here = jnp.concatenate(
        [
            w_query.reshape(D, here, HD),
            rope_here,
            -rope_here[:, :, half:],
            rope_here[:, :, :half],
        ],
        axis=2,
    ).reshape(D, here * LANES)
    up_here = jnp.concatenate(
        [w_key_up.reshape(LAT, here, HD), w_value_up.reshape(LAT, here, HD)], axis=2
    ).reshape(LAT, here * LANES)
    near = jnp.concatenate(
        [
            lax.dynamic_slice_in_dim(query_here, row_at * cut, cut, 0),
            lax.dynamic_slice_in_dim(up_here, row_at * (LAT // n_rows), LAT // n_rows, 0),
        ],
        axis=0,
    )
    large = jnp.concatenate(
        [part_of(w_gate.T), part_of(w_up.T), part_of(w_down), part_of(w_out)], axis=0
    )
    direct = cut % LANES == 0
    if direct:
        window, near_all, large_all = gather_weights(shape, latent, near, large, block, own, halo)
    else:
        pieces = [
            lax.ppermute(latent[halo_rows(k)], "heads", halo_pairs(k)) for k in range(halo, 0, -1)
        ]
        window = jnp.concatenate(pieces + [latent], axis=0)
        near_all = lax.all_gather(near, ("rows", "heads"), axis=0).reshape(
            (n_rows, n_heads) + near.shape
        )
        large_all = lax.all_gather(large, ("rows", "heads"), axis=0).reshape(
            (n_rows, n_heads) + large.shape
        )
    query_weights, out_weights = [], []
    for p in range(len(parts)):
        e, begin = p * GROUP // n_heads, p * GROUP % n_heads
        weight = near_all[:, begin : begin + GROUP, :cut, e * LANES : (e + 1) * LANES]
        query_weights.append(weight.transpose(0, 2, 1, 3).reshape(D, GROUP * LANES))
        weight = large_all[:, begin : begin + GROUP, 3 * units + e * HD : 3 * units + (e + 1) * HD]
        out_weights.append(weight.transpose(1, 2, 0, 3).reshape(GROUP * HD, D))
    out_weights, query_weights = lax.optimization_barrier((out_weights, query_weights))

    queries = project_queries(normed, near_all, query_cos, query_sin)
    forward = [
        attend_forward(p, groups, places, queries, window, near_all, block, own, halo)
        for p, groups in enumerate(parts)
    ]
    hidden = source
    for f, weight in zip(forward, out_weights):
        hidden = hidden + dot_tn(f[0], weight)

    scale_mlp = rms_scale(hidden)
    gain_two = gain_mlp.astype(f32)
    normed_mlp = (hidden * scale_mlp * gain_two).astype(bf16)
    seq_weights = jnp.sum(
        (domain[:, None] == jnp.arange(group_weight.shape[0])[None, :]).astype(f32)
        * group_weight[None, :],
        axis=1,
    )
    token_seq = (start + jnp.arange(local)) // LEN
    token_weight = jnp.sum(
        (token_seq[:, None] == jnp.arange(domain.shape[0])[None, :]).astype(f32)
        * seq_weights[None, :],
        axis=1,
    )
    grad_output = cotangent.astype(f32) * token_weight[:, None]
    core = upper_bit("rows", 0)
    if direct:
        feed_out, grad_normed_mlp, feed_kept, feed_sent = feed_forward_both(
            core.astype(jnp.int32).reshape(1),
            normed_mlp,
            grad_output.astype(bf16),
            large_all,
            units,
        )
    else:
        feed_weights = large_all[:, :, : 3 * units].transpose(1, 2, 0, 3)
        feed_weights = feed_weights.reshape(n_heads, 3 * units, 2, D // 2)
        feed_out, grad_normed_mlp, low_half, high_half = feed_forward_both(
            jnp.zeros((1,), jnp.int32),
            normed_mlp,
            grad_output.astype(bf16),
            feed_weights.transpose(2, 0, 1, 3),
            units,
        )
        grad_feed = jnp.concatenate([low_half[0], high_half[0]], axis=2)
        grad_feed = grad_feed.reshape(n_heads, 3 * units, n_rows // 2, 2, cut)
        grad_feed = grad_feed.transpose(3, 2, 0, 1, 4)
        feed_kept = lax.dynamic_index_in_dim(grad_feed, core, 0, keepdims=False)
        feed_sent = lax.dynamic_index_in_dim(grad_feed, 1 - core, 0, keepdims=False)
    feed_got = lax.ppermute(feed_sent, "rows", bit_pairs(n_rows, 0))
    middle = 3 * units // 2
    scatter_feed = [
        Scatter(shape, 0, feed_kept[:, :, :middle], feed_got[:, :, :middle]),
        Scatter(shape, 1, feed_kept[:, :, middle:], feed_got[:, :, middle:]),
    ]
    block_output = (hidden + feed_out).astype(bf16)
    grad_hidden_part, grad_gain_two = norm_backward(hidden, scale_mlp, gain_two, grad_normed_mlp)
    grad_hidden = grad_output + grad_hidden_part
    grad_hidden_low = grad_hidden.astype(bf16)

    grad_mixed = [dot_nt(weight, grad_hidden_low).astype(bf16) for weight in out_weights]
    grad_out_weight = []
    for f in forward:
        by_cut = [
            dot_nn(f[0], grad_hidden_low[:, r * cut : (r + 1) * cut]).astype(bf16)
            for r in range(n_rows)
        ]
        grad_out_weight.append(jnp.stack(by_cut).reshape(n_rows, GROUP, HD, cut))
    if GROUP % n_heads == 0:
        grad_out_weight = jnp.concatenate(grad_out_weight, axis=2)
    else:
        grad_out_weight = jnp.concatenate(grad_out_weight, axis=1)
    tables = (back_cos, back_low, back_high)

    def pieces_of(grad_query_part, grad_up_part):
        both = []
        for grad in (grad_query_part, grad_up_part):
            tall = grad.shape[0] // n_rows
            grad = grad.astype(bf16).reshape(n_rows, tall, -1, n_heads, LANES)
            both.append(grad.transpose(0, 3, 1, 2, 4).reshape(n_rows, n_heads, tall, -1))
        return jnp.concatenate(both, axis=2)

    by_part = GROUP % n_heads == 0
    scatter_near, backward = [], []
    scatter_out = Scatter(shape, 0, grad_out_weight)
    for p, groups in enumerate(parts):
        under_way = scatter_feed + ([scatter_out] + scatter_near if p else [])
        queries = step_all(under_way, queries)
        backward.append(
            attend_backward(
                p, groups, places, queries, window, near_all, forward[p][0], forward[p][1],
                grad_mixed[p], tables, block, own, halo,
            )
        )
        if by_part:
            last = backward[-1]
            scatter_near.append(Scatter(shape, 1, pieces_of(dot_tn(normed, last[0]), last[3])))
    if not by_part:
        grad_query_weight = dot_tn(normed, jnp.concatenate([b[0] for b in backward], axis=1))
        grad_up_weight = jnp.concatenate([b[3] for b in backward], axis=1)
        scatter_near.append(Scatter(shape, 1, pieces_of(grad_query_weight, grad_up_weight)))
    grad_window = jnp.concatenate(
        [sum(b[1].astype(f32) for b in backward), sum(b[2] for b in backward)], axis=1
    ).astype(bf16)
    own_blocks = [
        grad_window[(halo + j) * block : (halo + j + 1) * block].astype(f32) for j in range(own)
    ]
    for k in range(1, halo + 1):
        got = lax.ppermute(
            grad_window[(halo - k) * block : (halo - k + 1) * block],
            "heads",
            [(b, a) for a, b in halo_pairs(k)],
        )
        at = own - 1 - (k - 1) % own
        own_blocks[at] = own_blocks[at] + got.astype(f32)
    grad_own = jnp.concatenate(own_blocks, axis=0)
    at = LGROUPS * LAT
    grad_rope_own = grad_own[:, at:]
    grad_rope_own = (
        grad_rope_own * key_cos
        + jnp.roll(grad_rope_own, half, axis=1) * back_low
        + jnp.roll(grad_rope_own, -half, axis=1) * back_high
    )
    grad_own = jnp.concatenate([grad_own[:, :at], grad_rope_own], axis=1).astype(bf16)

    grad_normed = dot_nt(grad_own, latent_weight)
    for p, b in enumerate(backward):
        grad_normed = grad_normed + dot_nt(b[0], query_weights[p])
    grad_source_part, grad_gain_one = norm_backward(source, scale_attn, gain_one, grad_normed)
    grad_tokens = grad_hidden + grad_source_part
    grad_latent_weight = dot_tn(normed, grad_own)
    grad_latent_weight = jnp.concatenate(
        [
            grad_latent_weight[:, :at],
            grad_gain_one[:, None],
            grad_gain_two[:, None],
            jnp.zeros((D, HD - 2), f32),
            grad_latent_weight[:, at + HD :],
        ],
        axis=1,
    ).astype(bf16)
    grad_latent_weight = grad_latent_weight.reshape(
        n_rows, n_heads, D // (n_rows * n_heads), at + LANES
    )
    scatter_latent = Scatter(shape, 0, grad_latent_weight)
    own_first, own_second, own_out, own_latent, *own_small = scatter_rest(
        shape, scatter_feed + [scatter_out, scatter_latent] + scatter_near
    )
    own_feed = jnp.concatenate([own_first, own_second], axis=0)
    own_small = jnp.concatenate(own_small, axis=1)
    own_query = own_small[: D // n_rows].reshape(D // n_rows, here, LANES)
    own_up = own_small[D // n_rows :].reshape(LAT // n_rows, here, LANES)
    return (
        block_output,
        grad_tokens,
        own_latent[:, at],
        own_query[:, :, :HD].reshape(D // n_rows, here * HD),
        own_query[:, :, HD : HD + RD].reshape(D // n_rows, here * RD),
        own_latent[:, :at],
        own_latent[:, at + HD : at + HD + RD],
        own_up[:, :, :HD].reshape(LAT // n_rows, here * HD),
        own_up[:, :, HD:].reshape(LAT // n_rows, here * HD),
        own_out,
        own_latent[:, at + 1],
        own_feed[:units].T,
        own_feed[units : 2 * units].T,
        own_feed[2 * units :],
    )


def solution(mesh):
    in_specs = (
        P(("rows", "heads"), None),
        P(("rows", "heads"), None),
        P("rows"),
        P(),
        P(),
        P(None, "heads"),
        P(None, "heads"),
        P(),
        P(),
        P(None, "heads"),
        P(None, "heads"),
        P("heads", None),
        P(),
        P(None, "heads"),
        P(None, "heads"),
        P("heads", None),
    )
    out_specs = (
        P(("rows", "heads"), None),
        P(("rows", "heads"), None),
        P(("rows", "heads")),
        P("rows", "heads"),
        P("rows", "heads"),
        P(("rows", "heads"), None),
        P(("rows", "heads"), None),
        P("rows", "heads"),
        P("rows", "heads"),
        P("heads", "rows"),
        P(("rows", "heads")),
        P("rows", "heads"),
        P("rows", "heads"),
        P("heads", "rows"),
    )
    return jax.shard_map(
        functools.partial(on_device, dict(mesh.shape)),
        mesh=mesh,
        in_specs=in_specs,
        out_specs=out_specs,
        check_vma=False,
    )
```

```python
import functools
import math

import jax
import jax.numpy as jnp
from jax import lax
from jax.experimental import pallas as pl
from jax.experimental.pallas import tpu as pltpu
from jax.sharding import PartitionSpec as P

D = 1024
HEADS = 16
HD = 64
LGROUPS = 2
LAT = 256
RD = 32
LEN = 2048
EPS = 1e-05
THETA = 10000.0
NEG_LARGE = -1e30
LANES = 128
PAIR = 2
GROUP = HEADS // LGROUPS
TALL = 80
CHUNKS = 4
SHARES = (2, 2, 1)
LOG2E = math.log2(math.e)
LN2 = math.log(2.0)
SCALE = (HD + RD) ** (-0.5)

bf16 = jnp.bfloat16
f32 = jnp.float32


def dot_nn(a, b):
    return jnp.dot(a, b, preferred_element_type=f32)


def dot_nt(a, b):
    return lax.dot_general(a, b, (((1,), (1,)), ((), ())), preferred_element_type=f32)


def dot_tn(a, b):
    return lax.dot_general(a, b, (((0,), (0,)), ((), ())), preferred_element_type=f32)


def rms_scale(values):
    return lax.rsqrt(jnp.mean(values * values, axis=-1, keepdims=True) + EPS)


def rotate_lanes(values, cos, sin):
    lane = lax.broadcasted_iota(jnp.int32, values.shape, 1)
    turned = (lane >= HD) & (lane < HD + RD)
    cos = jnp.where(lane < HD, 1.0, jnp.where(turned, cos, 0.0))
    sin = jnp.where(turned, sin, 0.0)
    half = RD // 2
    swapped = jnp.where(
        lane < HD + half, -pltpu.roll(values, LANES - half, 1), pltpu.roll(values, half, 1)
    )
    return values * cos + swapped * sin


def rope_weight(w_key_rope):
    rows = w_key_rope.shape[0]
    blank = jnp.zeros((rows, HD), bf16)
    return jnp.concatenate([blank, w_key_rope, blank[:, : LANES - HD - RD]], axis=1)


def prepare_kernel(tokens_ref, gain_ref, latent_ref, rope_ref, cos_ref, sin_ref, normed_ref, out_ref):
    source = tokens_ref[...].astype(f32)
    normed = (source * rms_scale(source) * gain_ref[...].astype(f32)).astype(bf16)
    normed_ref[...] = normed
    out_ref[:, : LGROUPS * LAT] = dot_nn(normed, latent_ref[...]).astype(bf16)
    turned = rotate_lanes(dot_nn(normed, rope_weight(rope_ref[...])), cos_ref[...], sin_ref[...])
    out_ref[:, LGROUPS * LAT :] = turned.astype(bf16)


def prepare(tokens, gain, w_latent, w_key_rope, cos, sin):
    rows = tokens.shape[0]
    return pl.pallas_call(
        prepare_kernel,
        out_shape=[
            jax.ShapeDtypeStruct((rows, D), bf16),
            jax.ShapeDtypeStruct((rows, LGROUPS * LAT + LANES), bf16),
        ],
        compiler_params=pltpu.CompilerParams(vmem_limit_bytes=40 << 20),
        name="prepare",
    )(tokens, gain, w_latent, w_key_rope, cos, sin)


def pack_kernel(
    here, side_ref, query_ref, rope_ref, key_ref, value_ref, out_ref, gate_ref, up_ref, down_ref,
    near_ref, large_ref,
):
    cut, units = gate_ref.shape
    blank = jnp.zeros((cut, LANES - HD - RD), bf16)
    small = key_ref.shape[0]
    for e in range(here):
        lanes = slice(e * LANES, (e + 1) * LANES)
        heads, turns = slice(e * HD, (e + 1) * HD), slice(e * RD, (e + 1) * RD)
        near_ref[:cut, lanes] = jnp.concatenate(
            [query_ref[:, heads], rope_ref[:, turns], blank], axis=1
        )
        near_ref[cut : cut + small, lanes] = jnp.concatenate(
            [key_ref[:, heads], value_ref[:, heads]], axis=1
        )
    near_ref[cut + small :, :] = out_ref[...]
    large_ref[:units, :] = gate_ref[...].T
    large_ref[units : 2 * units, :] = up_ref[...].T
    large_ref[2 * units :, :] = down_ref[...]


def pack(side, n_rows, w_query, w_query_rope, w_key_up, w_value_up, w_out, w_gate, w_up, w_down):
    here, units = w_query.shape[1] // HD, w_gate.shape[1]
    cut, small = D // n_rows, LAT // n_rows

    def by_rows(weight):
        tall = weight.shape[0] // n_rows
        return pl.BlockSpec((tall, weight.shape[1]), lambda g, s: (s[0], 0))

    def by_columns(weight):
        return pl.BlockSpec((weight.shape[0], cut), lambda g, s: (0, s[0]))

    near = (cut + small + here * HD, here * LANES)
    large = (3 * units, cut)
    return pl.pallas_call(
        functools.partial(pack_kernel, here),
        grid_spec=pltpu.PrefetchScalarGridSpec(
            num_scalar_prefetch=1,
            grid=(1,),
            in_specs=[
                by_rows(w_query),
                by_rows(w_query_rope),
                by_rows(w_key_up),
                by_rows(w_value_up),
                by_columns(w_out),
                by_rows(w_gate),
                by_rows(w_up),
                by_columns(w_down),
            ],
            out_specs=[
                pl.BlockSpec(near, lambda g, s: (0, 0)),
                pl.BlockSpec(large, lambda g, s: (0, 0)),
            ],
        ),
        out_shape=[jax.ShapeDtypeStruct(near, bf16), jax.ShapeDtypeStruct(large, bf16)],
        name="pack",
    )(side, w_query, w_query_rope, w_key_up, w_value_up, w_out, w_gate, w_up, w_down)


def keys_values(groups, latent_ref, rope_ref, up_ref, rows, count):
    rope = rope_ref[rows, :]
    lane = lax.broadcasted_iota(jnp.int32, (count, LANES), 1)
    keys, values = [], []
    for e in range(0, GROUP, PAIR):
        latent = latent_ref[rows, groups[e] * LAT : (groups[e] + 1) * LAT]
        up = [up_ref[:, e + i].reshape(LAT, LANES) for i in range(PAIR)]
        up = jnp.concatenate(up, axis=1)
        wide = dot_nn(latent, up).astype(bf16)
        for i in range(PAIR):
            both = wide[:, i * LANES : (i + 1) * LANES]
            keys.append(jnp.where(lane < HD, both, rope))
            values.append(both)
    return keys, values


def values_ones(value):
    count = value.shape[0]
    return jnp.concatenate([value.T[HD:], jnp.ones((TALL - HD, count), bf16)], axis=0)


def shard_block(part, shards, rows_at):
    return lambda g, p: (0, part * GROUP % shards // GROUP, rows_at, part * GROUP // shards)


def forward_body(
    groups, block, own, halo, ahead, meanwhile, normed_ref, weight_ref, cos_ref, sin_ref, latent_ref, rope_ref,
    up_ref, mixed_ref, log_ref, q_ref, query_s, top_s, sum_s,
):
    rows = own * block
    until = halo + 1 - ahead
    weight = jnp.concatenate(
        [weight_ref[:, e].reshape(D, LANES) for e in range(GROUP)], axis=1
    )
    raw = dot_nn(normed_ref[...], weight)
    for e in range(GROUP):
        lanes = slice(e * LANES, (e + 1) * LANES)
        query = rotate_lanes(raw[:, lanes], cos_ref[...], sin_ref[...])
        query = (query * (SCALE * LOG2E)).astype(bf16)
        q_ref[:, lanes] = query
        query_s[e] = query.T
    keys, values = keys_values(
        groups, latent_ref, rope_ref, up_ref, slice(halo * block, (halo + own) * block), rows
    )
    values = [values_ones(value) for value in values]
    for j in range(own):
        count = (j + 1) * block
        key_at = lax.broadcasted_iota(jnp.int32, (count, block), 0)
        query_at = lax.broadcasted_iota(jnp.int32, (count, block), 1) + j * block
        keep = (key_at <= query_at) & (key_at >= jnp.where(j >= until, until * block, 0))
        cols = slice(j * block, count)
        scores = [
            jnp.where(keep, dot_nn(keys[e][:count], query_s[e, :, cols]), NEG_LARGE)
            for e in range(GROUP)
        ]
        for e in range(GROUP):
            top = jnp.max(scores[e], axis=0, keepdims=True)
            terms = jnp.exp2(scores[e] - top).astype(bf16)
            top_s[e, :, cols] = top
            sum_s[e, :, cols] = dot_nn(values[e][:, :count], terms)
    meanwhile(0)
    for blocks in range(1, own + 1):
        wide = blocks * block

        def step(index, _):
            at = pl.ds(pl.multiple_of(index * block, block), block)
            keys, values = keys_values(groups, latent_ref, rope_ref, up_ref, at, block)
            values = [values_ones(value) for value in values]
            scores = [dot_nn(keys[e], query_s[e, :, :wide]) for e in range(GROUP)]
            for e in range(GROUP):
                top = top_s[e, :, :wide]
                higher = jnp.maximum(top, jnp.max(scores[e], axis=0, keepdims=True))
                shrink = jnp.exp2(top - higher)
                terms = jnp.exp2(scores[e] - higher).astype(bf16)
                top_s[e, :, :wide] = higher
                sum_s[e, :, :wide] = sum_s[e, :, :wide] * shrink + dot_nn(values[e], terms)
            return 0

        @pl.when(until == blocks if blocks < own else until >= own)
        def _():
            lax.fori_loop(halo - ahead, halo, step, 0)

    meanwhile(1)
    for e in range(GROUP):
        total = sum_s[e]
        sums = total[HD : HD + 1]
        mixed_ref[e * HD : (e + 1) * HD, :] = (total[:HD] * (1.0 / sums)).astype(bf16)
        log_ref[e] = top_s[e] + jnp.log2(sums)


def attend_forward_kernel(groups, block, own, halo, place_ref, *refs):
    forward_body(groups, block, own, halo, place_ref[0], lambda at: None, *refs)


def attend_forward(part, groups, places, normed, near, cos, sin, window, block, own, halo):
    rows, wide = own * block, (halo + own) * block
    cuts, shards, once = near.shape[0], near.shape[1], pl.Buffered(1)

    def whole(shape):
        return pl.BlockSpec(shape, lambda g, p: (0,) * len(shape), pipeline_mode=once)

    return pl.pallas_call(
        functools.partial(attend_forward_kernel, groups, block, own, halo),
        grid_spec=pltpu.PrefetchScalarGridSpec(
            num_scalar_prefetch=1,
            grid=(1,),
            in_specs=[
                whole((rows, D)),
                pl.BlockSpec(
                    (cuts, GROUP, D // cuts, LANES),
                    shard_block(part, shards, 0),
                    pipeline_mode=once,
                ),
                whole((rows, LANES)),
                whole((rows, LANES)),
                whole((wide, LGROUPS * LAT)),
                pl.BlockSpec(
                    (wide, LANES), lambda g, p: (0, LGROUPS * LAT // LANES), pipeline_mode=once
                ),
                pl.BlockSpec(
                    (cuts, GROUP, LAT // cuts, LANES),
                    shard_block(part, shards, D // LAT),
                    pipeline_mode=once,
                ),
            ],
            out_specs=[
                whole((GROUP * HD, rows)),
                whole((GROUP, 1, rows)),
                whole((rows, GROUP * LANES)),
            ],
            scratch_shapes=[
                pltpu.VMEM((GROUP, LANES, rows), bf16),
                pltpu.VMEM((GROUP, 1, rows), f32),
                pltpu.VMEM((GROUP, TALL, rows), f32),
            ],
        ),
        out_shape=[
            jax.ShapeDtypeStruct((GROUP * HD, rows), bf16),
            jax.ShapeDtypeStruct((GROUP, 1, rows), f32),
            jax.ShapeDtypeStruct((rows, GROUP * LANES), bf16),
        ],
        compiler_params=pltpu.CompilerParams(vmem_limit_bytes=56 << 20),
        name="attend_forward",
    )(places, normed, near, cos, sin, window, window, near)


def attend_backward_kernel(
    groups, block, own, halo, carried, place_ref, q_ref, latent_ref, rope_ref, up_ref, mixed_ref, log_ref,
    grad_ref, cos_ref, sin_ref, normed_ref, weight_ref, *refs
):
    before = refs[:2] if carried else None
    dwindow_ref, dnormed_ref, dnear_ref, query_s, grad_s, inner_s, dquery_s, both_s, rope_s = refs[-9:]
    rows = own * block
    ahead, until = place_ref[0], place_ref[1]
    first = halo - ahead
    rope_s[...] = jnp.zeros_like(rope_s)

    def clear(index, _):
        at = pl.ds(pl.multiple_of(index * block, block), block)
        both_s[at, :] = jnp.zeros((block, GROUP * LANES), bf16)
        return 0

    lax.fori_loop(0, first, clear, 0)
    for e in range(GROUP):
        query_s[e] = q_ref[:, e * LANES : (e + 1) * LANES].T
        grad = grad_ref[e * HD : (e + 1) * HD, :]
        grad_s[e] = jnp.concatenate([jnp.zeros((rows, HD), bf16), grad.T], axis=1)
        inner_s[e] = jnp.sum(
            grad.astype(f32) * mixed_ref[e * HD : (e + 1) * HD, :].astype(f32),
            axis=0,
            keepdims=True,
        )
        dquery_s[e] = jnp.zeros((LANES, rows), f32)
    lane = lax.broadcasted_iota(jnp.int32, (block, LANES), 1)

    def strip(at, low, high, keep):
        cols = slice(low, high)
        keys, values = keys_values(groups, latent_ref, rope_ref, up_ref, at, block)
        scores = [dot_nn(keys[e], query_s[e, :, cols]) for e in range(GROUP)]
        grads = [
            dot_nn(values[e][:, HD:], grad_ref[e * HD : (e + 1) * HD, cols]) for e in range(GROUP)
        ]
        grad_rope = None
        for e in range(GROUP):
            score = scores[e] if keep is None else jnp.where(keep, scores[e], NEG_LARGE)
            probs = jnp.exp2(score - log_ref[e, :, cols])
            grad_scores = (probs * (grads[e] - inner_s[e, :, cols])).astype(bf16)
            grad_value = dot_nn(probs.astype(bf16), grad_s[e, cols, :])
            grad_key = dot_nn(grad_scores, q_ref[cols, e * LANES : (e + 1) * LANES]) * LN2
            dquery_s[e, :, cols] += dot_nn(keys[e].T, grad_scores)
            both_s[at, e * LANES : (e + 1) * LANES] = jnp.where(
                lane < HD, grad_key, grad_value
            ).astype(bf16)
            grad_rope = grad_key if grad_rope is None else grad_rope + grad_key
        rope_s[at, :] = grad_rope

    for i in range(own):
        count = rows - i * block
        key_at = lax.broadcasted_iota(jnp.int32, (block, count), 0)
        query_at = lax.broadcasted_iota(jnp.int32, (block, count), 1)
        keep = (key_at <= query_at) & (query_at < jnp.where(i < until, (until - i) * block, rows))
        strip(slice((halo + i) * block, (halo + i + 1) * block), i * block, rows, keep)
    for blocks in range(1, own + 1):

        def step(index, _):
            strip(pl.ds(pl.multiple_of(index * block, block), block), 0, blocks * block, None)
            return 0

        lax.fori_loop(jnp.where(until == blocks, first, halo), halo, step, 0)
    grads = []
    for e in range(GROUP):
        grad = rotate_lanes(dquery_s[e].T * SCALE, cos_ref[...], -sin_ref[...])
        grads.append(grad.astype(bf16))
    dquery = jnp.concatenate(grads, axis=1)
    cuts = weight_ref.shape[0]
    cut, small = D // cuts, LAT // cuts
    for q in range(cuts):
        weight = jnp.concatenate([weight_ref[q, e] for e in range(GROUP)], axis=1)
        part = dot_nt(dquery, weight)
        if carried:
            part = part + before[1][:, q * cut : (q + 1) * cut]
        dnormed_ref[:, q * cut : (q + 1) * cut] = part
    grad = dot_tn(normed_ref[...], dquery).astype(bf16)
    for q in range(cuts):
        for e in range(GROUP):
            dnear_ref[q, e, :cut, :] = grad[q * cut : (q + 1) * cut, e * LANES : (e + 1) * LANES]
    for group in range(LGROUPS):
        at = slice(group * LAT, (group + 1) * LAT)
        heads = [e for e in range(GROUP) if groups[e] == group]
        if heads:
            lanes = slice(heads[0] * LANES, (heads[-1] + 1) * LANES)
            up = jnp.concatenate([up_ref[:, e].reshape(LAT, LANES) for e in heads], axis=1)
            grad = dot_nt(both_s[:, lanes], up)
            dup = dot_nn(latent_ref[:, at].T, both_s[:, lanes]).astype(bf16)
            for q in range(cuts):
                for i, e in enumerate(heads):
                    dnear_ref[q, e, cut:, :] = dup[
                        q * small : (q + 1) * small, i * LANES : (i + 1) * LANES
                    ]
        else:
            grad = jnp.zeros((dwindow_ref.shape[0], LAT), f32)
        if carried:
            grad = grad + before[0][:, at].astype(f32)
        dwindow_ref[:, at] = grad.astype(bf16)
    grad = rope_s[...]
    if carried:
        grad = grad + before[0][:, LGROUPS * LAT :].astype(f32)
    dwindow_ref[:, LGROUPS * LAT :] = grad.astype(bf16)


def attend_backward(
    part, groups, places, forward, normed, near, cos, sin, window, grad_mixed, before, block, own, halo
):
    rows, wide = own * block, (halo + own) * block
    cuts, shards, once = near.shape[0], near.shape[1], pl.Buffered(1)
    near_rows = (D + LAT) // cuts
    lanes = LGROUPS * LAT + LANES
    mixed, logs, queries = forward

    def whole(shape):
        return pl.BlockSpec(shape, lambda g, p: (0,) * len(shape), pipeline_mode=once)

    return pl.pallas_call(
        functools.partial(attend_backward_kernel, groups, block, own, halo, before is not None),
        grid_spec=pltpu.PrefetchScalarGridSpec(
            num_scalar_prefetch=1,
            grid=(1,),
            in_specs=[
                whole((rows, GROUP * LANES)),
                whole((wide, LGROUPS * LAT)),
                pl.BlockSpec(
                    (wide, LANES), lambda g, p: (0, LGROUPS * LAT // LANES), pipeline_mode=once
                ),
                pl.BlockSpec(
                    (cuts, GROUP, LAT // cuts, LANES),
                    shard_block(part, shards, D // LAT),
                    pipeline_mode=once,
                ),
                whole((GROUP * HD, rows)),
                whole((GROUP, 1, rows)),
                whole((GROUP * HD, rows)),
                whole((rows, LANES)),
                whole((rows, LANES)),
                whole((rows, D)),
                pl.BlockSpec(
                    (cuts, GROUP, D // cuts, LANES),
                    shard_block(part, shards, 0),
                    pipeline_mode=once,
                ),
            ]
            + ([] if before is None else [whole((wide, lanes)), whole((rows, D))]),
            out_specs=[
                whole((wide, lanes)),
                whole((rows, D)),
                whole((cuts, GROUP, near_rows, LANES)),
            ],
            scratch_shapes=[
                pltpu.VMEM((GROUP, LANES, rows), bf16),
                pltpu.VMEM((GROUP, rows, LANES), bf16),
                pltpu.VMEM((GROUP, 1, rows), f32),
                pltpu.VMEM((GROUP, LANES, rows), f32),
                pltpu.VMEM((wide, GROUP * LANES), bf16),
                pltpu.VMEM((wide, LANES), f32),
            ],
        ),
        out_shape=[
            jax.ShapeDtypeStruct((wide, lanes), bf16),
            jax.ShapeDtypeStruct((rows, D), f32),
            jax.ShapeDtypeStruct((cuts, GROUP, near_rows, LANES), bf16),
        ],
        compiler_params=pltpu.CompilerParams(vmem_limit_bytes=60 << 20),
        cost_estimate=pl.CostEstimate(
            flops=40 * 10**9, bytes_accessed=30 * 10**6, transcendentals=0
        ),
        name="attend_backward",
    )(
        places, queries, window, window, near, mixed, logs, grad_mixed, cos, sin, normed, near,
        *(before or ()),
    )


def join_kernel(parts, tokens_ref, gain_ref, *refs):
    mixed, weights, (hidden_ref, normed_ref) = refs[:parts], refs[parts : 2 * parts], refs[2 * parts :]
    cuts, _, _, cut = weights[0].shape
    squares = 0.0
    for q in range(cuts):
        cols = slice(q * cut, (q + 1) * cut)
        total = tokens_ref[:, cols].astype(f32)
        for m, w in zip(mixed, weights):
            total = total + dot_tn(m[...], w[q].reshape(GROUP * HD, cut))
        hidden_ref[:, cols] = total
        squares = squares + jnp.sum(total * total, axis=1, keepdims=True)
    scale = lax.rsqrt(squares * (1.0 / D) + EPS)
    normed_ref[...] = (hidden_ref[...] * scale * gain_ref[...].astype(f32)).astype(bf16)


def out_specs_of(out, base, parts):
    cuts, shards, _, cut = out.shape
    return [
        pl.BlockSpec(
            (cuts, GROUP, HD, cut),
            lambda g, part=part: (
                0, part * GROUP % shards // GROUP, base // HD + part * GROUP // shards, 0
            ),
            pipeline_mode=pl.Buffered(1),
        )
        for part in range(parts)
    ]


def join(tokens, gain, mixed, out, base):
    rows, parts = tokens.shape[0], len(mixed)

    def whole(shape):
        return pl.BlockSpec(shape, lambda g: (0,) * len(shape), pipeline_mode=pl.Buffered(1))

    return pl.pallas_call(
        functools.partial(join_kernel, parts),
        grid=(1,),
        in_specs=[whole((rows, D)), whole((1, D))]
        + [whole((GROUP * HD, rows))] * parts
        + out_specs_of(out, base, parts),
        out_specs=[whole((rows, D)), whole((rows, D))],
        out_shape=[
            jax.ShapeDtypeStruct((rows, D), f32),
            jax.ShapeDtypeStruct((rows, D), bf16),
        ],
        compiler_params=pltpu.CompilerParams(vmem_limit_bytes=32 << 20),
        name="join",
    )(tokens, gain, *mixed, *([out] * parts))


def norm_backward(source, gain, grad_normed):
    scale = rms_scale(source)
    scaled = source * scale
    weighted = grad_normed * gain
    mean = jnp.mean(weighted * scaled, axis=-1, keepdims=True)
    return (
        scale * (weighted - scaled * mean),
        jnp.sum(grad_normed * scaled, axis=0, keepdims=True),
    )


def middle_kernel(parts, here, hidden_ref, feed_ref, dnormed_ref, cotangent_ref, weight_ref, gain_ref, *refs):
    mixed, weights = refs[:parts], refs[parts : 2 * parts]
    block_ref, grad_ref, dout_ref, dgain_ref = refs[2 * parts : 2 * parts + 4]
    dmixed = refs[2 * parts + 4 :]
    hidden = hidden_ref[...]
    block_ref[...] = (hidden + feed_ref[...]).astype(bf16)
    grad, dgain_ref[...] = norm_backward(hidden, gain_ref[...].astype(f32), dnormed_ref[...])
    grad = grad + cotangent_ref[...].astype(f32) * weight_ref[...]
    grad_ref[...] = grad
    low = grad.astype(bf16)
    cuts, _, _, cut = weights[0].shape
    shards = dout_ref.shape[1]
    for p in range(parts):
        e, begin = p * GROUP // shards, p * GROUP % shards
        total = None
        for q in range(cuts):
            cols = slice(q * cut, (q + 1) * cut)
            part = dot_nt(weights[p][q].reshape(GROUP * HD, cut), low[:, cols])
            total = part if total is None else total + part
            grad_out = dot_nn(mixed[p][...], low[:, cols]).astype(bf16)
            dout_ref[q, begin : begin + GROUP, e * HD : (e + 1) * HD, :] = grad_out.reshape(
                GROUP, HD, cut
            )
        dmixed[p][...] = total.astype(bf16)


def middle(hidden, feed, dnormed, cotangent, token_weight, gain, mixed, out, base):
    rows, parts = hidden.shape[0], len(mixed)
    cuts, shards, _, cut = out.shape
    here = HEADS // shards

    def whole(shape):
        return pl.BlockSpec(shape, lambda g: (0,) * len(shape), pipeline_mode=pl.Buffered(1))

    dout = (cuts, shards, here * HD, cut)
    return pl.pallas_call(
        functools.partial(middle_kernel, parts, here),
        grid=(1,),
        in_specs=[whole((rows, D))] * 4
        + [whole((rows, 1)), whole((1, D))]
        + [whole((GROUP * HD, rows))] * parts
        + out_specs_of(out, base, parts),
        out_specs=[whole((rows, D)), whole((rows, D)), whole(dout), whole((1, D))]
        + [whole((GROUP * HD, rows))] * parts,
        out_shape=[
            jax.ShapeDtypeStruct((rows, D), bf16),
            jax.ShapeDtypeStruct((rows, D), f32),
            jax.ShapeDtypeStruct(dout, bf16),
            jax.ShapeDtypeStruct((1, D), f32),
        ]
        + [jax.ShapeDtypeStruct((GROUP * HD, rows), bf16)] * parts,
        compiler_params=pltpu.CompilerParams(vmem_limit_bytes=50 << 20),
        name="middle",
    )(hidden, feed, dnormed, cotangent, token_weight, gain, *mixed, *([out] * parts))


def finish_kernel(
    block, own, halo, dwindow_ref, tokens_ref, normed_ref, dnormed_ref, grad_ref, gain_ref, latent_ref,
    rope_ref, cos_ref, sin_ref, *refs
):
    got, (dtokens_ref, dlatent_ref, dgain_ref) = refs[:halo], refs[halo:]
    at = LGROUPS * LAT
    grads = []
    for j in range(own):
        total = dwindow_ref[(halo + j) * block : (halo + j + 1) * block, :].astype(f32)
        for k in range(1, halo + 1):
            if own - 1 - (k - 1) % own == j:
                total = total + got[k - 1][...].astype(f32)
        grads.append(total)
    grad = jnp.concatenate(grads, axis=0)
    turned = rotate_lanes(grad[:, at:], cos_ref[...], -sin_ref[...])
    lane = lax.broadcasted_iota(jnp.int32, turned.shape, 1)
    turned = jnp.where(lane < HD, 0.0, turned).astype(bf16)
    grad = grad[:, :at].astype(bf16)
    dnormed = dnormed_ref[...] + dot_nt(grad, latent_ref[...])
    dnormed = dnormed + dot_nt(turned, rope_weight(rope_ref[...]))
    source = tokens_ref[...].astype(f32)
    dsource, dgain_ref[...] = norm_backward(source, gain_ref[...].astype(f32), dnormed)
    dtokens_ref[...] = grad_ref[...] + dsource
    dlatent_ref[:, :at] = dot_tn(normed_ref[...], grad).astype(bf16)
    dlatent_ref[:, at:] = dot_tn(normed_ref[...], turned).astype(bf16)


def finish(
    dwindow, got, tokens, normed, dnormed, grad_hidden, gain, w_latent, w_key_rope, cos, sin, block, own, halo
):
    rows = tokens.shape[0]
    return pl.pallas_call(
        functools.partial(finish_kernel, block, own, halo),
        out_shape=[
            jax.ShapeDtypeStruct((rows, D), f32),
            jax.ShapeDtypeStruct((D, LGROUPS * LAT + LANES), bf16),
            jax.ShapeDtypeStruct((1, D), f32),
        ],
        compiler_params=pltpu.CompilerParams(vmem_limit_bytes=60 << 20),
        name="finish",
    )(dwindow, tokens, normed, dnormed, grad_hidden, gain, w_latent, w_key_rope, cos, sin, *got)


def bits_of(size):
    return size.bit_length() - 1


def bit_pairs(size, bit):
    return [(i, i ^ (1 << bit)) for i in range(size)]


def upper_bit(axis, bit):
    return (lax.axis_index(axis) >> bit) & 1


def leading(shape):
    lead = [("rows", b) for b in reversed(range(bits_of(shape["rows"])))]
    return lead + [("heads", b) for b in reversed(range(bits_of(shape["heads"])))]


def gather_orders(shape):
    rows = [("rows", b) for b in reversed(range(1, bits_of(shape["rows"])))]
    heads = [("heads", b) for b in reversed(range(bits_of(shape["heads"])))]
    last = [("rows", 0)]
    return [
        heads + rows + last,
        heads[:1] + rows + heads[1:] + last,
        heads[-1:] + rows + heads[:-1] + last,
    ]


def flip(index, bit):
    size = 1 << bit
    return index + size * (1 - 2 * (index // size % 2))


def start_barrier(shape):
    barrier = pltpu.get_barrier_semaphore()
    for axis in ("rows", "heads"):
        for away in range(1, shape[axis]):
            pl.semaphore_signal(
                barrier,
                inc=1,
                device_id={axis: lax.rem(lax.axis_index(axis) + away, shape[axis])},
                device_id_type=pl.DeviceIdType.MESH,
            )
    pl.semaphore_wait(barrier, shape["rows"] + shape["heads"] - 2)


def exchange_index(lead, done, bits):
    return tuple(pl.ds(0, 2) if item in done else bits[item] for item in lead)


class Exchanges:

    def __init__(self, shape, plan, target, send_sem, recv_sem):
        self.orders, self.plan, self.target = gather_orders(shape), plan, target
        self.lead, self.stages = leading(shape), len(leading(shape))
        self.index = {axis: lax.axis_index(axis) for axis in ("rows", "heads")}
        self.bits = {
            (axis, bit): lax.rem(self.index[axis] // (1 << bit), 2) for axis, bit in self.lead
        }
        self.send_sem, self.recv_sem = send_sem, recv_sem
        self.times = max(item[0] for item in plan) + self.stages

    def mine(self):
        return self.target.at[exchange_index(self.lead, (), self.bits)]

    def copy(self, chunk, stage):
        _, order, begin, count = self.plan[chunk]
        axis, bit = self.orders[order][stage]
        held = exchange_index(self.lead, self.orders[order][:stage], self.bits)
        piece = self.target.at[held + (pl.ds(begin, count), slice(None))]
        return pltpu.make_async_remote_copy(
            src_ref=piece,
            dst_ref=piece,
            send_sem=self.send_sem.at[chunk * self.stages + stage],
            recv_sem=self.recv_sem.at[chunk * self.stages + stage],
            device_id={axis: flip(self.index[axis], bit)},
            device_id_type=pl.DeviceIdType.MESH,
        )

    def run(self, time):
        for chunk, item in enumerate(self.plan):
            stage = time - item[0]
            if 0 < stage <= self.stages:
                self.copy(chunk, stage - 1).wait()
            if 0 <= stage < self.stages:
                self.copy(chunk, stage).start()


def exchange_plan(rows, cuts):
    units, total, passed, plan = rows // 16, cuts * sum(SHARES), 0, []
    for i in range(cuts):
        for order, share in enumerate(SHARES):
            begin = 16 * (units * passed // total)
            passed += share
            plan.append((i, order, begin, 16 * (units * passed // total) - begin))
    return plan


def gather_kernel(
    shape, plan, block, own, halo, latent_ref, near_ref, window_ref, near_all,
    zero_s, local_sem, halo_send, halo_recv, send_sem, recv_sem,
):
    head = lax.axis_index("heads")
    exchanges = Exchanges(shape, plan, near_all, send_sem, recv_sem)
    zero_s[...] = jnp.zeros_like(zero_s)
    local = [
        pltpu.make_async_copy(near_ref, exchanges.mine(), local_sem.at[0]),
        pltpu.make_async_copy(
            latent_ref, window_ref.at[pl.ds(halo * block, own * block), :], local_sem.at[1]
        ),
    ]
    for copy in local:
        copy.start()
    start_barrier(shape)

    ahead = lax.rem(head * own, halo + 1)
    passed = []
    for k in range(1, halo + 1):
        back = -(-k // own)
        at = own - 1 - (k - 1) % own
        there = lax.rem(head + back, shape["heads"])
        copy = pltpu.make_async_remote_copy(
            src_ref=latent_ref.at[pl.ds(at * block, block), :],
            dst_ref=window_ref.at[pl.ds((halo - k) * block, block), :],
            send_sem=halo_send.at[k - 1],
            recv_sem=halo_recv.at[k - 1],
            device_id={"heads": there},
            device_id_type=pl.DeviceIdType.MESH,
        )
        blank = pltpu.make_async_copy(
            zero_s, window_ref.at[pl.ds((halo - k) * block, block), :], local_sem.at[2 + k]
        )
        goes = (head + back < shape["heads"]) & (lax.rem((head + back) * own, halo + 1) >= k)
        passed.append((copy, blank, goes, ahead >= k))

    for copy, blank, goes, comes in passed:

        @pl.when(goes)
        def _():
            copy.start()

        @pl.when(jnp.logical_not(comes))
        def _():
            blank.start()

    for copy in local:
        copy.wait()
    for time in range(exchanges.times + 1):
        exchanges.run(time)
    for copy, blank, goes, comes in passed:

        @pl.when(goes)
        def _():
            copy.wait_send()

        @pl.when(comes)
        def _():
            copy.wait_recv()

        @pl.when(jnp.logical_not(comes))
        def _():
            blank.wait()


def gather_near(shape, latent, near, block, own, halo):
    plan = exchange_plan(near.shape[0], 1)
    count = len(plan) * len(leading(shape))
    anywhere = pl.BlockSpec(memory_space=pl.ANY)
    outside = pl.BlockSpec(memory_space=pltpu.HBM)
    window, near_all = pl.pallas_call(
        functools.partial(gather_kernel, shape, plan, block, own, halo),
        in_specs=[anywhere] * 2,
        out_specs=[outside] * 2,
        out_shape=[
            jax.ShapeDtypeStruct(((halo + own) * block, latent.shape[1]), bf16),
            jax.ShapeDtypeStruct((2,) * len(leading(shape)) + near.shape, bf16),
        ],
        scratch_shapes=[
            pltpu.VMEM((block, latent.shape[1]), bf16),
            pltpu.SemaphoreType.DMA((3 + halo,)),
            pltpu.SemaphoreType.DMA((halo,)),
            pltpu.SemaphoreType.DMA((halo,)),
            pltpu.SemaphoreType.DMA((count,)),
            pltpu.SemaphoreType.DMA((count,)),
        ],
        compiler_params=pltpu.CompilerParams(
            collective_id=0, has_side_effects=True, vmem_limit_bytes=16 << 20
        ),
        name="gather_near",
    )(latent, near)
    return window, near_all.reshape((shape["rows"], shape["heads"]) + near.shape)


def attend_gather_kernel(
    shape, plan, groups, block, own, halo, normed_ref, weight_ref, cos_ref, sin_ref, latent_ref, rope_ref,
    up_ref, large_ref, mixed_ref, log_ref, q_ref, large_all, query_s, top_s, sum_s, local_sem, send_sem, recv_sem,
):
    part, parts = pl.program_id(0), HEADS // GROUP
    exchanges = Exchanges(shape, plan, large_all, send_sem, recv_sem)

    @pl.when(part == 0)
    def _():
        copy = pltpu.make_async_copy(large_ref, exchanges.mine(), local_sem.at[0])
        copy.start()
        start_barrier(shape)
        copy.wait()
        exchanges.run(0)

    def meanwhile(at):
        for p in range(parts):
            time = 1 + 2 * p + at

            @pl.when(part == p)
            def _():
                exchanges.run(time)

    ahead = lax.rem(lax.axis_index("heads") * own, halo + 1)
    forward_body(
        groups, block, own, halo, ahead, meanwhile, normed_ref, weight_ref, cos_ref, sin_ref, latent_ref,
        rope_ref, up_ref, mixed_ref, log_ref, q_ref, query_s, top_s, sum_s,
    )

    @pl.when(part == parts - 1)
    def _():
        for time in range(1 + 2 * parts, exchanges.times + 1):
            exchanges.run(time)


def attend_gather(shape, groups, normed, near, cos, sin, window, large, block, own, halo):
    rows, wide = own * block, (halo + own) * block
    cuts, shards, once = near.shape[0], near.shape[1], pl.Buffered(1)
    plan = exchange_plan(large.shape[0], CHUNKS)
    count = len(plan) * len(leading(shape))

    def whole(shape):
        return pl.BlockSpec(shape, lambda g: (0,) * len(shape), pipeline_mode=once)

    def heads_block(rows_at):
        return lambda g: (0, g * GROUP % shards // GROUP, rows_at, g * GROUP // shards)

    mixed, logs, queries, large_all = pl.pallas_call(
        functools.partial(attend_gather_kernel, shape, plan, groups, block, own, halo),
        grid=(HEADS // GROUP,),
        in_specs=[
            whole((rows, D)),
            pl.BlockSpec((cuts, GROUP, D // cuts, LANES), heads_block(0)),
            whole((rows, LANES)),
            whole((rows, LANES)),
            whole((wide, LGROUPS * LAT)),
            pl.BlockSpec((wide, LANES), lambda g: (0, LGROUPS * LAT // LANES), pipeline_mode=once),
            pl.BlockSpec((cuts, GROUP, LAT // cuts, LANES), heads_block(D // LAT)),
            pl.BlockSpec(memory_space=pl.ANY),
        ],
        out_specs=[
            pl.BlockSpec((None, GROUP * HD, rows), lambda g: (g, 0, 0)),
            pl.BlockSpec((None, GROUP, 1, rows), lambda g: (g, 0, 0, 0)),
            pl.BlockSpec((None, rows, GROUP * LANES), lambda g: (g, 0, 0)),
            pl.BlockSpec(memory_space=pltpu.HBM),
        ],
        out_shape=[
            jax.ShapeDtypeStruct((HEADS // GROUP, GROUP * HD, rows), bf16),
            jax.ShapeDtypeStruct((HEADS // GROUP, GROUP, 1, rows), f32),
            jax.ShapeDtypeStruct((HEADS // GROUP, rows, GROUP * LANES), bf16),
            jax.ShapeDtypeStruct((2,) * len(leading(shape)) + large.shape, bf16),
        ],
        scratch_shapes=[
            pltpu.VMEM((GROUP, LANES, rows), bf16),
            pltpu.VMEM((GROUP, 1, rows), f32),
            pltpu.VMEM((GROUP, TALL, rows), f32),
            pltpu.SemaphoreType.DMA((1,)),
            pltpu.SemaphoreType.DMA((count,)),
            pltpu.SemaphoreType.DMA((count,)),
        ],
        compiler_params=pltpu.CompilerParams(
            collective_id=2, has_side_effects=True, vmem_limit_bytes=60 << 20
        ),
        name="attend_gather",
    )(normed, near, cos, sin, window, window, near, large)
    large_all = large_all.reshape((shape["rows"], shape["heads"]) + large.shape)
    return [(mixed[p], logs[p], queries[p]) for p in range(HEADS // GROUP)], large_all


def feed_kernel(
    cuts, shards, units, side_ref, normed_ref, grad_ref, weight_ref, out_ref, dnormed_ref, kept_ref, sent_ref
):
    def whole(which):
        return jnp.concatenate(
            [
                jnp.concatenate(
                    [weight_ref[q, t, which * units : (which + 1) * units, :] for q in range(cuts)],
                    axis=1,
                )
                for t in range(shards)
            ],
            axis=0,
        )

    wide = D // cuts
    side = side_ref[0]

    def put(which, grad):
        at = slice(which * units, (which + 1) * units)
        for t in range(shards):
            rows = slice(t * units, (t + 1) * units)
            for q in range(cuts // 2):
                even = grad[rows, 2 * q * wide : (2 * q + 1) * wide].astype(bf16)
                odd = grad[rows, (2 * q + 1) * wide : (2 * q + 2) * wide].astype(bf16)
                kept_ref[q, t, at, :] = jnp.where(side == 0, even, odd)
                sent_ref[q, t, at, :] = jnp.where(side == 0, odd, even)

    @pl.when(pl.program_id(0) == 0)
    def _():
        out_ref[...] = jnp.zeros_like(out_ref)
        dnormed_ref[...] = jnp.zeros_like(dnormed_ref)

    normed = normed_ref[...]
    grad = grad_ref[...]
    w_gate, w_up, w_down = whole(0), whole(1), whole(2)
    gate = dot_nt(w_gate, normed)
    upper = dot_nt(w_up, normed)
    grad_inner = dot_nt(w_down, grad)
    sig = jax.nn.sigmoid(gate)
    silu = gate * sig
    inner = (silu * upper).astype(bf16)
    grad_gate = (grad_inner * upper * sig * (1.0 + gate * (1.0 - sig))).astype(bf16)
    grad_upper = (grad_inner * silu).astype(bf16)
    out_ref[...] += dot_tn(inner, w_down)
    dnormed_ref[...] += dot_tn(grad_gate, w_gate)
    dnormed_ref[...] += dot_tn(grad_upper, w_up)
    put(0, dot_nn(grad_gate, normed))
    put(1, dot_nn(grad_upper, normed))
    put(2, dot_nn(inner, grad))


def feed_forward_both(side, normed, grad, weights, units):
    rows = normed.shape[0]
    cuts, pieces, _, wide = weights.shape
    shards = max(1, min(pieces, 704 // units))
    once = pl.Buffered(1)
    half = (cuts // 2, shards, 3 * units, wide)
    whole = pl.BlockSpec((rows, D), lambda f, s: (0, 0), pipeline_mode=once)
    return pl.pallas_call(
        functools.partial(feed_kernel, cuts, shards, units),
        grid_spec=pltpu.PrefetchScalarGridSpec(
            num_scalar_prefetch=1,
            grid=(pieces // shards,),
            in_specs=[
                whole,
                whole,
                pl.BlockSpec((cuts, shards, 3 * units, wide), lambda f, s: (0, f, 0, 0)),
            ],
            out_specs=[
                whole,
                whole,
                pl.BlockSpec(half, lambda f, s: (0, f, 0, 0)),
                pl.BlockSpec(half, lambda f, s: (0, f, 0, 0)),
            ],
        ),
        out_shape=[
            jax.ShapeDtypeStruct((rows, D), f32),
            jax.ShapeDtypeStruct((rows, D), f32),
            jax.ShapeDtypeStruct((cuts // 2, pieces, 3 * units, wide), bf16),
            jax.ShapeDtypeStruct((cuts // 2, pieces, 3 * units, wide), bf16),
        ],
        compiler_params=pltpu.CompilerParams(vmem_limit_bytes=60 << 20),
        cost_estimate=pl.CostEstimate(
            flops=40 * 10**9, bytes_accessed=50 * 10**6, transcendentals=0
        ),
        name="feed_forward_both",
    )(side, normed, grad, weights)


def scatter_orders(shape):
    return [order[::-1] for order in gather_orders(shape)]


class Scatter:

    def __init__(self, shape, order, array, started=None):
        self.shape = shape
        self.order = list(scatter_orders(shape)[order])
        self.lead = leading(shape)
        self.terms = [array]
        if started is not None:
            self.order.pop(0)
            self.lead.remove(("rows", 0))
            self.terms = [array, started]
        self.terms = [t.reshape((2,) * len(self.lead) + t.shape[2:]) for t in self.terms]

    def total(self, terms):
        if len(terms) == 1:
            return terms[0]
        return sum(t.astype(f32) for t in terms).astype(bf16)

    def halves(self):
        axis, bit = self.order[0]
        at = self.lead.index((axis, bit))
        upper = upper_bit(axis, bit)

        def half(which):
            return self.total(
                [lax.dynamic_index_in_dim(t, which, at, keepdims=False) for t in self.terms]
            )

        return half(upper), half(1 - upper)

    def send(self, kept, sent):
        axis, bit = self.order.pop(0)
        self.lead.remove((axis, bit))
        self.terms = [kept, lax.ppermute(sent, axis, bit_pairs(self.shape[axis], bit))]

    def left(self):
        perm = [self.lead.index(item) for item in self.order]
        array = self.total(self.terms)
        array = array.transpose(perm + list(range(len(perm), array.ndim)))
        return array.reshape((2 ** len(perm),) + array.shape[len(perm) :])


def step_all(scatters, tied):
    halves = [scatter.halves() for scatter in scatters]
    sent, tied = lax.optimization_barrier(([half[1] for half in halves], tied))
    for scatter, half, out in zip(scatters, halves, sent):
        scatter.send(half[0], out)
    return tied


def scatter_kernel(shape, orders, *refs):
    count = len(orders)
    arrays, outs = refs[:count], refs[count : 2 * count]
    scratch, (send_sem, recv_sem) = list(refs[2 * count : -2]), refs[-2:]
    index = {"rows": lax.axis_index("rows"), "heads": lax.axis_index("heads")}
    start_barrier(shape)
    held, flying = list(arrays), [None] * count
    semaphore = 0
    for stage in range(max(len(order) for order in orders) + 1):
        for i, order in enumerate(orders):
            if flying[i] is not None:
                copy, kept, landed, begin, half = flying[i]
                copy.wait()
                flying[i] = None
                if stage < len(order):
                    summed = scratch.pop(0)

                    def add(at, _):
                        both = kept[begin + at].astype(f32) + landed[at].astype(f32)
                        summed[at] = both.astype(bf16)
                        return 0

                    lax.fori_loop(0, half, add, 0)
                    held[i] = summed
                else:
                    outs[i][...] = kept[begin].astype(f32) + landed[0].astype(f32)
            if stage < len(order):
                axis, bit = order[stage]
                upper = lax.rem(index[axis] // (1 << bit), 2)
                half = held[i].shape[0] // 2
                landed = scratch.pop(0)
                copy = pltpu.make_async_remote_copy(
                    src_ref=held[i].at[pl.ds((1 - upper) * half, half)],
                    dst_ref=landed,
                    send_sem=send_sem.at[semaphore],
                    recv_sem=recv_sem.at[semaphore],
                    device_id={axis: flip(index[axis], bit)},
                    device_id_type=pl.DeviceIdType.MESH,
                )
                copy.start()
                flying[i] = (copy, held[i], landed, upper * half, half)
                semaphore += 1


def scatter_rest(shape, scatters):
    orders = [tuple(scatter.order) for scatter in scatters]
    arrays = [scatter.left() for scatter in scatters]
    scratch = []
    for stage in range(max(len(order) for order in orders) + 1):
        for order, array in zip(orders, arrays):
            tail = array.shape[1:]
            if 0 < stage < len(order):
                scratch.append(pltpu.VMEM((array.shape[0] >> stage,) + tail, bf16))
            if stage < len(order):
                scratch.append(pltpu.VMEM((array.shape[0] >> (stage + 1),) + tail, bf16))
    total = sum(len(order) for order in orders)
    inside = pl.BlockSpec(memory_space=pltpu.VMEM)
    return pl.pallas_call(
        functools.partial(scatter_kernel, shape, orders),
        in_specs=[inside] * len(arrays),
        out_specs=[inside] * len(arrays),
        out_shape=[jax.ShapeDtypeStruct(array.shape[1:], f32) for array in arrays],
        scratch_shapes=scratch
        + [pltpu.SemaphoreType.DMA((total,)), pltpu.SemaphoreType.DMA((total,))],
        compiler_params=pltpu.CompilerParams(
            collective_id=1, has_side_effects=True, vmem_limit_bytes=48 << 20
        ),
        name="scatter_rest",
    )(*arrays)


def on_device(
    shape,
    tokens,
    cotangent,
    domain,
    group_weight,
    gain_attn,
    w_query,
    w_query_rope,
    w_latent,
    w_key_rope,
    w_key_up,
    w_value_up,
    w_out,
    gain_mlp,
    w_gate,
    w_up,
    w_down,
):
    n_rows, n_heads = shape["rows"], shape["heads"]
    row_at, head_at = lax.axis_index("rows"), lax.axis_index("heads")
    local = tokens.shape[0]
    block = math.gcd(local, LEN)
    own, halo = local // block, LEN // block - 1
    here = w_query.shape[1] // HD
    units = w_gate.shape[1]
    cut = D // n_rows
    half = RD // 2

    head_of = [(i % n_heads) * here + i // n_heads for i in range(HEADS)]
    group_of = [head // GROUP for head in head_of]
    parts = [tuple(group_of[p * GROUP : (p + 1) * GROUP]) for p in range(HEADS // GROUP)]

    start = head_at * local
    positions = ((start + jnp.arange(local)) % LEN).astype(f32)
    frequency = THETA ** (-(jnp.arange(LANES) % half).astype(f32) / half)
    angles = positions[:, None] * frequency[None, :]
    cos, sin = jnp.cos(angles), jnp.sin(angles)
    ahead = start // block % (LEN // block)
    places = jnp.stack([ahead, jnp.minimum(LEN // block - ahead, own)]).astype(jnp.int32)

    gain_one, gain_two = gain_attn.reshape(1, D), gain_mlp.reshape(1, D)
    normed, latent = prepare(tokens, gain_one, w_latent, w_key_rope, cos, sin)

    def halo_pairs(k):
        back = -(-k // own)
        needs = [i for i in range(n_heads) if (i * local % LEN) // block >= k]
        return [(i - back, i) for i in needs]

    direct = cut % LANES == 0 and GROUP % n_heads == 0
    if direct:
        near, large = pack(
            row_at.astype(jnp.int32).reshape(1),
            n_rows, w_query, w_query_rope, w_key_up, w_value_up, w_out, w_gate, w_up, w_down,
        )
        window, near = gather_near(shape, latent, near, block, own, halo)
        out, base = near, (D + LAT) // n_rows
    else:
        pieces = []
        for k in range(halo, 0, -1):
            at = own - 1 - (k - 1) % own
            pieces.append(
                lax.ppermute(latent[at * block : (at + 1) * block], "heads", halo_pairs(k))
            )
        window = jnp.concatenate(pieces + [latent], axis=0)
        queries = jnp.concatenate(
            [
                w_query.reshape(D, here, HD),
                w_query_rope.reshape(D, here, RD),
                jnp.zeros((D, here, LANES - HD - RD), bf16),
            ],
            axis=2,
        ).reshape(n_rows, cut, here * LANES)
        ups = jnp.concatenate(
            [w_key_up.reshape(LAT, here, HD), w_value_up.reshape(LAT, here, HD)], axis=2
        ).reshape(n_rows, LAT // n_rows, here * LANES)
        near = jnp.concatenate([queries, ups], axis=1)
        near = lax.all_gather(near, "heads", axis=1)
        out, base = lax.all_gather(w_out, "heads", axis=0)[None], 0
        large = jnp.concatenate([w_gate.T, w_up.T, w_down], axis=0)
        large = lax.all_gather(large, "heads", axis=0).reshape(n_heads, 3 * units, 2, D // 2)
        large = large.transpose(2, 0, 1, 3)

    if direct:
        forward, large = attend_gather(
            shape, parts[0], normed, near, cos, sin, window, large, block, own, halo
        )
    else:
        forward = [
            attend_forward(p, groups, places, normed, near, cos, sin, window, block, own, halo)
            for p, groups in enumerate(parts)
        ]
    mixed = [f[0] for f in forward]
    hidden, normed_mlp = join(tokens, gain_two, mixed, out, base)

    seq_weights = jnp.sum(
        (domain[:, None] == jnp.arange(group_weight.shape[0])[None, :]).astype(f32)
        * group_weight[None, :],
        axis=1,
    )
    token_seq = (start + jnp.arange(local)) // LEN
    token_weight = jnp.sum(
        (token_seq[:, None] == jnp.arange(domain.shape[0])[None, :]).astype(f32)
        * seq_weights[None, :],
        axis=1,
    )[:, None]
    grad_low = (cotangent.astype(f32) * token_weight).astype(bf16)
    core = upper_bit("rows", 0)
    side = core if direct else jnp.zeros_like(core)
    feed_out, grad_normed_mlp, feed_kept, feed_sent = feed_forward_both(
        side.astype(jnp.int32).reshape(1), normed_mlp, grad_low, large, units
    )
    if not direct:
        grad_feed = jnp.concatenate([feed_kept[0], feed_sent[0]], axis=2)
        grad_feed = grad_feed.reshape(n_heads, 3 * units, n_rows // 2, 2, cut)
        grad_feed = grad_feed.transpose(3, 2, 0, 1, 4)
        feed_kept = lax.dynamic_index_in_dim(grad_feed, core, 0, keepdims=False)
        feed_sent = lax.dynamic_index_in_dim(grad_feed, 1 - core, 0, keepdims=False)
    feed_got = lax.ppermute(feed_sent, "rows", bit_pairs(n_rows, 0))
    half_way = 3 * units // 2
    scatter_feed = [
        Scatter(shape, 0, feed_kept[:, :, :half_way], feed_got[:, :, :half_way]),
        Scatter(shape, 1, feed_kept[:, :, half_way:], feed_got[:, :, half_way:]),
    ]
    block_output, grad_hidden, grad_out, grad_gain_two, *grad_mixed = middle(
        hidden, feed_out, grad_normed_mlp, cotangent, token_weight, gain_two, mixed, out, base
    )
    if not direct:
        grad_out = grad_out.reshape(n_heads, here * HD, n_rows, cut).transpose(2, 0, 1, 3)

    by_part = GROUP % n_heads == 0
    scatter_near, pieces, before = [], [], None
    scatter_out = Scatter(shape, 0, grad_out)
    for p, groups in enumerate(parts):
        under_way = scatter_feed + ([scatter_out] + scatter_near if p else [])
        grad_mixed[p] = step_all(under_way, grad_mixed[p])
        *before, grad_near = attend_backward(
            p, groups, places, forward[p], normed, near, cos, sin, window, grad_mixed[p], before,
            block, own, halo,
        )
        if by_part:
            scatter_near.append(Scatter(shape, 1, grad_near))
        else:
            pieces.append(grad_near)
    if not by_part:
        scatter_near.append(Scatter(shape, 1, jnp.concatenate(pieces, axis=1)))
    grad_window, grad_normed = before
    got = [
        lax.ppermute(
            grad_window[(halo - k) * block : (halo - k + 1) * block],
            "heads",
            [(b, a) for a, b in halo_pairs(k)],
        )
        for k in range(1, halo + 1)
    ]
    grad_normed = step_all(scatter_feed + [scatter_out] + scatter_near, grad_normed)
    grad_tokens, grad_latent, grad_gain_one = finish(
        grad_window, got, tokens, normed, grad_normed, grad_hidden, gain_one, w_latent, w_key_rope, cos, sin,
        block, own, halo,
    )
    gains = jnp.concatenate([grad_gain_one, grad_gain_two], axis=0).astype(bf16)
    gains = gains.reshape(2, n_rows, n_heads, -1).transpose(1, 2, 0, 3)
    gains = jnp.pad(gains, ((0, 0), (0, 0), (0, 14), (0, LANES - gains.shape[3])))
    grad_latent = grad_latent.reshape(n_rows, n_heads, D // (n_rows * n_heads), -1)
    own_first, own_second, own_out, own_latent, own_gain, *own_near = scatter_rest(
        shape,
        scatter_feed
        + [scatter_out, Scatter(shape, 0, grad_latent), Scatter(shape, 1, gains)]
        + scatter_near,
    )
    own_feed = jnp.concatenate([own_first, own_second], axis=0)
    own_near = jnp.concatenate(own_near, axis=1)
    own_query = own_near[:cut].reshape(cut, here, LANES)
    own_up = own_near[cut:].reshape(LAT // n_rows, here, LANES)
    at, gain_cut = LGROUPS * LAT, D // (n_rows * n_heads)
    return (
        block_output,
        grad_tokens,
        own_gain[0, :gain_cut],
        own_query[:, :, :HD].reshape(cut, here * HD),
        own_query[:, :, HD : HD + RD].reshape(cut, here * RD),
        own_latent[:, :at],
        own_latent[:, at + HD : at + HD + RD],
        own_up[:, :, :HD].reshape(LAT // n_rows, here * HD),
        own_up[:, :, HD:].reshape(LAT // n_rows, here * HD),
        own_out,
        own_gain[1, :gain_cut],
        own_feed[:units].T,
        own_feed[units : 2 * units].T,
        own_feed[2 * units :],
    )


def solution(mesh):
    in_specs = (
        P(("rows", "heads"), None),
        P(("rows", "heads"), None),
        P("rows"),
        P(),
        P(),
        P(None, "heads"),
        P(None, "heads"),
        P(),
        P(),
        P(None, "heads"),
        P(None, "heads"),
        P("heads", None),
        P(),
        P(None, "heads"),
        P(None, "heads"),
        P("heads", None),
    )
    out_specs = (
        P(("rows", "heads"), None),
        P(("rows", "heads"), None),
        P(("rows", "heads")),
        P("rows", "heads"),
        P("rows", "heads"),
        P(("rows", "heads"), None),
        P(("rows", "heads"), None),
        P("rows", "heads"),
        P("rows", "heads"),
        P("heads", "rows"),
        P(("rows", "heads")),
        P("rows", "heads"),
        P("rows", "heads"),
        P("heads", "rows"),
    )
    return jax.shard_map(
        functools.partial(on_device, dict(mesh.shape)),
        mesh=mesh,
        in_specs=in_specs,
        out_specs=out_specs,
        check_vma=False,
    )
```

```python
import functools
import math

import jax
import jax.numpy as jnp
from jax import lax
from jax.experimental import pallas as pl
from jax.experimental.pallas import tpu as pltpu
from jax.sharding import PartitionSpec as P

D = 1024
HEADS = 16
HD = 64
LGROUPS = 2
LAT = 256
RD = 32
LEN = 2048
EPS = 1e-05
THETA = 10000.0
NEG_LARGE = -1e30
LANES = 128
PAIR = 2
GROUP = HEADS // LGROUPS
TALL = 80
CHUNKS = 4
SHARES = (2, 2, 1)
LOG2E = math.log2(math.e)
LN2 = math.log(2.0)
SCALE = (HD + RD) ** (-0.5)

bf16 = jnp.bfloat16
f32 = jnp.float32


def dot_nn(a, b):
    return jnp.dot(a, b, preferred_element_type=f32)


def dot_nt(a, b):
    return lax.dot_general(a, b, (((1,), (1,)), ((), ())), preferred_element_type=f32)


def dot_tn(a, b):
    return lax.dot_general(a, b, (((0,), (0,)), ((), ())), preferred_element_type=f32)


def rms_scale(values):
    return lax.rsqrt(jnp.mean(values * values, axis=-1, keepdims=True) + EPS)


def rotate_lanes(values, cos, sin):
    lane = lax.broadcasted_iota(jnp.int32, values.shape, 1)
    turned = (lane >= HD) & (lane < HD + RD)
    cos = jnp.where(lane < HD, 1.0, jnp.where(turned, cos, 0.0))
    sin = jnp.where(turned, sin, 0.0)
    half = RD // 2
    swapped = jnp.where(
        lane < HD + half, -pltpu.roll(values, LANES - half, 1), pltpu.roll(values, half, 1)
    )
    return values * cos + swapped * sin


def rope_weight(w_key_rope):
    blank = jnp.zeros((HD, w_key_rope.shape[1]), bf16)
    return jnp.concatenate([blank, w_key_rope, blank[: LANES - HD - RD]], axis=0)


def prepare_kernel(tokens_ref, gain_ref, latent_ref, rope_ref, cos_ref, sin_ref, normed_ref, out_ref):
    source = tokens_ref[...].astype(f32)
    normed = (source * rms_scale(source) * gain_ref[...].astype(f32)).astype(bf16)
    normed_ref[...] = normed
    out_ref[:, : LGROUPS * LAT] = dot_nn(normed, latent_ref[...]).astype(bf16)
    turned = rotate_lanes(dot_nt(normed, rope_weight(rope_ref[...])), cos_ref[...], sin_ref[...])
    out_ref[:, LGROUPS * LAT :] = turned.astype(bf16)


def prepare(tokens, gain, w_latent, w_key_rope, cos, sin):
    rows = tokens.shape[0]
    return pl.pallas_call(
        prepare_kernel,
        out_shape=[
            jax.ShapeDtypeStruct((rows, D), bf16),
            jax.ShapeDtypeStruct((rows, LGROUPS * LAT + LANES), bf16),
        ],
        compiler_params=pltpu.CompilerParams(vmem_limit_bytes=40 << 20),
        name="prepare",
    )(tokens, gain, w_latent, w_key_rope, cos, sin)


def pack_kernel(
    here, side_ref, query_ref, rope_ref, key_ref, value_ref, out_ref, gate_ref, up_ref, down_ref,
    near_ref, large_ref,
):
    units, cut = gate_ref.shape
    blank = jnp.zeros((cut, LANES - HD - RD), bf16)
    small = key_ref.shape[0]
    turned = rope_ref[...].T
    for e in range(here):
        lanes = slice(e * LANES, (e + 1) * LANES)
        heads, turns = slice(e * HD, (e + 1) * HD), slice(e * RD, (e + 1) * RD)
        near_ref[:cut, lanes] = jnp.concatenate(
            [query_ref[:, heads], turned[:, turns], blank], axis=1
        )
        near_ref[cut : cut + small, lanes] = jnp.concatenate(
            [key_ref[:, heads], value_ref[:, heads]], axis=1
        )
    near_ref[cut + small :, :] = out_ref[...]
    large_ref[:units, :] = gate_ref[...]
    large_ref[units : 2 * units, :] = up_ref[...]
    large_ref[2 * units :, :] = down_ref[...]


def pack(side, n_rows, w_query, w_query_rope, w_key_up, w_value_up, w_out, w_gate, w_up, w_down):
    here, units = w_query.shape[1] // HD, w_gate.shape[0]
    cut, small = D // n_rows, LAT // n_rows

    def by_rows(weight):
        tall = weight.shape[0] // n_rows
        return pl.BlockSpec((tall, weight.shape[1]), lambda g, s: (s[0], 0))

    def by_columns(weight):
        return pl.BlockSpec((weight.shape[0], cut), lambda g, s: (0, s[0]))

    near = (cut + small + here * HD, here * LANES)
    large = (3 * units, cut)
    return pl.pallas_call(
        functools.partial(pack_kernel, here),
        grid_spec=pltpu.PrefetchScalarGridSpec(
            num_scalar_prefetch=1,
            grid=(1,),
            in_specs=[
                by_rows(w_query),
                by_columns(w_query_rope),
                by_rows(w_key_up),
                by_rows(w_value_up),
                by_columns(w_out),
                by_columns(w_gate),
                by_columns(w_up),
                by_columns(w_down),
            ],
            out_specs=[
                pl.BlockSpec(near, lambda g, s: (0, 0)),
                pl.BlockSpec(large, lambda g, s: (0, 0)),
            ],
        ),
        out_shape=[jax.ShapeDtypeStruct(near, bf16), jax.ShapeDtypeStruct(large, bf16)],
        name="pack",
    )(side, w_query, w_query_rope, w_key_up, w_value_up, w_out, w_gate, w_up, w_down)


def keys_values(groups, window_ref, up_of, rows, count):
    rope = window_ref[rows, LGROUPS * LAT :]
    lane = lax.broadcasted_iota(jnp.int32, (count, LANES), 1)
    keys, values = [], []
    for e in range(0, GROUP, PAIR):
        latent = window_ref[rows, groups[e] * LAT : (groups[e] + 1) * LAT]
        up = jnp.concatenate([up_of(e + i) for i in range(PAIR)], axis=1)
        wide = dot_nn(latent, up).astype(bf16)
        for i in range(PAIR):
            both = wide[:, i * LANES : (i + 1) * LANES]
            keys.append(jnp.where(lane < HD, both, rope))
            values.append(both)
    return keys, values


def values_ones(value):
    count = value.shape[0]
    return jnp.concatenate([value.T[HD:], jnp.ones((TALL - HD, count), bf16)], axis=0)


def shard_block(part, shards, rows_at):
    return lambda g, p: (0, part * GROUP % shards // GROUP, rows_at, part * GROUP // shards)


def forward_body(
    groups, block, own, halo, ahead, meanwhile, weight_of, up_of, normed_ref, cos_ref, sin_ref, window_ref,
    mixed_ref, log_ref, q_ref, query_s, top_s, sum_s,
):
    rows = own * block
    until = halo + 1 - ahead
    weight = jnp.concatenate([weight_of(e) for e in range(GROUP)], axis=1)
    raw = dot_nn(normed_ref[...], weight)
    for e in range(GROUP):
        lanes = slice(e * LANES, (e + 1) * LANES)
        query = rotate_lanes(raw[:, lanes], cos_ref[...], sin_ref[...])
        query = (query * (SCALE * LOG2E)).astype(bf16)
        q_ref[:, lanes] = query
        query_s[e] = query.T
    keys, values = keys_values(
        groups, window_ref, up_of, slice(halo * block, (halo + own) * block), rows
    )
    values = [values_ones(value) for value in values]
    for j in range(own):
        count = (j + 1) * block
        key_at = lax.broadcasted_iota(jnp.int32, (count, block), 0)
        query_at = lax.broadcasted_iota(jnp.int32, (count, block), 1) + j * block
        keep = (key_at <= query_at) & (key_at >= jnp.where(j >= until, until * block, 0))
        cols = slice(j * block, count)
        scores = [
            jnp.where(keep, dot_nn(keys[e][:count], query_s[e, :, cols]), NEG_LARGE)
            for e in range(GROUP)
        ]
        for e in range(GROUP):
            top = jnp.max(scores[e], axis=0, keepdims=True)
            terms = jnp.exp2(scores[e] - top).astype(bf16)
            top_s[e, :, cols] = top
            sum_s[e, :, cols] = dot_nn(values[e][:, :count], terms)
    meanwhile(0)
    for blocks in range(1, own + 1):
        wide = blocks * block

        def step(index, _):
            at = pl.ds(pl.multiple_of(index * block, block), block)
            keys, values = keys_values(groups, window_ref, up_of, at, block)
            values = [values_ones(value) for value in values]
            scores = [dot_nn(keys[e], query_s[e, :, :wide]) for e in range(GROUP)]
            for e in range(GROUP):
                top = top_s[e, :, :wide]
                higher = jnp.maximum(top, jnp.max(scores[e], axis=0, keepdims=True))
                shrink = jnp.exp2(top - higher)
                terms = jnp.exp2(scores[e] - higher).astype(bf16)
                top_s[e, :, :wide] = higher
                sum_s[e, :, :wide] = sum_s[e, :, :wide] * shrink + dot_nn(values[e], terms)
            return 0

        @pl.when(until == blocks if blocks < own else until >= own)
        def _():
            lax.fori_loop(halo - ahead, halo, step, 0)

    meanwhile(1)
    for e in range(GROUP):
        total = sum_s[e]
        sums = total[HD : HD + 1]
        mixed_ref[e * HD : (e + 1) * HD, :] = (total[:HD] * (1.0 / sums)).astype(bf16)
        log_ref[e] = top_s[e] + jnp.log2(sums)


def attend_forward_kernel(groups, block, own, halo, place_ref, weight_ref, up_ref, *refs):
    forward_body(
        groups, block, own, halo, place_ref[0], lambda at: None,
        lambda e: weight_ref[:, e].reshape(D, LANES),
        lambda e: up_ref[:, e].reshape(LAT, LANES),
        *refs,
    )


def attend_forward(part, groups, places, normed, near, cos, sin, window, block, own, halo):
    rows, wide = own * block, (halo + own) * block
    cuts, shards, once = near.shape[0], near.shape[1], pl.Buffered(1)

    def whole(shape):
        return pl.BlockSpec(shape, lambda g, p: (0,) * len(shape), pipeline_mode=once)

    return pl.pallas_call(
        functools.partial(attend_forward_kernel, groups, block, own, halo),
        grid_spec=pltpu.PrefetchScalarGridSpec(
            num_scalar_prefetch=1,
            grid=(1,),
            in_specs=[
                pl.BlockSpec(
                    (cuts, GROUP, D // cuts, LANES),
                    shard_block(part, shards, 0),
                    pipeline_mode=once,
                ),
                pl.BlockSpec(
                    (cuts, GROUP, LAT // cuts, LANES),
                    shard_block(part, shards, D // LAT),
                    pipeline_mode=once,
                ),
                whole((rows, D)),
                whole((rows, LANES)),
                whole((rows, LANES)),
                whole((wide, LGROUPS * LAT + LANES)),
            ],
            out_specs=[
                whole((GROUP * HD, rows)),
                whole((GROUP, 1, rows)),
                whole((rows, GROUP * LANES)),
            ],
            scratch_shapes=[
                pltpu.VMEM((GROUP, LANES, rows), bf16),
                pltpu.VMEM((GROUP, 1, rows), f32),
                pltpu.VMEM((GROUP, TALL, rows), f32),
            ],
        ),
        out_shape=[
            jax.ShapeDtypeStruct((GROUP * HD, rows), bf16),
            jax.ShapeDtypeStruct((GROUP, 1, rows), f32),
            jax.ShapeDtypeStruct((rows, GROUP * LANES), bf16),
        ],
        compiler_params=pltpu.CompilerParams(vmem_limit_bytes=56 << 20),
        name="attend_forward",
    )(places, near, near, normed, cos, sin, window)


def attend_backward_kernel(
    groups, block, own, halo, carried, place_ref, q_ref, window_ref, up_ref, mixed_ref, log_ref,
    grad_ref, cos_ref, sin_ref, normed_ref, weight_ref, *refs
):
    before = refs[:2] if carried else None
    dwindow_ref, dnormed_ref, dnear_ref, query_s, grad_s, inner_s, dquery_s, both_s, rope_s = refs[-9:]
    rows = own * block
    ahead, until = place_ref[0], place_ref[1]
    first = halo - ahead

    def up_of(e):
        return up_ref[:, e].reshape(LAT, LANES)

    rope_s[...] = jnp.zeros_like(rope_s)

    def clear(index, _):
        at = pl.ds(pl.multiple_of(index * block, block), block)
        both_s[at, :] = jnp.zeros((block, GROUP * LANES), bf16)
        return 0

    lax.fori_loop(0, first, clear, 0)
    for e in range(GROUP):
        query_s[e] = q_ref[:, e * LANES : (e + 1) * LANES].T
        grad = grad_ref[e * HD : (e + 1) * HD, :]
        grad_s[e] = jnp.concatenate([jnp.zeros((rows, HD), bf16), grad.T], axis=1)
        inner_s[e] = jnp.sum(
            grad.astype(f32) * mixed_ref[e * HD : (e + 1) * HD, :].astype(f32),
            axis=0,
            keepdims=True,
        )
        dquery_s[e] = jnp.zeros((LANES, rows), f32)
    lane = lax.broadcasted_iota(jnp.int32, (block, LANES), 1)

    def strip(at, low, high, keep):
        cols = slice(low, high)
        keys, values = keys_values(groups, window_ref, up_of, at, block)
        scores = [dot_nn(keys[e], query_s[e, :, cols]) for e in range(GROUP)]
        grads = [
            dot_nn(values[e][:, HD:], grad_ref[e * HD : (e + 1) * HD, cols]) for e in range(GROUP)
        ]
        grad_rope = None
        for e in range(GROUP):
            score = scores[e] if keep is None else jnp.where(keep, scores[e], NEG_LARGE)
            probs = jnp.exp2(score - log_ref[e, :, cols])
            grad_scores = (probs * (grads[e] - inner_s[e, :, cols])).astype(bf16)
            grad_value = dot_nn(probs.astype(bf16), grad_s[e, cols, :])
            grad_key = dot_nn(grad_scores, q_ref[cols, e * LANES : (e + 1) * LANES]) * LN2
            dquery_s[e, :, cols] += dot_nn(keys[e].T, grad_scores)
            both_s[at, e * LANES : (e + 1) * LANES] = jnp.where(
                lane < HD, grad_key, grad_value
            ).astype(bf16)
            grad_rope = grad_key if grad_rope is None else grad_rope + grad_key
        rope_s[at, :] = grad_rope

    for i in range(own):
        count = rows - i * block
        key_at = lax.broadcasted_iota(jnp.int32, (block, count), 0)
        query_at = lax.broadcasted_iota(jnp.int32, (block, count), 1)
        keep = (key_at <= query_at) & (query_at < jnp.where(i < until, (until - i) * block, rows))
        strip(slice((halo + i) * block, (halo + i + 1) * block), i * block, rows, keep)
    for blocks in range(1, own + 1):

        def step(index, _):
            strip(pl.ds(pl.multiple_of(index * block, block), block), 0, blocks * block, None)
            return 0

        lax.fori_loop(jnp.where(until == blocks, first, halo), halo, step, 0)
    grads = []
    for e in range(GROUP):
        grad = rotate_lanes(dquery_s[e].T * SCALE, cos_ref[...], -sin_ref[...])
        grads.append(grad.astype(bf16))
    dquery = jnp.concatenate(grads, axis=1)
    cuts = weight_ref.shape[0]
    cut, small = D // cuts, LAT // cuts
    for q in range(cuts):
        weight = jnp.concatenate([weight_ref[q, e] for e in range(GROUP)], axis=1)
        part = dot_nt(dquery, weight)
        if carried:
            part = part + before[1][:, q * cut : (q + 1) * cut]
        dnormed_ref[:, q * cut : (q + 1) * cut] = part
    grad = dot_tn(normed_ref[...], dquery).astype(bf16)
    for q in range(cuts):
        for e in range(GROUP):
            dnear_ref[q, e, :cut, :] = grad[q * cut : (q + 1) * cut, e * LANES : (e + 1) * LANES]
    for group in range(LGROUPS):
        at = slice(group * LAT, (group + 1) * LAT)
        heads = [e for e in range(GROUP) if groups[e] == group]
        if heads:
            lanes = slice(heads[0] * LANES, (heads[-1] + 1) * LANES)
            up = jnp.concatenate([up_of(e) for e in heads], axis=1)
            grad = dot_nt(both_s[:, lanes], up)
            dup = dot_nn(window_ref[:, at].T, both_s[:, lanes]).astype(bf16)
            for q in range(cuts):
                for i, e in enumerate(heads):
                    dnear_ref[q, e, cut:, :] = dup[
                        q * small : (q + 1) * small, i * LANES : (i + 1) * LANES
                    ]
        else:
            grad = jnp.zeros((dwindow_ref.shape[0], LAT), f32)
        if carried:
            grad = grad + before[0][:, at].astype(f32)
        dwindow_ref[:, at] = grad.astype(bf16)
    grad = rope_s[...]
    if carried:
        grad = grad + before[0][:, LGROUPS * LAT :].astype(f32)
    dwindow_ref[:, LGROUPS * LAT :] = grad.astype(bf16)


def attend_backward(
    part, groups, places, forward, normed, near, cos, sin, window, grad_mixed, before, block, own, halo
):
    rows, wide = own * block, (halo + own) * block
    cuts, shards, once = near.shape[0], near.shape[1], pl.Buffered(1)
    near_rows = (D + LAT) // cuts
    lanes = LGROUPS * LAT + LANES
    mixed, logs, queries = forward

    def whole(shape):
        return pl.BlockSpec(shape, lambda g, p: (0,) * len(shape), pipeline_mode=once)

    def of_part(shape):
        return pl.BlockSpec(
            (None,) + shape, lambda g, p: (part,) + (0,) * len(shape), pipeline_mode=once
        )

    return pl.pallas_call(
        functools.partial(attend_backward_kernel, groups, block, own, halo, before is not None),
        grid_spec=pltpu.PrefetchScalarGridSpec(
            num_scalar_prefetch=1,
            grid=(1,),
            in_specs=[
                of_part((rows, GROUP * LANES)),
                whole((wide, lanes)),
                pl.BlockSpec(
                    (cuts, GROUP, LAT // cuts, LANES),
                    shard_block(part, shards, D // LAT),
                    pipeline_mode=once,
                ),
                of_part((GROUP * HD, rows)),
                of_part((GROUP, 1, rows)),
                whole((GROUP * HD, rows)),
                whole((rows, LANES)),
                whole((rows, LANES)),
                whole((rows, D)),
                pl.BlockSpec(
                    (cuts, GROUP, D // cuts, LANES),
                    shard_block(part, shards, 0),
                    pipeline_mode=once,
                ),
            ]
            + ([] if before is None else [whole((wide, lanes)), whole((rows, D))]),
            out_specs=[
                whole((wide, lanes)),
                whole((rows, D)),
                whole((cuts, GROUP, near_rows, LANES)),
            ],
            scratch_shapes=[
                pltpu.VMEM((GROUP, LANES, rows), bf16),
                pltpu.VMEM((GROUP, rows, LANES), bf16),
                pltpu.VMEM((GROUP, 1, rows), f32),
                pltpu.VMEM((GROUP, LANES, rows), f32),
                pltpu.VMEM((wide, GROUP * LANES), bf16),
                pltpu.VMEM((wide, LANES), f32),
            ],
        ),
        out_shape=[
            jax.ShapeDtypeStruct((wide, lanes), bf16),
            jax.ShapeDtypeStruct((rows, D), f32),
            jax.ShapeDtypeStruct((cuts, GROUP, near_rows, LANES), bf16),
        ],
        compiler_params=pltpu.CompilerParams(vmem_limit_bytes=60 << 20),
        cost_estimate=pl.CostEstimate(
            flops=40 * 10**9, bytes_accessed=30 * 10**6, transcendentals=0
        ),
        name="attend_backward",
    )(
        places, queries, window, near, mixed, logs, grad_mixed, cos, sin, normed, near,
        *(before or ()),
    )


def join_kernel(parts, tokens_ref, gain_ref, *refs):
    mixed, weights, (hidden_ref, normed_ref) = refs[:parts], refs[parts : 2 * parts], refs[2 * parts :]
    cuts, _, _, cut = weights[0].shape
    squares = 0.0
    for q in range(cuts):
        cols = slice(q * cut, (q + 1) * cut)
        total = tokens_ref[:, cols].astype(f32)
        for m, w in zip(mixed, weights):
            total = total + dot_tn(m[...], w[q].reshape(GROUP * HD, cut))
        hidden_ref[:, cols] = total
        squares = squares + jnp.sum(total * total, axis=1, keepdims=True)
    scale = lax.rsqrt(squares * (1.0 / D) + EPS)
    normed_ref[...] = (hidden_ref[...] * scale * gain_ref[...].astype(f32)).astype(bf16)


def out_specs_of(out, base, parts):
    cuts, shards, _, cut = out.shape
    return [
        pl.BlockSpec(
            (cuts, GROUP, HD, cut),
            lambda g, part=part: (
                0, part * GROUP % shards // GROUP, base // HD + part * GROUP // shards, 0
            ),
            pipeline_mode=pl.Buffered(1),
        )
        for part in range(parts)
    ]


def join(tokens, gain, mixed, out, base):
    rows, parts = tokens.shape[0], mixed.shape[0]

    def whole(shape):
        return pl.BlockSpec(shape, lambda g: (0,) * len(shape), pipeline_mode=pl.Buffered(1))

    return pl.pallas_call(
        functools.partial(join_kernel, parts),
        grid=(1,),
        in_specs=[whole((rows, D)), whole((1, D))]
        + [
            pl.BlockSpec(
                (None, GROUP * HD, rows), lambda g, part=part: (part, 0, 0), pipeline_mode=pl.Buffered(1)
            )
            for part in range(parts)
        ]
        + out_specs_of(out, base, parts),
        out_specs=[whole((rows, D)), whole((rows, D))],
        out_shape=[
            jax.ShapeDtypeStruct((rows, D), f32),
            jax.ShapeDtypeStruct((rows, D), bf16),
        ],
        compiler_params=pltpu.CompilerParams(vmem_limit_bytes=32 << 20),
        name="join",
    )(tokens, gain, *([mixed] * parts), *([out] * parts))


def norm_backward(source, gain, grad_normed):
    scale = rms_scale(source)
    scaled = source * scale
    weighted = grad_normed * gain
    mean = jnp.mean(weighted * scaled, axis=-1, keepdims=True)
    return (
        scale * (weighted - scaled * mean),
        jnp.sum(grad_normed * scaled, axis=0, keepdims=True),
    )


def middle_kernel(parts, here, hidden_ref, feed_ref, dnormed_ref, cotangent_ref, weight_ref, gain_ref, *refs):
    mixed, weights = refs[:parts], refs[parts : 2 * parts]
    block_ref, grad_ref, dout_ref, dgain_ref = refs[2 * parts : 2 * parts + 4]
    dmixed = refs[2 * parts + 4 :]
    hidden = hidden_ref[...]
    block_ref[...] = (hidden + feed_ref[...]).astype(bf16)
    grad, dgain_ref[...] = norm_backward(hidden, gain_ref[...].astype(f32), dnormed_ref[...])
    grad = grad + cotangent_ref[...].astype(f32) * weight_ref[...]
    grad_ref[...] = grad
    low = grad.astype(bf16)
    cuts, _, _, cut = weights[0].shape
    shards = dout_ref.shape[1]
    for p in range(parts):
        e, begin = p * GROUP // shards, p * GROUP % shards
        total = None
        for q in range(cuts):
            cols = slice(q * cut, (q + 1) * cut)
            part = dot_nt(weights[p][q].reshape(GROUP * HD, cut), low[:, cols])
            total = part if total is None else total + part
            grad_out = dot_nn(mixed[p][...], low[:, cols]).astype(bf16)
            dout_ref[q, begin : begin + GROUP, e * HD : (e + 1) * HD, :] = grad_out.reshape(
                GROUP, HD, cut
            )
        dmixed[p][...] = total.astype(bf16)


def middle(hidden, feed, dnormed, cotangent, token_weight, gain, mixed, out, base):
    rows, parts = hidden.shape[0], mixed.shape[0]
    cuts, shards, _, cut = out.shape
    here = HEADS // shards

    def whole(shape):
        return pl.BlockSpec(shape, lambda g: (0,) * len(shape), pipeline_mode=pl.Buffered(1))

    dout = (cuts, shards, here * HD, cut)
    return pl.pallas_call(
        functools.partial(middle_kernel, parts, here),
        grid=(1,),
        in_specs=[whole((rows, D))] * 4
        + [whole((rows, 1)), whole((1, D))]
        + [
            pl.BlockSpec(
                (None, GROUP * HD, rows), lambda g, part=part: (part, 0, 0), pipeline_mode=pl.Buffered(1)
            )
            for part in range(parts)
        ]
        + out_specs_of(out, base, parts),
        out_specs=[whole((rows, D)), whole((rows, D)), whole(dout), whole((1, D))]
        + [whole((GROUP * HD, rows))] * parts,
        out_shape=[
            jax.ShapeDtypeStruct((rows, D), bf16),
            jax.ShapeDtypeStruct((rows, D), f32),
            jax.ShapeDtypeStruct(dout, bf16),
            jax.ShapeDtypeStruct((1, D), f32),
        ]
        + [jax.ShapeDtypeStruct((GROUP * HD, rows), bf16)] * parts,
        compiler_params=pltpu.CompilerParams(vmem_limit_bytes=50 << 20),
        name="middle",
    )(hidden, feed, dnormed, cotangent, token_weight, gain, *([mixed] * parts), *([out] * parts))


def finish_kernel(
    block, own, halo, dwindow_ref, tokens_ref, normed_ref, dnormed_ref, grad_ref, gain_ref, latent_ref,
    rope_ref, cos_ref, sin_ref, *refs
):
    got, (dtokens_ref, dlatent_ref, dgain_ref) = refs[:halo], refs[halo:]
    at = LGROUPS * LAT
    grads = []
    for j in range(own):
        total = dwindow_ref[(halo + j) * block : (halo + j + 1) * block, :].astype(f32)
        for k in range(1, halo + 1):
            if own - 1 - (k - 1) % own == j:
                total = total + got[k - 1][...].astype(f32)
        grads.append(total)
    grad = jnp.concatenate(grads, axis=0)
    turned = rotate_lanes(grad[:, at:], cos_ref[...], -sin_ref[...])
    lane = lax.broadcasted_iota(jnp.int32, turned.shape, 1)
    turned = jnp.where(lane < HD, 0.0, turned).astype(bf16)
    grad = grad[:, :at].astype(bf16)
    dnormed = dnormed_ref[...] + dot_nt(grad, latent_ref[...])
    dnormed = dnormed + dot_nn(turned, rope_weight(rope_ref[...]))
    source = tokens_ref[...].astype(f32)
    dsource, dgain_ref[...] = norm_backward(source, gain_ref[...].astype(f32), dnormed)
    dtokens_ref[...] = grad_ref[...] + dsource
    dlatent_ref[:, :at] = dot_tn(normed_ref[...], grad).astype(bf16)
    dlatent_ref[:, at:] = dot_tn(normed_ref[...], turned).astype(bf16)


def finish(
    dwindow, got, tokens, normed, dnormed, grad_hidden, gain, w_latent, w_key_rope, cos, sin, block, own, halo
):
    rows = tokens.shape[0]
    return pl.pallas_call(
        functools.partial(finish_kernel, block, own, halo),
        out_shape=[
            jax.ShapeDtypeStruct((rows, D), f32),
            jax.ShapeDtypeStruct((D, LGROUPS * LAT + LANES), bf16),
            jax.ShapeDtypeStruct((1, D), f32),
        ],
        compiler_params=pltpu.CompilerParams(vmem_limit_bytes=60 << 20),
        name="finish",
    )(dwindow, tokens, normed, dnormed, grad_hidden, gain, w_latent, w_key_rope, cos, sin, *got)


def bits_of(size):
    return size.bit_length() - 1


def bit_pairs(size, bit):
    return [(i, i ^ (1 << bit)) for i in range(size)]


def upper_bit(axis, bit):
    return (lax.axis_index(axis) >> bit) & 1


def leading(shape):
    lead = [("rows", b) for b in reversed(range(bits_of(shape["rows"])))]
    return lead + [("heads", b) for b in reversed(range(bits_of(shape["heads"])))]


def gather_orders(shape):
    rows = [("rows", b) for b in reversed(range(1, bits_of(shape["rows"])))]
    heads = [("heads", b) for b in reversed(range(bits_of(shape["heads"])))]
    last = [("rows", 0)]
    return [
        heads + rows + last,
        heads[:1] + rows + heads[1:] + last,
        heads[-1:] + rows + heads[:-1] + last,
    ]


def flip(index, bit):
    size = 1 << bit
    return index + size * (1 - 2 * (index // size % 2))


def start_barrier(shape):
    barrier = pltpu.get_barrier_semaphore()
    for axis in ("rows", "heads"):
        for away in range(1, shape[axis]):
            pl.semaphore_signal(
                barrier,
                inc=1,
                device_id={axis: lax.rem(lax.axis_index(axis) + away, shape[axis])},
                device_id_type=pl.DeviceIdType.MESH,
            )
    pl.semaphore_wait(barrier, shape["rows"] + shape["heads"] - 2)


def exchange_index(lead, done, bits):
    return tuple(pl.ds(0, 2) if item in done else bits[item] for item in lead)


class Exchanges:

    def __init__(self, shape, plan, targets, send_sem, recv_sem):
        self.orders, self.plan, self.targets = gather_orders(shape), plan, targets
        self.lead, self.stages = leading(shape), len(leading(shape))
        self.index = {axis: lax.axis_index(axis) for axis in ("rows", "heads")}
        self.bits = {
            (axis, bit): lax.rem(self.index[axis] // (1 << bit), 2) for axis, bit in self.lead
        }
        self.send_sem, self.recv_sem = send_sem, recv_sem
        self.times = max(item[0] for item in plan) + self.stages

    def mine(self, which):
        return self.targets[which].at[exchange_index(self.lead, (), self.bits)]

    def copy(self, chunk, stage):
        _, which, order, begin, count = self.plan[chunk]
        axis, bit = self.orders[order][stage]
        held = exchange_index(self.lead, self.orders[order][:stage], self.bits)
        piece = self.targets[which].at[held + (pl.ds(begin, count), slice(None))]
        return pltpu.make_async_remote_copy(
            src_ref=piece,
            dst_ref=piece,
            send_sem=self.send_sem.at[chunk * self.stages + stage],
            recv_sem=self.recv_sem.at[chunk * self.stages + stage],
            device_id={axis: flip(self.index[axis], bit)},
            device_id_type=pl.DeviceIdType.MESH,
        )

    def run(self, time):
        for chunk, item in enumerate(self.plan):
            stage = time - item[0]
            if 0 < stage <= self.stages:
                self.copy(chunk, stage - 1).wait()
            if 0 <= stage < self.stages:
                self.copy(chunk, stage).start()


def exchange_plan(delay, which, first, rows, cuts):
    units, total, passed, plan = rows // 16, cuts * sum(SHARES), 0, []
    for i in range(cuts):
        for order, share in enumerate(SHARES):
            begin = 16 * (units * passed // total)
            passed += share
            count = 16 * (units * passed // total) - begin
            plan.append((delay + i, which, order, first + begin, count))
    return plan


def attend_gather_kernel(
    shape, plan, ready, groups, block, own, halo, normed_ref, cos_ref, sin_ref, latent_ref, near_ref, large_ref,
    mixed_ref, log_ref, q_ref, near_all, large_all, window_ref, query_s, top_s, sum_s, window_s, weight_s, up_s,
    local_sem, halo_send, halo_recv, send_sem, recv_sem,
):
    part, parts = pl.program_id(0), HEADS // GROUP
    head = lax.axis_index("heads")
    exchanges = Exchanges(shape, plan, (near_all, large_all), send_sem, recv_sem)
    ahead = lax.rem(head * own, halo + 1)

    def latent_copies():
        for k in range(1, halo + 1):
            back = -(-k // own)
            at = halo + own - 1 - (k - 1) % own
            copy = pltpu.make_async_remote_copy(
                src_ref=window_s.at[pl.ds(at * block, block), :],
                dst_ref=window_s.at[pl.ds((halo - k) * block, block), :],
                send_sem=halo_send.at[k - 1],
                recv_sem=halo_recv.at[k - 1],
                device_id={"heads": lax.rem(head + back, shape["heads"])},
                device_id_type=pl.DeviceIdType.MESH,
            )
            there = lax.rem((head + back) * own, halo + 1)
            yield k, copy, (head + back < shape["heads"]) & (there >= k)

    keep_window = pltpu.make_async_copy(window_s, window_ref, local_sem.at[2])

    @pl.when(part == 0)
    def _():
        local = [
            pltpu.make_async_copy(near_ref, exchanges.mine(0), local_sem.at[0]),
            pltpu.make_async_copy(large_ref, exchanges.mine(1), local_sem.at[1]),
        ]
        for copy in local:
            copy.start()
        window_s[halo * block :, :] = latent_ref[...]
        for k in range(1, halo + 1):

            @pl.when(ahead < k)
            def _():
                blank = jnp.zeros((block, window_s.shape[1]), bf16)
                window_s[(halo - k) * block : (halo - k + 1) * block, :] = blank

        start_barrier(shape)
        for copy in local:
            copy.wait()
        for time in range(ready + 1):
            exchanges.run(time)
            if time == 0:
                for _, copy, goes in latent_copies():

                    @pl.when(goes)
                    def _():
                        copy.start()

        for k, copy, goes in latent_copies():

            @pl.when(goes)
            def _():
                copy.wait_send()

            @pl.when(ahead >= k)
            def _():
                copy.wait_recv()

        keep_window.start()

    lead = exchanges.lead
    everything = exchange_index(lead, lead, exchanges.bits)
    cut = weight_s.shape[-2]
    lanes = pl.ds(pl.multiple_of(part * LANES, LANES), LANES)
    loads = [
        pltpu.make_async_copy(
            near_all.at[everything + (pl.ds(0, cut), lanes)], weight_s, local_sem.at[3]
        ),
        pltpu.make_async_copy(
            near_all.at[everything + (pl.ds(cut, up_s.shape[-2]), lanes)], up_s, local_sem.at[4]
        ),
    ]
    for copy in loads:
        copy.start()
    for copy in loads:
        copy.wait()

    def of_shard(ref, rows):
        count = bits_of(shape["rows"])

        def get(e):
            bits = [(e >> bit) & 1 for axis, bit in lead if axis == "heads"]
            return ref[(slice(None),) * count + tuple(bits)].reshape(rows, LANES)

        return get

    def meanwhile(at):
        for p in range(parts):
            time = ready + 1 + 2 * p + at

            @pl.when(part == p)
            def _():
                exchanges.run(time)

    forward_body(
        groups, block, own, halo, ahead, meanwhile, of_shard(weight_s, D), of_shard(up_s, LAT),
        normed_ref, cos_ref, sin_ref, window_s, mixed_ref, log_ref, q_ref, query_s, top_s, sum_s,
    )

    @pl.when(part == parts - 1)
    def _():
        for time in range(ready + 1 + 2 * parts, exchanges.times + 1):
            exchanges.run(time)
        keep_window.wait()


def attend_gather(shape, groups, normed, latent, near, large, cos, sin, block, own, halo):
    rows, wide = own * block, (halo + own) * block
    cut, small = D // shape["rows"], LAT // shape["rows"]
    once = pl.Buffered(1)
    first = cut + small
    plan = exchange_plan(0, 0, 0, first, 2)
    ready = max(item[0] for item in plan) + len(leading(shape))
    plan = plan + exchange_plan(2, 1, 0, large.shape[0], CHUNKS)
    plan = plan + exchange_plan(1 + CHUNKS, 0, first, near.shape[0] - first, 1)
    count = len(plan) * len(leading(shape))
    twos = (2,) * len(leading(shape))
    anywhere = pl.BlockSpec(memory_space=pl.ANY)
    outside = pl.BlockSpec(memory_space=pltpu.HBM)

    def whole(shape):
        return pl.BlockSpec(shape, lambda g: (0,) * len(shape), pipeline_mode=once)

    mixed, logs, queries, near_all, large_all, window = pl.pallas_call(
        functools.partial(attend_gather_kernel, shape, plan, ready, groups, block, own, halo),
        grid=(HEADS // GROUP,),
        in_specs=[
            whole((rows, D)),
            whole((rows, LANES)),
            whole((rows, LANES)),
            whole(latent.shape),
            anywhere,
            anywhere,
        ],
        out_specs=[
            pl.BlockSpec((None, GROUP * HD, rows), lambda g: (g, 0, 0)),
            pl.BlockSpec((None, GROUP, 1, rows), lambda g: (g, 0, 0, 0)),
            pl.BlockSpec((None, rows, GROUP * LANES), lambda g: (g, 0, 0)),
            outside,
            outside,
            outside,
        ],
        out_shape=[
            jax.ShapeDtypeStruct((HEADS // GROUP, GROUP * HD, rows), bf16),
            jax.ShapeDtypeStruct((HEADS // GROUP, GROUP, 1, rows), f32),
            jax.ShapeDtypeStruct((HEADS // GROUP, rows, GROUP * LANES), bf16),
            jax.ShapeDtypeStruct(twos + near.shape, bf16),
            jax.ShapeDtypeStruct(twos + large.shape, bf16),
            jax.ShapeDtypeStruct((wide, latent.shape[1]), bf16),
        ],
        scratch_shapes=[
            pltpu.VMEM((GROUP, LANES, rows), bf16),
            pltpu.VMEM((GROUP, 1, rows), f32),
            pltpu.VMEM((GROUP, TALL, rows), f32),
            pltpu.VMEM((wide, latent.shape[1]), bf16),
            pltpu.VMEM(twos + (cut, LANES), bf16),
            pltpu.VMEM(twos + (small, LANES), bf16),
            pltpu.SemaphoreType.DMA((5,)),
            pltpu.SemaphoreType.DMA((halo,)),
            pltpu.SemaphoreType.DMA((halo,)),
            pltpu.SemaphoreType.DMA((count,)),
            pltpu.SemaphoreType.DMA((count,)),
        ],
        compiler_params=pltpu.CompilerParams(
            collective_id=0, has_side_effects=True, vmem_limit_bytes=60 << 20
        ),
        name="attend_gather",
    )(normed, cos, sin, latent, near, large)
    full = (shape["rows"], shape["heads"])
    return (mixed, logs, queries), near_all.reshape(full + near.shape), large_all.reshape(full + large.shape), window


def feed_kernel(
    cuts, shards, units, side_ref, normed_ref, cotangent_ref, token_ref, weight_ref, out_ref, dnormed_ref,
    kept_ref, sent_ref,
):
    def whole(which):
        return jnp.concatenate(
            [
                jnp.concatenate(
                    [weight_ref[q, t, which * units : (which + 1) * units, :] for q in range(cuts)],
                    axis=1,
                )
                for t in range(shards)
            ],
            axis=0,
        )

    wide = D // cuts
    side = side_ref[0]

    def put(which, grad):
        at = slice(which * units, (which + 1) * units)
        for t in range(shards):
            rows = slice(t * units, (t + 1) * units)
            for q in range(cuts // 2):
                even = grad[rows, 2 * q * wide : (2 * q + 1) * wide].astype(bf16)
                odd = grad[rows, (2 * q + 1) * wide : (2 * q + 2) * wide].astype(bf16)
                kept_ref[q, t, at, :] = jnp.where(side == 0, even, odd)
                sent_ref[q, t, at, :] = jnp.where(side == 0, odd, even)

    @pl.when(pl.program_id(0) == 0)
    def _():
        out_ref[...] = jnp.zeros_like(out_ref)
        dnormed_ref[...] = jnp.zeros_like(dnormed_ref)

    normed = normed_ref[...]
    grad = (cotangent_ref[...].astype(f32) * token_ref[...]).astype(bf16)
    w_gate, w_up, w_down = whole(0), whole(1), whole(2)
    gate = dot_nt(w_gate, normed)
    upper = dot_nt(w_up, normed)
    grad_inner = dot_nt(w_down, grad)
    sig = jax.nn.sigmoid(gate)
    silu = gate * sig
    inner = (silu * upper).astype(bf16)
    grad_gate = (grad_inner * upper * sig * (1.0 + gate * (1.0 - sig))).astype(bf16)
    grad_upper = (grad_inner * silu).astype(bf16)
    out_ref[...] += dot_tn(inner, w_down)
    dnormed_ref[...] += dot_tn(grad_gate, w_gate)
    dnormed_ref[...] += dot_tn(grad_upper, w_up)
    put(0, dot_nn(grad_gate, normed))
    put(1, dot_nn(grad_upper, normed))
    put(2, dot_nn(inner, grad))


def feed_forward_both(side, normed, cotangent, token_weight, weights, units):
    rows = normed.shape[0]
    cuts, pieces, _, wide = weights.shape
    shards = max(1, min(pieces, 704 // units))
    once = pl.Buffered(1)
    half = (cuts // 2, shards, 3 * units, wide)
    whole = pl.BlockSpec((rows, D), lambda f, s: (0, 0), pipeline_mode=once)
    return pl.pallas_call(
        functools.partial(feed_kernel, cuts, shards, units),
        grid_spec=pltpu.PrefetchScalarGridSpec(
            num_scalar_prefetch=1,
            grid=(pieces // shards,),
            in_specs=[
                whole,
                whole,
                pl.BlockSpec((rows, 1), lambda f, s: (0, 0), pipeline_mode=once),
                pl.BlockSpec((cuts, shards, 3 * units, wide), lambda f, s: (0, f, 0, 0)),
            ],
            out_specs=[
                whole,
                whole,
                pl.BlockSpec(half, lambda f, s: (0, f, 0, 0)),
                pl.BlockSpec(half, lambda f, s: (0, f, 0, 0)),
            ],
        ),
        out_shape=[
            jax.ShapeDtypeStruct((rows, D), f32),
            jax.ShapeDtypeStruct((rows, D), f32),
            jax.ShapeDtypeStruct((cuts // 2, pieces, 3 * units, wide), bf16),
            jax.ShapeDtypeStruct((cuts // 2, pieces, 3 * units, wide), bf16),
        ],
        compiler_params=pltpu.CompilerParams(vmem_limit_bytes=60 << 20),
        cost_estimate=pl.CostEstimate(
            flops=40 * 10**9, bytes_accessed=50 * 10**6, transcendentals=0
        ),
        name="feed_forward_both",
    )(side, normed, cotangent, token_weight, weights)


def scatter_orders(shape):
    return [order[::-1] for order in gather_orders(shape)]


class Scatter:

    def __init__(self, shape, order, array, started=None):
        self.shape = shape
        self.order = list(scatter_orders(shape)[order])
        self.lead = leading(shape)
        self.terms = [array]
        if started is not None:
            self.order.pop(0)
            self.lead.remove(("rows", 0))
            self.terms = [array, started]
        self.terms = [t.reshape((2,) * len(self.lead) + t.shape[2:]) for t in self.terms]

    def total(self, terms):
        if len(terms) == 1:
            return terms[0]
        return sum(t.astype(f32) for t in terms).astype(bf16)

    def view(self):
        at = self.lead.index(self.order[0])
        before, after = 2**at, 2 ** (len(self.lead) - 1 - at)
        return before, after, [
            t.reshape((before, 2, after) + t.shape[len(self.lead) :]) for t in self.terms
        ]

    def halves(self):
        axis, bit = self.order[0]
        at = self.lead.index((axis, bit))
        upper = upper_bit(axis, bit)

        def half(which):
            return self.total(
                [lax.dynamic_index_in_dim(t, which, at, keepdims=False) for t in self.terms]
            )

        return half(upper), half(1 - upper)

    def send(self, kept, sent):
        axis, bit = self.order.pop(0)
        self.lead.remove((axis, bit))
        self.terms = [kept, lax.ppermute(sent, axis, bit_pairs(self.shape[axis], bit))]

    def left(self):
        perm = [self.lead.index(item) for item in self.order]
        array = self.total(self.terms)
        array = array.transpose(perm + list(range(len(perm), array.ndim)))
        return array.reshape((2 ** len(perm),) + array.shape[len(perm) :])


def fold_kernel(counts, side_ref, *refs):
    refs = list(refs)
    ins = [[refs.pop(0) for _ in range(2 * count)] for count in counts]
    for terms in ins:
        half = len(terms) // 2
        for part in (terms[:half], terms[half:]):
            total = part[0][...].astype(f32)
            for term in part[1:]:
                total = total + term[...].astype(f32)
            refs.pop(0)[...] = total.astype(bf16)


def fold(scatters, blocks):
    sides = jnp.stack([upper_bit(*scatter.order[0]) for scatter in scatters]).astype(jnp.int32)
    ins, in_specs, out_specs, out_shape, steps = [], [], [], [], None
    for i, (scatter, (row_block, rows)) in enumerate(zip(scatters, blocks)):
        before, after, terms = scatter.view()
        steps = before * after
        columns = terms[0].shape[4]
        for other in (0, 1):
            spec = pl.BlockSpec(
                (None, None, None, rows, columns),
                lambda g, s, i=i, after=after, other=other, row_block=row_block: (
                    g // after, s[i] * (1 - 2 * other) + other, g % after, row_block, 0
                ),
            )
            in_specs += [spec] * len(terms)
            ins += terms
            out_specs.append(pl.BlockSpec((None, rows, columns), lambda g, s: (g, 0, 0)))
            out_shape.append(jax.ShapeDtypeStruct((steps, rows, columns), bf16))
    outs = pl.pallas_call(
        functools.partial(fold_kernel, [len(scatter.terms) for scatter in scatters]),
        grid_spec=pltpu.PrefetchScalarGridSpec(
            num_scalar_prefetch=1, grid=(steps,), in_specs=in_specs, out_specs=out_specs
        ),
        out_shape=out_shape,
        name="fold",
    )(sides, *ins)
    twos = [(2,) * (len(scatter.lead) - 1) for scatter in scatters for _ in (0, 1)]
    outs = [out.reshape(two + out.shape[1:]) for two, out in zip(twos, outs)]
    return list(zip(outs[::2], outs[1::2]))


def step_all(scatters, tied, folded=0, blocks=()):
    halves = fold(scatters[:folded], blocks) if folded else []
    halves = halves + [scatter.halves() for scatter in scatters[folded:]]
    sent, tied = lax.optimization_barrier(([half[1] for half in halves], tied))
    for scatter, half, out in zip(scatters, halves, sent):
        scatter.send(half[0], out)
    return tied


def scatter_kernel(shape, orders, *refs):
    count = len(orders)
    arrays, outs = refs[:count], refs[count : 2 * count]
    scratch, (send_sem, recv_sem) = list(refs[2 * count : -2]), refs[-2:]
    index = {"rows": lax.axis_index("rows"), "heads": lax.axis_index("heads")}
    start_barrier(shape)
    held, flying = list(arrays), [None] * count
    semaphore = 0
    for stage in range(max(len(order) for order in orders) + 1):
        for i, order in enumerate(orders):
            if flying[i] is not None:
                copy, kept, landed, begin, half = flying[i]
                copy.wait()
                flying[i] = None
                if stage < len(order):
                    summed = scratch.pop(0)

                    def add(at, _):
                        both = kept[begin + at].astype(f32) + landed[at].astype(f32)
                        summed[at] = both.astype(bf16)
                        return 0

                    lax.fori_loop(0, half, add, 0)
                    held[i] = summed
                else:
                    outs[i][...] = kept[begin].astype(f32) + landed[0].astype(f32)
            if stage < len(order):
                axis, bit = order[stage]
                upper = lax.rem(index[axis] // (1 << bit), 2)
                half = held[i].shape[0] // 2
                landed = scratch.pop(0)
                copy = pltpu.make_async_remote_copy(
                    src_ref=held[i].at[pl.ds((1 - upper) * half, half)],
                    dst_ref=landed,
                    send_sem=send_sem.at[semaphore],
                    recv_sem=recv_sem.at[semaphore],
                    device_id={axis: flip(index[axis], bit)},
                    device_id_type=pl.DeviceIdType.MESH,
                )
                copy.start()
                flying[i] = (copy, held[i], landed, upper * half, half)
                semaphore += 1


def scatter_rest(shape, scatters):
    orders = [tuple(scatter.order) for scatter in scatters]
    arrays = [scatter.left() for scatter in scatters]
    scratch = []
    for stage in range(max(len(order) for order in orders) + 1):
        for order, array in zip(orders, arrays):
            tail = array.shape[1:]
            if 0 < stage < len(order):
                scratch.append(pltpu.VMEM((array.shape[0] >> stage,) + tail, bf16))
            if stage < len(order):
                scratch.append(pltpu.VMEM((array.shape[0] >> (stage + 1),) + tail, bf16))
    total = sum(len(order) for order in orders)
    inside = pl.BlockSpec(memory_space=pltpu.VMEM)
    return pl.pallas_call(
        functools.partial(scatter_kernel, shape, orders),
        in_specs=[inside] * len(arrays),
        out_specs=[inside] * len(arrays),
        out_shape=[jax.ShapeDtypeStruct(array.shape[1:], f32) for array in arrays],
        scratch_shapes=scratch
        + [pltpu.SemaphoreType.DMA((total,)), pltpu.SemaphoreType.DMA((total,))],
        compiler_params=pltpu.CompilerParams(
            collective_id=1, has_side_effects=True, vmem_limit_bytes=48 << 20
        ),
        name="scatter_rest",
    )(*arrays)


def on_device(
    shape,
    tokens,
    cotangent,
    domain,
    group_weight,
    gain_attn,
    w_query,
    w_query_rope,
    w_latent,
    w_key_rope,
    w_key_up,
    w_value_up,
    w_out,
    gain_mlp,
    w_gate,
    w_up,
    w_down,
):
    n_rows, n_heads = shape["rows"], shape["heads"]
    row_at, head_at = lax.axis_index("rows"), lax.axis_index("heads")
    local = tokens.shape[0]
    block = math.gcd(local, LEN)
    own, halo = local // block, LEN // block - 1
    here = w_query.shape[1] // HD
    units = w_gate.shape[1]
    cut = D // n_rows
    half = RD // 2

    head_of = [(i % n_heads) * here + i // n_heads for i in range(HEADS)]
    group_of = [head // GROUP for head in head_of]
    parts = [tuple(group_of[p * GROUP : (p + 1) * GROUP]) for p in range(HEADS // GROUP)]

    start = head_at * local
    positions = ((start + jnp.arange(local)) % LEN).astype(f32)
    frequency = THETA ** (-(jnp.arange(LANES) % half).astype(f32) / half)
    angles = positions[:, None] * frequency[None, :]
    cos, sin = jnp.cos(angles), jnp.sin(angles)
    ahead = start // block % (LEN // block)
    places = jnp.stack([ahead, jnp.minimum(LEN // block - ahead, own)]).astype(jnp.int32)

    gain_one, gain_two = gain_attn.reshape(1, D), gain_mlp.reshape(1, D)
    normed, latent = prepare(tokens, gain_one, w_latent, w_key_rope.T, cos, sin)

    def halo_pairs(k):
        back = -(-k // own)
        needs = [i for i in range(n_heads) if (i * local % LEN) // block >= k]
        return [(i - back, i) for i in needs]

    direct = cut % LANES == 0 and GROUP % n_heads == 0
    if direct:
        near, large = pack(
            row_at.astype(jnp.int32).reshape(1),
            n_rows, w_query, w_query_rope.T, w_key_up, w_value_up, w_out, w_gate.T, w_up.T, w_down,
        )
        forward, near, large, window = attend_gather(
            shape, parts[0], normed, latent, near, large, cos, sin, block, own, halo
        )
        out, base = near, (D + LAT) // n_rows
    else:
        pieces = []
        for k in range(halo, 0, -1):
            at = own - 1 - (k - 1) % own
            pieces.append(
                lax.ppermute(latent[at * block : (at + 1) * block], "heads", halo_pairs(k))
            )
        window = jnp.concatenate(pieces + [latent], axis=0)
        queries = jnp.concatenate(
            [
                w_query.reshape(D, here, HD),
                w_query_rope.reshape(D, here, RD),
                jnp.zeros((D, here, LANES - HD - RD), bf16),
            ],
            axis=2,
        ).reshape(n_rows, cut, here * LANES)
        ups = jnp.concatenate(
            [w_key_up.reshape(LAT, here, HD), w_value_up.reshape(LAT, here, HD)], axis=2
        ).reshape(n_rows, LAT // n_rows, here * LANES)
        near = jnp.concatenate([queries, ups], axis=1)
        near = lax.all_gather(near, "heads", axis=1)
        out, base = lax.all_gather(w_out, "heads", axis=0)[None], 0
        large = jnp.concatenate([w_gate.T, w_up.T, w_down], axis=0)
        large = lax.all_gather(large, "heads", axis=0).reshape(n_heads, 3 * units, 2, D // 2)
        large = large.transpose(2, 0, 1, 3)
        forward = [
            attend_forward(p, groups, places, normed, near, cos, sin, window, block, own, halo)
            for p, groups in enumerate(parts)
        ]
        forward = [jnp.stack(arrays) for arrays in zip(*forward)]
    mixed = forward[0]
    hidden, normed_mlp = join(tokens, gain_two, mixed, out, base)

    seq_weights = jnp.sum(
        (domain[:, None] == jnp.arange(group_weight.shape[0])[None, :]).astype(f32)
        * group_weight[None, :],
        axis=1,
    )
    token_seq = (start + jnp.arange(local)) // LEN
    token_weight = jnp.sum(
        (token_seq[:, None] == jnp.arange(domain.shape[0])[None, :]).astype(f32)
        * seq_weights[None, :],
        axis=1,
    )[:, None]
    core = upper_bit("rows", 0)
    side = core if direct else jnp.zeros_like(core)
    feed_out, grad_normed_mlp, feed_kept, feed_sent = feed_forward_both(
        side.astype(jnp.int32).reshape(1), normed_mlp, cotangent, token_weight, large, units
    )
    if not direct:
        grad_feed = jnp.concatenate([feed_kept[0], feed_sent[0]], axis=2)
        grad_feed = grad_feed.reshape(n_heads, 3 * units, n_rows // 2, 2, cut)
        grad_feed = grad_feed.transpose(3, 2, 0, 1, 4)
        feed_kept = lax.dynamic_index_in_dim(grad_feed, core, 0, keepdims=False)
        feed_sent = lax.dynamic_index_in_dim(grad_feed, 1 - core, 0, keepdims=False)
    feed_got = lax.ppermute(feed_sent, "rows", bit_pairs(n_rows, 0))
    half_way = 3 * units // 2
    scatter_feed = [
        Scatter(shape, 0, feed_kept, feed_got),
        Scatter(shape, 1, feed_kept, feed_got),
    ]
    block_output, grad_hidden, grad_out, grad_gain_two, *grad_mixed = middle(
        hidden, feed_out, grad_normed_mlp, cotangent, token_weight, gain_two, mixed, out, base
    )
    if not direct:
        grad_out = grad_out.reshape(n_heads, here * HD, n_rows, cut).transpose(2, 0, 1, 3)

    by_part = GROUP % n_heads == 0
    scatter_near, pieces, before = [], [], None
    scatter_out = Scatter(shape, 0, grad_out)
    for p, groups in enumerate(parts):
        under_way = scatter_feed + ([scatter_out] + scatter_near if p else [])
        blocks = [(0, half_way), (0 if p else 1, half_way)]
        grad_mixed[p] = step_all(under_way, grad_mixed[p], 2, blocks)
        *before, grad_near = attend_backward(
            p, groups, places, forward, normed, near, cos, sin, window, grad_mixed[p], before,
            block, own, halo,
        )
        if by_part:
            scatter_near.append(Scatter(shape, 1, grad_near))
        else:
            pieces.append(grad_near)
    if not by_part:
        scatter_near.append(Scatter(shape, 1, jnp.concatenate(pieces, axis=1)))
    grad_window, grad_normed = before
    got = [
        lax.ppermute(
            grad_window[(halo - k) * block : (halo - k + 1) * block],
            "heads",
            [(b, a) for a, b in halo_pairs(k)],
        )
        for k in range(1, halo + 1)
    ]
    grad_normed = step_all(scatter_feed + [scatter_out] + scatter_near, grad_normed)
    grad_tokens, grad_latent, grad_gain_one = finish(
        grad_window, got, tokens, normed, grad_normed, grad_hidden, gain_one, w_latent, w_key_rope.T, cos, sin,
        block, own, halo,
    )
    gains = jnp.concatenate([grad_gain_one, grad_gain_two], axis=0).astype(bf16)
    gains = gains.reshape(2, n_rows, n_heads, -1).transpose(1, 2, 0, 3)
    gains = jnp.pad(gains, ((0, 0), (0, 0), (0, 14), (0, LANES - gains.shape[3])))
    grad_latent = grad_latent.reshape(n_rows, n_heads, D // (n_rows * n_heads), -1)
    own_first, own_second, own_out, own_latent, own_gain, *own_near = scatter_rest(
        shape,
        scatter_feed
        + [scatter_out, Scatter(shape, 0, grad_latent), Scatter(shape, 1, gains)]
        + scatter_near,
    )
    own_feed = jnp.concatenate([own_first, own_second], axis=0)
    own_near = jnp.concatenate(own_near, axis=1)
    own_query = own_near[:cut].reshape(cut, here, LANES)
    own_up = own_near[cut:].reshape(LAT // n_rows, here, LANES)
    at, gain_cut = LGROUPS * LAT, D // (n_rows * n_heads)
    return (
        block_output,
        grad_tokens,
        own_gain[0, :gain_cut],
        own_query[:, :, :HD].reshape(cut, here * HD),
        own_query[:, :, HD : HD + RD].reshape(cut, here * RD),
        own_latent[:, :at],
        own_latent[:, at + HD : at + HD + RD],
        own_up[:, :, :HD].reshape(LAT // n_rows, here * HD),
        own_up[:, :, HD:].reshape(LAT // n_rows, here * HD),
        own_out,
        own_gain[1, :gain_cut],
        own_feed[:units].T,
        own_feed[units : 2 * units].T,
        own_feed[2 * units :],
    )


def solution(mesh):
    in_specs = (
        P(("rows", "heads"), None),
        P(("rows", "heads"), None),
        P("rows"),
        P(),
        P(),
        P(None, "heads"),
        P(None, "heads"),
        P(),
        P(),
        P(None, "heads"),
        P(None, "heads"),
        P("heads", None),
        P(),
        P(None, "heads"),
        P(None, "heads"),
        P("heads", None),
    )
    out_specs = (
        P(("rows", "heads"), None),
        P(("rows", "heads"), None),
        P(("rows", "heads")),
        P("rows", "heads"),
        P("rows", "heads"),
        P(("rows", "heads"), None),
        P(("rows", "heads"), None),
        P("rows", "heads"),
        P("rows", "heads"),
        P("heads", "rows"),
        P(("rows", "heads")),
        P("rows", "heads"),
        P("rows", "heads"),
        P("heads", "rows"),
    )
    return jax.shard_map(
        functools.partial(on_device, dict(mesh.shape)),
        mesh=mesh,
        in_specs=in_specs,
        out_specs=out_specs,
        check_vma=False,
    )
```

```python
import functools
import math

import jax
import jax.numpy as jnp
from jax import lax
from jax.experimental import pallas as pl
from jax.experimental.pallas import tpu as pltpu
from jax.sharding import PartitionSpec as P

D = 1024
HEADS = 16
HD = 64
LGROUPS = 2
LAT = 256
RD = 32
LEN = 2048
EPS = 1e-05
THETA = 10000.0
NEG_LARGE = -1e30
LANES = 128
PAIR = 2
GROUP = HEADS // LGROUPS
TALL = 80
CHUNKS = 4
SHARES = (2, 2, 1)
LOG2E = math.log2(math.e)
LN2 = math.log(2.0)
SCALE = (HD + RD) ** (-0.5)

bf16 = jnp.bfloat16
f32 = jnp.float32


def dot_nn(a, b):
    return jnp.dot(a, b, preferred_element_type=f32)


def dot_nt(a, b):
    return lax.dot_general(a, b, (((1,), (1,)), ((), ())), preferred_element_type=f32)


def dot_tn(a, b):
    return lax.dot_general(a, b, (((0,), (0,)), ((), ())), preferred_element_type=f32)


def rms_scale(values):
    return lax.rsqrt(jnp.mean(values * values, axis=-1, keepdims=True) + EPS)


def rotate_lanes(values, cos, sin):
    lane = lax.broadcasted_iota(jnp.int32, values.shape, 1)
    turned = (lane >= HD) & (lane < HD + RD)
    cos = jnp.where(lane < HD, 1.0, jnp.where(turned, cos, 0.0))
    sin = jnp.where(turned, sin, 0.0)
    half = RD // 2
    swapped = jnp.where(
        lane < HD + half, -pltpu.roll(values, LANES - half, 1), pltpu.roll(values, half, 1)
    )
    return values * cos + swapped * sin


def rope_weight(w_key_rope):
    blank = jnp.zeros((HD, w_key_rope.shape[1]), bf16)
    return jnp.concatenate([blank, w_key_rope, blank[: LANES - HD - RD]], axis=0)


def prepare_kernel(tokens_ref, gain_ref, latent_ref, rope_ref, cos_ref, sin_ref, normed_ref, out_ref):
    source = tokens_ref[...].astype(f32)
    normed = (source * rms_scale(source) * gain_ref[...].astype(f32)).astype(bf16)
    normed_ref[...] = normed
    out_ref[:, : LGROUPS * LAT] = dot_nn(normed, latent_ref[...]).astype(bf16)
    turned = rotate_lanes(dot_nt(normed, rope_weight(rope_ref[...])), cos_ref[...], sin_ref[...])
    out_ref[:, LGROUPS * LAT :] = turned.astype(bf16)


def prepare(tokens, gain, w_latent, w_key_rope, cos, sin):
    rows = tokens.shape[0]
    return pl.pallas_call(
        prepare_kernel,
        out_shape=[
            jax.ShapeDtypeStruct((rows, D), bf16),
            jax.ShapeDtypeStruct((rows, LGROUPS * LAT + LANES), bf16),
        ],
        compiler_params=pltpu.CompilerParams(vmem_limit_bytes=40 << 20),
        name="prepare",
    )(tokens, gain, w_latent, w_key_rope, cos, sin)


def pack_kernel(
    here, side_ref, query_ref, rope_ref, key_ref, value_ref, out_ref, gate_ref, up_ref, down_ref,
    near_ref, large_ref,
):
    units, cut = gate_ref.shape
    blank = jnp.zeros((cut, LANES - HD - RD), bf16)
    small = key_ref.shape[0]
    turned = rope_ref[...].T
    for e in range(here):
        lanes = slice(e * LANES, (e + 1) * LANES)
        heads, turns = slice(e * HD, (e + 1) * HD), slice(e * RD, (e + 1) * RD)
        near_ref[:cut, lanes] = jnp.concatenate(
            [query_ref[:, heads], turned[:, turns], blank], axis=1
        )
        near_ref[cut : cut + small, lanes] = jnp.concatenate(
            [key_ref[:, heads], value_ref[:, heads]], axis=1
        )
    near_ref[cut + small :, :] = out_ref[...]
    large_ref[:units, :] = gate_ref[...]
    large_ref[units : 2 * units, :] = up_ref[...]
    large_ref[2 * units :, :] = down_ref[...]


def pack(side, n_rows, w_query, w_query_rope, w_key_up, w_value_up, w_out, w_gate, w_up, w_down):
    here, units = w_query.shape[1] // HD, w_gate.shape[0]
    cut, small = D // n_rows, LAT // n_rows

    def by_rows(weight):
        tall = weight.shape[0] // n_rows
        return pl.BlockSpec((tall, weight.shape[1]), lambda g, s: (s[0], 0))

    def by_columns(weight):
        return pl.BlockSpec((weight.shape[0], cut), lambda g, s: (0, s[0]))

    near = (cut + small + here * HD, here * LANES)
    large = (3 * units, cut)
    return pl.pallas_call(
        functools.partial(pack_kernel, here),
        grid_spec=pltpu.PrefetchScalarGridSpec(
            num_scalar_prefetch=1,
            grid=(1,),
            in_specs=[
                by_rows(w_query),
                by_columns(w_query_rope),
                by_rows(w_key_up),
                by_rows(w_value_up),
                by_columns(w_out),
                by_columns(w_gate),
                by_columns(w_up),
                by_columns(w_down),
            ],
            out_specs=[
                pl.BlockSpec(near, lambda g, s: (0, 0)),
                pl.BlockSpec(large, lambda g, s: (0, 0)),
            ],
        ),
        out_shape=[jax.ShapeDtypeStruct(near, bf16), jax.ShapeDtypeStruct(large, bf16)],
        name="pack",
    )(side, w_query, w_query_rope, w_key_up, w_value_up, w_out, w_gate, w_up, w_down)


def keys_values(groups, window_ref, up_of, rows, count):
    rope = window_ref[rows, LGROUPS * LAT :]
    lane = lax.broadcasted_iota(jnp.int32, (count, LANES), 1)
    keys, values = [], []
    for e in range(0, GROUP, PAIR):
        latent = window_ref[rows, groups[e] * LAT : (groups[e] + 1) * LAT]
        up = jnp.concatenate([up_of(e + i) for i in range(PAIR)], axis=1)
        wide = dot_nn(latent, up).astype(bf16)
        for i in range(PAIR):
            both = wide[:, i * LANES : (i + 1) * LANES]
            keys.append(jnp.where(lane < HD, both, rope))
            values.append(both)
    return keys, values


def values_ones(value):
    count = value.shape[0]
    return jnp.concatenate([value.T[HD:], jnp.ones((TALL - HD, count), bf16)], axis=0)


def shard_block(part, shards, rows_at):
    return lambda g, p: (0, part * GROUP % shards // GROUP, rows_at, part * GROUP // shards)


def forward_body(
    groups, block, own, halo, ahead, meanwhile, weight_of, up_of, normed_ref, cos_ref, sin_ref, window_ref,
    mixed_ref, log_ref, q_ref, query_s, top_s, sum_s,
):
    rows = own * block
    until = halo + 1 - ahead
    weight = jnp.concatenate([weight_of(e) for e in range(GROUP)], axis=1)
    raw = dot_nn(normed_ref[...], weight)
    for e in range(GROUP):
        lanes = slice(e * LANES, (e + 1) * LANES)
        query = rotate_lanes(raw[:, lanes], cos_ref[...], sin_ref[...])
        query = (query * (SCALE * LOG2E)).astype(bf16)
        q_ref[:, lanes] = query
        query_s[e] = query.T
    keys, values = keys_values(
        groups, window_ref, up_of, slice(halo * block, (halo + own) * block), rows
    )
    values = [values_ones(value) for value in values]
    for j in range(own):
        count = (j + 1) * block
        key_at = lax.broadcasted_iota(jnp.int32, (count, block), 0)
        query_at = lax.broadcasted_iota(jnp.int32, (count, block), 1) + j * block
        keep = (key_at <= query_at) & (key_at >= jnp.where(j >= until, until * block, 0))
        cols = slice(j * block, count)
        scores = [
            jnp.where(keep, dot_nn(keys[e][:count], query_s[e, :, cols]), NEG_LARGE)
            for e in range(GROUP)
        ]
        for e in range(GROUP):
            top = jnp.max(scores[e], axis=0, keepdims=True)
            terms = jnp.exp2(scores[e] - top).astype(bf16)
            top_s[e, :, cols] = top
            sum_s[e, :, cols] = dot_nn(values[e][:, :count], terms)
    meanwhile(0)
    for blocks in range(1, own + 1):
        wide = blocks * block

        def step(index, _):
            at = pl.ds(pl.multiple_of(index * block, block), block)
            keys, values = keys_values(groups, window_ref, up_of, at, block)
            values = [values_ones(value) for value in values]
            scores = [dot_nn(keys[e], query_s[e, :, :wide]) for e in range(GROUP)]
            for e in range(GROUP):
                top = top_s[e, :, :wide]
                higher = jnp.maximum(top, jnp.max(scores[e], axis=0, keepdims=True))
                shrink = jnp.exp2(top - higher)
                terms = jnp.exp2(scores[e] - higher).astype(bf16)
                top_s[e, :, :wide] = higher
                sum_s[e, :, :wide] = sum_s[e, :, :wide] * shrink + dot_nn(values[e], terms)
            return 0

        @pl.when(until == blocks if blocks < own else until >= own)
        def _():
            lax.fori_loop(halo - ahead, halo, step, 0)

    meanwhile(1)
    for e in range(GROUP):
        total = sum_s[e]
        sums = total[HD : HD + 1]
        mixed_ref[e * HD : (e + 1) * HD, :] = (total[:HD] * (1.0 / sums)).astype(bf16)
        log_ref[e] = top_s[e] + jnp.log2(sums)


def attend_forward_kernel(groups, block, own, halo, place_ref, weight_ref, up_ref, *refs):
    forward_body(
        groups, block, own, halo, place_ref[0], lambda at: None,
        lambda e: weight_ref[:, e].reshape(D, LANES),
        lambda e: up_ref[:, e].reshape(LAT, LANES),
        *refs,
    )


def attend_forward(part, groups, places, normed, near, cos, sin, window, block, own, halo):
    rows, wide = own * block, (halo + own) * block
    cuts, shards, once = near.shape[0], near.shape[1], pl.Buffered(1)

    def whole(shape):
        return pl.BlockSpec(shape, lambda g, p: (0,) * len(shape), pipeline_mode=once)

    return pl.pallas_call(
        functools.partial(attend_forward_kernel, groups, block, own, halo),
        grid_spec=pltpu.PrefetchScalarGridSpec(
            num_scalar_prefetch=1,
            grid=(1,),
            in_specs=[
                pl.BlockSpec(
                    (cuts, GROUP, D // cuts, LANES),
                    shard_block(part, shards, 0),
                    pipeline_mode=once,
                ),
                pl.BlockSpec(
                    (cuts, GROUP, LAT // cuts, LANES),
                    shard_block(part, shards, D // LAT),
                    pipeline_mode=once,
                ),
                whole((rows, D)),
                whole((rows, LANES)),
                whole((rows, LANES)),
                whole((wide, LGROUPS * LAT + LANES)),
            ],
            out_specs=[
                whole((GROUP * HD, rows)),
                whole((GROUP, 1, rows)),
                whole((rows, GROUP * LANES)),
            ],
            scratch_shapes=[
                pltpu.VMEM((GROUP, LANES, rows), bf16),
                pltpu.VMEM((GROUP, 1, rows), f32),
                pltpu.VMEM((GROUP, TALL, rows), f32),
            ],
        ),
        out_shape=[
            jax.ShapeDtypeStruct((GROUP * HD, rows), bf16),
            jax.ShapeDtypeStruct((GROUP, 1, rows), f32),
            jax.ShapeDtypeStruct((rows, GROUP * LANES), bf16),
        ],
        compiler_params=pltpu.CompilerParams(vmem_limit_bytes=56 << 20),
        name="attend_forward",
    )(places, near, near, normed, cos, sin, window)


def attend_backward_kernel(
    groups, block, own, halo, carried, place_ref, q_ref, window_ref, up_ref, mixed_ref, log_ref,
    grad_ref, cos_ref, sin_ref, normed_ref, weight_ref, *refs
):
    before = refs[:2] if carried else None
    dwindow_ref, dnormed_ref, dnear_ref, query_s, grad_s, inner_s, dquery_s, both_s, rope_s = refs[-9:]
    rows = own * block
    ahead, until = place_ref[0], place_ref[1]
    first = halo - ahead

    def up_of(e):
        return up_ref[:, e].reshape(LAT, LANES)

    rope_s[...] = jnp.zeros_like(rope_s)

    def clear(index, _):
        at = pl.ds(pl.multiple_of(index * block, block), block)
        both_s[at, :] = jnp.zeros((block, GROUP * LANES), bf16)
        return 0

    lax.fori_loop(0, first, clear, 0)
    for e in range(GROUP):
        query_s[e] = q_ref[:, e * LANES : (e + 1) * LANES].T
        grad = grad_ref[e * HD : (e + 1) * HD, :]
        grad_s[e] = jnp.concatenate([jnp.zeros((rows, HD), bf16), grad.T], axis=1)
        inner_s[e] = jnp.sum(
            grad.astype(f32) * mixed_ref[e * HD : (e + 1) * HD, :].astype(f32),
            axis=0,
            keepdims=True,
        )
        dquery_s[e] = jnp.zeros((LANES, rows), f32)
    lane = lax.broadcasted_iota(jnp.int32, (block, LANES), 1)

    def strip(at, low, high, keep):
        cols = slice(low, high)
        keys, values = keys_values(groups, window_ref, up_of, at, block)
        scores = [dot_nn(keys[e], query_s[e, :, cols]) for e in range(GROUP)]
        grads = [
            dot_nn(values[e][:, HD:], grad_ref[e * HD : (e + 1) * HD, cols]) for e in range(GROUP)
        ]
        grad_rope = None
        for e in range(GROUP):
            score = scores[e] if keep is None else jnp.where(keep, scores[e], NEG_LARGE)
            probs = jnp.exp2(score - log_ref[e, :, cols])
            grad_scores = (probs * (grads[e] - inner_s[e, :, cols])).astype(bf16)
            grad_value = dot_nn(probs.astype(bf16), grad_s[e, cols, :])
            grad_key = dot_nn(grad_scores, q_ref[cols, e * LANES : (e + 1) * LANES]) * LN2
            dquery_s[e, :, cols] += dot_nn(keys[e].T, grad_scores)
            both_s[at, e * LANES : (e + 1) * LANES] = jnp.where(
                lane < HD, grad_key, grad_value
            ).astype(bf16)
            grad_rope = grad_key if grad_rope is None else grad_rope + grad_key
        rope_s[at, :] = grad_rope

    for i in range(own):
        count = rows - i * block
        key_at = lax.broadcasted_iota(jnp.int32, (block, count), 0)
        query_at = lax.broadcasted_iota(jnp.int32, (block, count), 1)
        keep = (key_at <= query_at) & (query_at < jnp.where(i < until, (until - i) * block, rows))
        strip(slice((halo + i) * block, (halo + i + 1) * block), i * block, rows, keep)
    for blocks in range(1, own + 1):

        def step(index, _):
            strip(pl.ds(pl.multiple_of(index * block, block), block), 0, blocks * block, None)
            return 0

        lax.fori_loop(jnp.where(until == blocks, first, halo), halo, step, 0)
    grads = []
    for e in range(GROUP):
        grad = rotate_lanes(dquery_s[e].T * SCALE, cos_ref[...], -sin_ref[...])
        grads.append(grad.astype(bf16))
    dquery = jnp.concatenate(grads, axis=1)
    cuts = weight_ref.shape[0]
    cut, small = D // cuts, LAT // cuts
    for q in range(cuts):
        weight = jnp.concatenate([weight_ref[q, e] for e in range(GROUP)], axis=1)
        part = dot_nt(dquery, weight)
        if carried:
            part = part + before[1][:, q * cut : (q + 1) * cut]
        dnormed_ref[:, q * cut : (q + 1) * cut] = part
    grad = dot_tn(normed_ref[...], dquery).astype(bf16)
    for q in range(cuts):
        for e in range(GROUP):
            dnear_ref[q, e, :cut, :] = grad[q * cut : (q + 1) * cut, e * LANES : (e + 1) * LANES]
    for group in range(LGROUPS):
        at = slice(group * LAT, (group + 1) * LAT)
        heads = [e for e in range(GROUP) if groups[e] == group]
        if heads:
            lanes = slice(heads[0] * LANES, (heads[-1] + 1) * LANES)
            up = jnp.concatenate([up_of(e) for e in heads], axis=1)
            grad = dot_nt(both_s[:, lanes], up)
            dup = dot_nn(window_ref[:, at].T, both_s[:, lanes]).astype(bf16)
            for q in range(cuts):
                for i, e in enumerate(heads):
                    dnear_ref[q, e, cut:, :] = dup[
                        q * small : (q + 1) * small, i * LANES : (i + 1) * LANES
                    ]
        else:
            grad = jnp.zeros((dwindow_ref.shape[0], LAT), f32)
        if carried:
            grad = grad + before[0][:, at].astype(f32)
        dwindow_ref[:, at] = grad.astype(bf16)
    grad = rope_s[...]
    if carried:
        grad = grad + before[0][:, LGROUPS * LAT :].astype(f32)
    dwindow_ref[:, LGROUPS * LAT :] = grad.astype(bf16)


def attend_backward(
    part, groups, places, forward, normed, near, cos, sin, window, grad_mixed, before, block, own, halo
):
    rows, wide = own * block, (halo + own) * block
    cuts, shards, once = near.shape[0], near.shape[1], pl.Buffered(1)
    near_rows = (D + LAT) // cuts
    lanes = LGROUPS * LAT + LANES
    mixed, logs, queries = forward

    def whole(shape):
        return pl.BlockSpec(shape, lambda g, p: (0,) * len(shape), pipeline_mode=once)

    def of_part(shape):
        return pl.BlockSpec(
            (None,) + shape, lambda g, p: (part,) + (0,) * len(shape), pipeline_mode=once
        )

    return pl.pallas_call(
        functools.partial(attend_backward_kernel, groups, block, own, halo, before is not None),
        grid_spec=pltpu.PrefetchScalarGridSpec(
            num_scalar_prefetch=1,
            grid=(1,),
            in_specs=[
                of_part((rows, GROUP * LANES)),
                whole((wide, lanes)),
                pl.BlockSpec(
                    (cuts, GROUP, LAT // cuts, LANES),
                    shard_block(part, shards, D // LAT),
                    pipeline_mode=once,
                ),
                of_part((GROUP * HD, rows)),
                of_part((GROUP, 1, rows)),
                whole((GROUP * HD, rows)),
                whole((rows, LANES)),
                whole((rows, LANES)),
                whole((rows, D)),
                pl.BlockSpec(
                    (cuts, GROUP, D // cuts, LANES),
                    shard_block(part, shards, 0),
                    pipeline_mode=once,
                ),
            ]
            + ([] if before is None else [whole((wide, lanes)), whole((rows, D))]),
            out_specs=[
                whole((wide, lanes)),
                whole((rows, D)),
                whole((cuts, GROUP, near_rows, LANES)),
            ],
            scratch_shapes=[
                pltpu.VMEM((GROUP, LANES, rows), bf16),
                pltpu.VMEM((GROUP, rows, LANES), bf16),
                pltpu.VMEM((GROUP, 1, rows), f32),
                pltpu.VMEM((GROUP, LANES, rows), f32),
                pltpu.VMEM((wide, GROUP * LANES), bf16),
                pltpu.VMEM((wide, LANES), f32),
            ],
        ),
        out_shape=[
            jax.ShapeDtypeStruct((wide, lanes), bf16),
            jax.ShapeDtypeStruct((rows, D), f32),
            jax.ShapeDtypeStruct((cuts, GROUP, near_rows, LANES), bf16),
        ],
        compiler_params=pltpu.CompilerParams(vmem_limit_bytes=60 << 20),
        cost_estimate=pl.CostEstimate(
            flops=40 * 10**9, bytes_accessed=30 * 10**6, transcendentals=0
        ),
        name="attend_backward",
    )(
        places, queries, window, near, mixed, logs, grad_mixed, cos, sin, normed, near,
        *(before or ()),
    )


def join_kernel(parts, tokens_ref, gain_ref, *refs):
    mixed, weights, (hidden_ref, normed_ref) = refs[:parts], refs[parts : 2 * parts], refs[2 * parts :]
    cuts, _, _, cut = weights[0].shape
    squares = 0.0
    for q in range(cuts):
        cols = slice(q * cut, (q + 1) * cut)
        total = tokens_ref[:, cols].astype(f32)
        for m, w in zip(mixed, weights):
            total = total + dot_tn(m[...], w[q].reshape(GROUP * HD, cut))
        hidden_ref[:, cols] = total
        squares = squares + jnp.sum(total * total, axis=1, keepdims=True)
    scale = lax.rsqrt(squares * (1.0 / D) + EPS)
    normed_ref[...] = (hidden_ref[...] * scale * gain_ref[...].astype(f32)).astype(bf16)


def out_specs_of(out, base, parts):
    cuts, shards, _, cut = out.shape
    return [
        pl.BlockSpec(
            (cuts, GROUP, HD, cut),
            lambda g, part=part: (
                0, part * GROUP % shards // GROUP, base // HD + part * GROUP // shards, 0
            ),
            pipeline_mode=pl.Buffered(1),
        )
        for part in range(parts)
    ]


def join(tokens, gain, mixed, out, base):
    rows, parts = tokens.shape[0], mixed.shape[0]

    def whole(shape):
        return pl.BlockSpec(shape, lambda g: (0,) * len(shape), pipeline_mode=pl.Buffered(1))

    return pl.pallas_call(
        functools.partial(join_kernel, parts),
        grid=(1,),
        in_specs=[whole((rows, D)), whole((1, D))]
        + [
            pl.BlockSpec(
                (None, GROUP * HD, rows), lambda g, part=part: (part, 0, 0), pipeline_mode=pl.Buffered(1)
            )
            for part in range(parts)
        ]
        + out_specs_of(out, base, parts),
        out_specs=[whole((rows, D)), whole((rows, D))],
        out_shape=[
            jax.ShapeDtypeStruct((rows, D), f32),
            jax.ShapeDtypeStruct((rows, D), bf16),
        ],
        compiler_params=pltpu.CompilerParams(vmem_limit_bytes=32 << 20),
        name="join",
    )(tokens, gain, *([mixed] * parts), *([out] * parts))


def norm_backward(source, gain, grad_normed):
    scale = rms_scale(source)
    scaled = source * scale
    weighted = grad_normed * gain
    mean = jnp.mean(weighted * scaled, axis=-1, keepdims=True)
    return (
        scale * (weighted - scaled * mean),
        jnp.sum(grad_normed * scaled, axis=0, keepdims=True),
    )


def middle_kernel(parts, here, hidden_ref, feed_ref, dnormed_ref, cotangent_ref, weight_ref, gain_ref, *refs):
    mixed, weights = refs[:parts], refs[parts : 2 * parts]
    block_ref, grad_ref, dout_ref, dgain_ref = refs[2 * parts : 2 * parts + 4]
    dmixed = refs[2 * parts + 4 :]
    hidden = hidden_ref[...]
    block_ref[...] = (hidden + feed_ref[...]).astype(bf16)
    grad, dgain_ref[...] = norm_backward(hidden, gain_ref[...].astype(f32), dnormed_ref[...])
    grad = grad + cotangent_ref[...].astype(f32) * weight_ref[...]
    grad_ref[...] = grad
    low = grad.astype(bf16)
    cuts, _, _, cut = weights[0].shape
    shards = dout_ref.shape[1]
    for p in range(parts):
        e, begin = p * GROUP // shards, p * GROUP % shards
        total = None
        for q in range(cuts):
            cols = slice(q * cut, (q + 1) * cut)
            part = dot_nt(weights[p][q].reshape(GROUP * HD, cut), low[:, cols])
            total = part if total is None else total + part
            grad_out = dot_nn(mixed[p][...], low[:, cols]).astype(bf16)
            dout_ref[q, begin : begin + GROUP, e * HD : (e + 1) * HD, :] = grad_out.reshape(
                GROUP, HD, cut
            )
        dmixed[p][...] = total.astype(bf16)


def middle(hidden, feed, dnormed, cotangent, token_weight, gain, mixed, out, base):
    rows, parts = hidden.shape[0], mixed.shape[0]
    cuts, shards, _, cut = out.shape
    here = HEADS // shards

    def whole(shape):
        return pl.BlockSpec(shape, lambda g: (0,) * len(shape), pipeline_mode=pl.Buffered(1))

    dout = (cuts, shards, here * HD, cut)
    return pl.pallas_call(
        functools.partial(middle_kernel, parts, here),
        grid=(1,),
        in_specs=[whole((rows, D))] * 4
        + [whole((rows, 1)), whole((1, D))]
        + [
            pl.BlockSpec(
                (None, GROUP * HD, rows), lambda g, part=part: (part, 0, 0), pipeline_mode=pl.Buffered(1)
            )
            for part in range(parts)
        ]
        + out_specs_of(out, base, parts),
        out_specs=[whole((rows, D)), whole((rows, D)), whole(dout), whole((1, D))]
        + [whole((GROUP * HD, rows))] * parts,
        out_shape=[
            jax.ShapeDtypeStruct((rows, D), bf16),
            jax.ShapeDtypeStruct((rows, D), f32),
            jax.ShapeDtypeStruct(dout, bf16),
            jax.ShapeDtypeStruct((1, D), f32),
        ]
        + [jax.ShapeDtypeStruct((GROUP * HD, rows), bf16)] * parts,
        compiler_params=pltpu.CompilerParams(vmem_limit_bytes=50 << 20),
        name="middle",
    )(hidden, feed, dnormed, cotangent, token_weight, gain, *([mixed] * parts), *([out] * parts))


def finish_kernel(
    block, own, halo, dwindow_ref, tokens_ref, normed_ref, dnormed_ref, grad_ref, gain_ref, latent_ref,
    rope_ref, cos_ref, sin_ref, *refs
):
    got, (dtokens_ref, dlatent_ref, dgain_ref) = refs[:halo], refs[halo:]
    at = LGROUPS * LAT
    grads = []
    for j in range(own):
        total = dwindow_ref[(halo + j) * block : (halo + j + 1) * block, :].astype(f32)
        for k in range(1, halo + 1):
            if own - 1 - (k - 1) % own == j:
                total = total + got[k - 1][...].astype(f32)
        grads.append(total)
    grad = jnp.concatenate(grads, axis=0)
    turned = rotate_lanes(grad[:, at:], cos_ref[...], -sin_ref[...])
    lane = lax.broadcasted_iota(jnp.int32, turned.shape, 1)
    turned = jnp.where(lane < HD, 0.0, turned).astype(bf16)
    grad = grad[:, :at].astype(bf16)
    dnormed = dnormed_ref[...] + dot_nt(grad, latent_ref[...])
    dnormed = dnormed + dot_nn(turned, rope_weight(rope_ref[...]))
    source = tokens_ref[...].astype(f32)
    dsource, dgain_ref[...] = norm_backward(source, gain_ref[...].astype(f32), dnormed)
    dtokens_ref[...] = grad_ref[...] + dsource
    dlatent_ref[:, :at] = dot_tn(normed_ref[...], grad).astype(bf16)
    dlatent_ref[:, at:] = dot_tn(normed_ref[...], turned).astype(bf16)


def finish(
    dwindow, got, tokens, normed, dnormed, grad_hidden, gain, w_latent, w_key_rope, cos, sin, block, own, halo
):
    rows = tokens.shape[0]
    return pl.pallas_call(
        functools.partial(finish_kernel, block, own, halo),
        out_shape=[
            jax.ShapeDtypeStruct((rows, D), f32),
            jax.ShapeDtypeStruct((D, LGROUPS * LAT + LANES), bf16),
            jax.ShapeDtypeStruct((1, D), f32),
        ],
        compiler_params=pltpu.CompilerParams(vmem_limit_bytes=60 << 20),
        name="finish",
    )(dwindow, tokens, normed, dnormed, grad_hidden, gain, w_latent, w_key_rope, cos, sin, *got)


def bits_of(size):
    return size.bit_length() - 1


def bit_pairs(size, bit):
    return [(i, i ^ (1 << bit)) for i in range(size)]


def upper_bit(axis, bit):
    return (lax.axis_index(axis) >> bit) & 1


def leading(shape):
    lead = [("rows", b) for b in reversed(range(bits_of(shape["rows"])))]
    return lead + [("heads", b) for b in reversed(range(bits_of(shape["heads"])))]


def gather_orders(shape):
    rows = [("rows", b) for b in reversed(range(1, bits_of(shape["rows"])))]
    heads = [("heads", b) for b in reversed(range(bits_of(shape["heads"])))]
    last = [("rows", 0)]
    return [
        heads + rows + last,
        heads[:1] + rows + heads[1:] + last,
        heads[-1:] + rows + heads[:-1] + last,
    ]


def flip(index, bit):
    size = 1 << bit
    return index + size * (1 - 2 * (index // size % 2))


def start_barrier(shape):
    barrier = pltpu.get_barrier_semaphore()
    for axis in ("rows", "heads"):
        for away in range(1, shape[axis]):
            pl.semaphore_signal(
                barrier,
                inc=1,
                device_id={axis: lax.rem(lax.axis_index(axis) + away, shape[axis])},
                device_id_type=pl.DeviceIdType.MESH,
            )
    pl.semaphore_wait(barrier, shape["rows"] + shape["heads"] - 2)


def exchange_index(lead, done, bits):
    return tuple(pl.ds(0, 2) if item in done else bits[item] for item in lead)


class Exchanges:

    def __init__(self, shape, plan, targets, send_sem, recv_sem):
        self.orders, self.plan, self.targets = gather_orders(shape), plan, targets
        self.lead, self.stages = leading(shape), len(leading(shape))
        self.index = {axis: lax.axis_index(axis) for axis in ("rows", "heads")}
        self.bits = {
            (axis, bit): lax.rem(self.index[axis] // (1 << bit), 2) for axis, bit in self.lead
        }
        self.send_sem, self.recv_sem = send_sem, recv_sem
        self.times = max(item[0] for item in plan) + self.stages

    def mine(self, which):
        return self.targets[which].at[exchange_index(self.lead, (), self.bits)]

    def copy(self, chunk, stage):
        _, which, order, begin, count = self.plan[chunk]
        axis, bit = self.orders[order][stage]
        held = exchange_index(self.lead, self.orders[order][:stage], self.bits)
        piece = self.targets[which].at[held + (pl.ds(begin, count), slice(None))]
        return pltpu.make_async_remote_copy(
            src_ref=piece,
            dst_ref=piece,
            send_sem=self.send_sem.at[chunk * self.stages + stage],
            recv_sem=self.recv_sem.at[chunk * self.stages + stage],
            device_id={axis: flip(self.index[axis], bit)},
            device_id_type=pl.DeviceIdType.MESH,
        )

    def run(self, time):
        for chunk, item in enumerate(self.plan):
            stage = time - item[0]
            if 0 < stage <= self.stages:
                self.copy(chunk, stage - 1).wait()
            if 0 <= stage < self.stages:
                self.copy(chunk, stage).start()


def exchange_plan(delay, which, first, rows, cuts):
    units, total, passed, plan = rows // 16, cuts * sum(SHARES), 0, []
    for i in range(cuts):
        for order, share in enumerate(SHARES):
            begin = 16 * (units * passed // total)
            passed += share
            count = 16 * (units * passed // total) - begin
            plan.append((delay + i, which, order, first + begin, count))
    return plan


def attend_gather_kernel(
    shape, plan, ready, groups, block, own, halo, normed_ref, cos_ref, sin_ref, latent_ref, near_ref, large_ref,
    mixed_ref, log_ref, q_ref, near_all, large_all, window_ref, query_s, top_s, sum_s, window_s, weight_s, up_s,
    local_sem, halo_send, halo_recv, send_sem, recv_sem,
):
    part, parts = pl.program_id(0), HEADS // GROUP
    head = lax.axis_index("heads")
    exchanges = Exchanges(shape, plan, (near_all, large_all), send_sem, recv_sem)
    ahead = lax.rem(head * own, halo + 1)

    def latent_copies():
        for k in range(1, halo + 1):
            back = -(-k // own)
            at = halo + own - 1 - (k - 1) % own
            copy = pltpu.make_async_remote_copy(
                src_ref=window_s.at[pl.ds(at * block, block), :],
                dst_ref=window_s.at[pl.ds((halo - k) * block, block), :],
                send_sem=halo_send.at[k - 1],
                recv_sem=halo_recv.at[k - 1],
                device_id={"heads": lax.rem(head + back, shape["heads"])},
                device_id_type=pl.DeviceIdType.MESH,
            )
            there = lax.rem((head + back) * own, halo + 1)
            yield k, copy, (head + back < shape["heads"]) & (there >= k)

    keep_window = pltpu.make_async_copy(window_s, window_ref, local_sem.at[2])

    @pl.when(part == 0)
    def _():
        local = [
            pltpu.make_async_copy(near_ref, exchanges.mine(0), local_sem.at[0]),
            pltpu.make_async_copy(large_ref, exchanges.mine(1), local_sem.at[1]),
        ]
        for copy in local:
            copy.start()
        window_s[halo * block :, :] = latent_ref[...]
        for k in range(1, halo + 1):

            @pl.when(ahead < k)
            def _():
                blank = jnp.zeros((block, window_s.shape[1]), bf16)
                window_s[(halo - k) * block : (halo - k + 1) * block, :] = blank

        start_barrier(shape)
        for copy in local:
            copy.wait()
        for time in range(ready + 1):
            exchanges.run(time)
            if time == 0:
                for _, copy, goes in latent_copies():

                    @pl.when(goes)
                    def _():
                        copy.start()

        for k, copy, goes in latent_copies():

            @pl.when(goes)
            def _():
                copy.wait_send()

            @pl.when(ahead >= k)
            def _():
                copy.wait_recv()

        keep_window.start()

    lead = exchanges.lead
    everything = exchange_index(lead, lead, exchanges.bits)
    cut = weight_s.shape[-2]
    lanes = pl.ds(pl.multiple_of(part * LANES, LANES), LANES)
    loads = [
        pltpu.make_async_copy(
            near_all.at[everything + (pl.ds(0, cut), lanes)], weight_s, local_sem.at[3]
        ),
        pltpu.make_async_copy(
            near_all.at[everything + (pl.ds(cut, up_s.shape[-2]), lanes)], up_s, local_sem.at[4]
        ),
    ]
    for copy in loads:
        copy.start()
    for copy in loads:
        copy.wait()

    def of_shard(ref, rows):
        count = bits_of(shape["rows"])

        def get(e):
            bits = [(e >> bit) & 1 for axis, bit in lead if axis == "heads"]
            return ref[(slice(None),) * count + tuple(bits)].reshape(rows, LANES)

        return get

    def meanwhile(at):
        for p in range(parts):
            time = ready + 1 + 2 * p + at

            @pl.when(part == p)
            def _():
                exchanges.run(time)

    forward_body(
        groups, block, own, halo, ahead, meanwhile, of_shard(weight_s, D), of_shard(up_s, LAT),
        normed_ref, cos_ref, sin_ref, window_s, mixed_ref, log_ref, q_ref, query_s, top_s, sum_s,
    )

    @pl.when(part == parts - 1)
    def _():
        for time in range(ready + 1 + 2 * parts, exchanges.times + 1):
            exchanges.run(time)
        keep_window.wait()


def attend_gather(shape, groups, normed, latent, near, large, cos, sin, block, own, halo):
    rows, wide = own * block, (halo + own) * block
    cut, small = D // shape["rows"], LAT // shape["rows"]
    once = pl.Buffered(1)
    first = cut + small
    plan = exchange_plan(0, 0, 0, first, 2)
    ready = max(item[0] for item in plan) + len(leading(shape))
    plan = plan + exchange_plan(2, 1, 0, large.shape[0], CHUNKS)
    plan = plan + exchange_plan(1 + CHUNKS, 0, first, near.shape[0] - first, 1)
    count = len(plan) * len(leading(shape))
    twos = (2,) * len(leading(shape))
    anywhere = pl.BlockSpec(memory_space=pl.ANY)
    outside = pl.BlockSpec(memory_space=pltpu.HBM)

    def whole(shape):
        return pl.BlockSpec(shape, lambda g: (0,) * len(shape), pipeline_mode=once)

    mixed, logs, queries, near_all, large_all, window = pl.pallas_call(
        functools.partial(attend_gather_kernel, shape, plan, ready, groups, block, own, halo),
        grid=(HEADS // GROUP,),
        in_specs=[
            whole((rows, D)),
            whole((rows, LANES)),
            whole((rows, LANES)),
            whole(latent.shape),
            anywhere,
            anywhere,
        ],
        out_specs=[
            pl.BlockSpec((None, GROUP * HD, rows), lambda g: (g, 0, 0)),
            pl.BlockSpec((None, GROUP, 1, rows), lambda g: (g, 0, 0, 0)),
            pl.BlockSpec((None, rows, GROUP * LANES), lambda g: (g, 0, 0)),
            outside,
            outside,
            outside,
        ],
        out_shape=[
            jax.ShapeDtypeStruct((HEADS // GROUP, GROUP * HD, rows), bf16),
            jax.ShapeDtypeStruct((HEADS // GROUP, GROUP, 1, rows), f32),
            jax.ShapeDtypeStruct((HEADS // GROUP, rows, GROUP * LANES), bf16),
            jax.ShapeDtypeStruct(twos + near.shape, bf16),
            jax.ShapeDtypeStruct(twos + large.shape, bf16),
            jax.ShapeDtypeStruct((wide, latent.shape[1]), bf16),
        ],
        scratch_shapes=[
            pltpu.VMEM((GROUP, LANES, rows), bf16),
            pltpu.VMEM((GROUP, 1, rows), f32),
            pltpu.VMEM((GROUP, TALL, rows), f32),
            pltpu.VMEM((wide, latent.shape[1]), bf16),
            pltpu.VMEM(twos + (cut, LANES), bf16),
            pltpu.VMEM(twos + (small, LANES), bf16),
            pltpu.SemaphoreType.DMA((5,)),
            pltpu.SemaphoreType.DMA((halo,)),
            pltpu.SemaphoreType.DMA((halo,)),
            pltpu.SemaphoreType.DMA((count,)),
            pltpu.SemaphoreType.DMA((count,)),
        ],
        compiler_params=pltpu.CompilerParams(
            collective_id=0, has_side_effects=True, vmem_limit_bytes=60 << 20
        ),
        name="attend_gather",
    )(normed, cos, sin, latent, near, large)
    full = (shape["rows"], shape["heads"])
    return (mixed, logs, queries), near_all.reshape(full + near.shape), large_all.reshape(full + large.shape), window


def feed_kernel(
    cuts, shards, units, side_ref, normed_ref, cotangent_ref, token_ref, weight_ref, out_ref, dnormed_ref,
    kept_ref, sent_ref,
):
    def whole(which):
        return jnp.concatenate(
            [
                jnp.concatenate(
                    [weight_ref[q, t, which * units : (which + 1) * units, :] for q in range(cuts)],
                    axis=1,
                )
                for t in range(shards)
            ],
            axis=0,
        )

    wide = D // cuts
    side = side_ref[0]

    def put(which, grad):
        at = slice(which * units, (which + 1) * units)
        for t in range(shards):
            rows = slice(t * units, (t + 1) * units)
            for q in range(cuts // 2):
                even = grad[rows, 2 * q * wide : (2 * q + 1) * wide].astype(bf16)
                odd = grad[rows, (2 * q + 1) * wide : (2 * q + 2) * wide].astype(bf16)
                kept_ref[q, t, at, :] = jnp.where(side == 0, even, odd)
                sent_ref[q, t, at, :] = jnp.where(side == 0, odd, even)

    @pl.when(pl.program_id(0) == 0)
    def _():
        out_ref[...] = jnp.zeros_like(out_ref)
        dnormed_ref[...] = jnp.zeros_like(dnormed_ref)

    normed = normed_ref[...]
    grad = (cotangent_ref[...].astype(f32) * token_ref[...]).astype(bf16)
    w_gate, w_up, w_down = whole(0), whole(1), whole(2)
    gate = dot_nt(w_gate, normed)
    upper = dot_nt(w_up, normed)
    grad_inner = dot_nt(w_down, grad)
    sig = jax.nn.sigmoid(gate)
    silu = gate * sig
    inner = (silu * upper).astype(bf16)
    grad_gate = (grad_inner * upper * sig * (1.0 + gate * (1.0 - sig))).astype(bf16)
    grad_upper = (grad_inner * silu).astype(bf16)
    out_ref[...] += dot_tn(inner, w_down)
    dnormed_ref[...] += dot_tn(grad_gate, w_gate)
    dnormed_ref[...] += dot_tn(grad_upper, w_up)
    put(0, dot_nn(grad_gate, normed))
    put(1, dot_nn(grad_upper, normed))
    put(2, dot_nn(inner, grad))


def feed_forward_both(side, normed, cotangent, token_weight, weights, units):
    rows = normed.shape[0]
    cuts, pieces, _, wide = weights.shape
    shards = max(1, min(pieces, 704 // units))
    once = pl.Buffered(1)
    half = (cuts // 2, shards, 3 * units, wide)
    whole = pl.BlockSpec((rows, D), lambda f, s: (0, 0), pipeline_mode=once)
    return pl.pallas_call(
        functools.partial(feed_kernel, cuts, shards, units),
        grid_spec=pltpu.PrefetchScalarGridSpec(
            num_scalar_prefetch=1,
            grid=(pieces // shards,),
            in_specs=[
                whole,
                whole,
                pl.BlockSpec((rows, 1), lambda f, s: (0, 0), pipeline_mode=once),
                pl.BlockSpec((cuts, shards, 3 * units, wide), lambda f, s: (0, f, 0, 0)),
            ],
            out_specs=[
                whole,
                whole,
                pl.BlockSpec(half, lambda f, s: (0, f, 0, 0)),
                pl.BlockSpec(half, lambda f, s: (0, f, 0, 0)),
            ],
        ),
        out_shape=[
            jax.ShapeDtypeStruct((rows, D), f32),
            jax.ShapeDtypeStruct((rows, D), f32),
            jax.ShapeDtypeStruct((cuts // 2, pieces, 3 * units, wide), bf16),
            jax.ShapeDtypeStruct((cuts // 2, pieces, 3 * units, wide), bf16),
        ],
        compiler_params=pltpu.CompilerParams(vmem_limit_bytes=60 << 20),
        cost_estimate=pl.CostEstimate(
            flops=40 * 10**9, bytes_accessed=50 * 10**6, transcendentals=0
        ),
        name="feed_forward_both",
    )(side, normed, cotangent, token_weight, weights)


def scatter_orders(shape):
    return [order[::-1] for order in gather_orders(shape)]


class Scatter:

    def __init__(self, shape, order, array, started=None):
        self.shape = shape
        self.order = list(scatter_orders(shape)[order])
        self.lead = leading(shape)
        self.terms = [array]
        if started is not None:
            self.order.pop(0)
            self.lead.remove(("rows", 0))
            self.terms = [array, started]
        self.terms = [t.reshape((2,) * len(self.lead) + t.shape[2:]) for t in self.terms]

    def total(self, terms):
        if len(terms) == 1:
            return terms[0]
        return sum(t.astype(f32) for t in terms).astype(bf16)

    def view(self):
        at = self.lead.index(self.order[0])
        before, after = 2**at, 2 ** (len(self.lead) - 1 - at)
        return before, after, [
            t.reshape((before, 2, after) + t.shape[len(self.lead) :]) for t in self.terms
        ]

    def halves(self):
        axis, bit = self.order[0]
        at = self.lead.index((axis, bit))
        upper = upper_bit(axis, bit)

        def half(which):
            return self.total(
                [lax.dynamic_index_in_dim(t, which, at, keepdims=False) for t in self.terms]
            )

        return half(upper), half(1 - upper)

    def send(self, kept, sent):
        axis, bit = self.order.pop(0)
        self.lead.remove((axis, bit))
        self.terms = [kept, lax.ppermute(sent, axis, bit_pairs(self.shape[axis], bit))]

    def left(self):
        perm = [self.lead.index(item) for item in self.order]
        array = self.total(self.terms)
        array = array.transpose(perm + list(range(len(perm), array.ndim)))
        return array.reshape((2 ** len(perm),) + array.shape[len(perm) :])


def fold_kernel(counts, side_ref, *refs):
    refs = list(refs)
    ins = [[refs.pop(0) for _ in range(2 * count)] for count in counts]
    for terms in ins:
        half = len(terms) // 2
        for part in (terms[:half], terms[half:]):
            total = part[0][...].astype(f32)
            for term in part[1:]:
                total = total + term[...].astype(f32)
            refs.pop(0)[...] = total.astype(bf16)


def fold(scatters, blocks):
    sides = jnp.stack([upper_bit(*scatter.order[0]) for scatter in scatters]).astype(jnp.int32)
    ins, in_specs, out_specs, out_shape, steps = [], [], [], [], None
    for i, (scatter, (row_block, rows)) in enumerate(zip(scatters, blocks)):
        before, after, terms = scatter.view()
        steps = before * after
        columns = terms[0].shape[4]
        for other in (0, 1):
            spec = pl.BlockSpec(
                (None, None, None, rows, columns),
                lambda g, s, i=i, after=after, other=other, row_block=row_block: (
                    g // after, s[i] * (1 - 2 * other) + other, g % after, row_block, 0
                ),
            )
            in_specs += [spec] * len(terms)
            ins += terms
            out_specs.append(pl.BlockSpec((None, rows, columns), lambda g, s: (g, 0, 0)))
            out_shape.append(jax.ShapeDtypeStruct((steps, rows, columns), bf16))
    outs = pl.pallas_call(
        functools.partial(fold_kernel, [len(scatter.terms) for scatter in scatters]),
        grid_spec=pltpu.PrefetchScalarGridSpec(
            num_scalar_prefetch=1, grid=(steps,), in_specs=in_specs, out_specs=out_specs
        ),
        out_shape=out_shape,
        name="fold",
    )(sides, *ins)
    twos = [(2,) * (len(scatter.lead) - 1) for scatter in scatters for _ in (0, 1)]
    outs = [out.reshape(two + out.shape[1:]) for two, out in zip(twos, outs)]
    return list(zip(outs[::2], outs[1::2]))


def step_all(scatters, tied, folded=0, blocks=()):
    halves = fold(scatters[:folded], blocks) if folded else []
    halves = halves + [scatter.halves() for scatter in scatters[folded:]]
    sent, tied = lax.optimization_barrier(([half[1] for half in halves], tied))
    for scatter, half, out in zip(scatters, halves, sent):
        scatter.send(half[0], out)
    return tied


def scatter_kernel(shape, orders, *refs):
    count = len(orders)
    arrays, outs = refs[:count], refs[count : 2 * count]
    scratch, (send_sem, recv_sem) = list(refs[2 * count : -2]), refs[-2:]
    index = {"rows": lax.axis_index("rows"), "heads": lax.axis_index("heads")}
    start_barrier(shape)
    held, flying = list(arrays), [None] * count
    semaphore = 0
    for stage in range(max(len(order) for order in orders) + 1):
        for i, order in enumerate(orders):
            if flying[i] is not None:
                copy, kept, landed, begin, half = flying[i]
                copy.wait()
                flying[i] = None
                if stage < len(order):
                    summed = scratch.pop(0)

                    def add(at, _):
                        both = kept[begin + at].astype(f32) + landed[at].astype(f32)
                        summed[at] = both.astype(bf16)
                        return 0

                    lax.fori_loop(0, half, add, 0)
                    held[i] = summed
                else:
                    outs[i][...] = kept[begin].astype(f32) + landed[0].astype(f32)
            if stage < len(order):
                axis, bit = order[stage]
                upper = lax.rem(index[axis] // (1 << bit), 2)
                half = held[i].shape[0] // 2
                landed = scratch.pop(0)
                copy = pltpu.make_async_remote_copy(
                    src_ref=held[i].at[pl.ds((1 - upper) * half, half)],
                    dst_ref=landed,
                    send_sem=send_sem.at[semaphore],
                    recv_sem=recv_sem.at[semaphore],
                    device_id={axis: flip(index[axis], bit)},
                    device_id_type=pl.DeviceIdType.MESH,
                )
                copy.start()
                flying[i] = (copy, held[i], landed, upper * half, half)
                semaphore += 1


def scatter_rest(shape, scatters):
    orders = [tuple(scatter.order) for scatter in scatters]
    arrays = [scatter.left() for scatter in scatters]
    scratch = []
    for stage in range(max(len(order) for order in orders) + 1):
        for order, array in zip(orders, arrays):
            tail = array.shape[1:]
            if 0 < stage < len(order):
                scratch.append(pltpu.VMEM((array.shape[0] >> stage,) + tail, bf16))
            if stage < len(order):
                scratch.append(pltpu.VMEM((array.shape[0] >> (stage + 1),) + tail, bf16))
    total = sum(len(order) for order in orders)
    inside = pl.BlockSpec(memory_space=pltpu.VMEM)
    return pl.pallas_call(
        functools.partial(scatter_kernel, shape, orders),
        in_specs=[inside] * len(arrays),
        out_specs=[inside] * len(arrays),
        out_shape=[jax.ShapeDtypeStruct(array.shape[1:], f32) for array in arrays],
        scratch_shapes=scratch
        + [pltpu.SemaphoreType.DMA((total,)), pltpu.SemaphoreType.DMA((total,))],
        compiler_params=pltpu.CompilerParams(
            collective_id=1, has_side_effects=True, vmem_limit_bytes=48 << 20
        ),
        name="scatter_rest",
    )(*arrays)


def on_device(
    shape,
    tokens,
    cotangent,
    domain,
    group_weight,
    gain_attn,
    w_query,
    w_query_rope,
    w_latent,
    w_key_rope,
    w_key_up,
    w_value_up,
    w_out,
    gain_mlp,
    w_gate,
    w_up,
    w_down,
):
    n_rows, n_heads = shape["rows"], shape["heads"]
    row_at, head_at = lax.axis_index("rows"), lax.axis_index("heads")
    local = tokens.shape[0]
    block = math.gcd(local, LEN)
    own, halo = local // block, LEN // block - 1
    here = w_query.shape[1] // HD
    units = w_gate.shape[1]
    cut = D // n_rows
    half = RD // 2

    head_of = [(i % n_heads) * here + i // n_heads for i in range(HEADS)]
    group_of = [head // GROUP for head in head_of]
    parts = [tuple(group_of[p * GROUP : (p + 1) * GROUP]) for p in range(HEADS // GROUP)]

    start = head_at * local
    positions = ((start + jnp.arange(local)) % LEN).astype(f32)
    frequency = THETA ** (-(jnp.arange(LANES) % half).astype(f32) / half)
    angles = positions[:, None] * frequency[None, :]
    cos, sin = jnp.cos(angles), jnp.sin(angles)
    ahead = start // block % (LEN // block)
    places = jnp.stack([ahead, jnp.minimum(LEN // block - ahead, own)]).astype(jnp.int32)

    gain_one, gain_two = gain_attn.reshape(1, D), gain_mlp.reshape(1, D)
    normed, latent = prepare(tokens, gain_one, w_latent, w_key_rope.T, cos, sin)

    def halo_pairs(k):
        back = -(-k // own)
        needs = [i for i in range(n_heads) if (i * local % LEN) // block >= k]
        return [(i - back, i) for i in needs]

    direct = cut % LANES == 0 and GROUP % n_heads == 0
    if direct:
        near, large = pack(
            row_at.astype(jnp.int32).reshape(1),
            n_rows, w_query, w_query_rope.T, w_key_up, w_value_up, w_out, w_gate.T, w_up.T, w_down,
        )
        forward, near, large, window = attend_gather(
            shape, parts[0], normed, latent, near, large, cos, sin, block, own, halo
        )
        out, base = near, (D + LAT) // n_rows
    else:
        pieces = []
        for k in range(halo, 0, -1):
            at = own - 1 - (k - 1) % own
            pieces.append(
                lax.ppermute(latent[at * block : (at + 1) * block], "heads", halo_pairs(k))
            )
        window = jnp.concatenate(pieces + [latent], axis=0)
        queries = jnp.concatenate(
            [
                w_query.reshape(D, here, HD),
                w_query_rope.reshape(D, here, RD),
                jnp.zeros((D, here, LANES - HD - RD), bf16),
            ],
            axis=2,
        ).reshape(n_rows, cut, here * LANES)
        ups = jnp.concatenate(
            [w_key_up.reshape(LAT, here, HD), w_value_up.reshape(LAT, here, HD)], axis=2
        ).reshape(n_rows, LAT // n_rows, here * LANES)
        near = jnp.concatenate([queries, ups], axis=1)
        near = lax.all_gather(near, "heads", axis=1)
        out, base = lax.all_gather(w_out, "heads", axis=0)[None], 0
        large = jnp.concatenate([w_gate.T, w_up.T, w_down], axis=0)
        large = lax.all_gather(large, "heads", axis=0).reshape(n_heads, 3 * units, 2, D // 2)
        large = large.transpose(2, 0, 1, 3)
        forward = [
            attend_forward(p, groups, places, normed, near, cos, sin, window, block, own, halo)
            for p, groups in enumerate(parts)
        ]
        forward = [jnp.stack(arrays) for arrays in zip(*forward)]
    mixed = forward[0]
    hidden, normed_mlp = join(tokens, gain_two, mixed, out, base)

    seq_weights = jnp.sum(
        (domain[:, None] == jnp.arange(group_weight.shape[0])[None, :]).astype(f32)
        * group_weight[None, :],
        axis=1,
    )
    token_seq = (start + jnp.arange(local)) // LEN
    token_weight = jnp.sum(
        (token_seq[:, None] == jnp.arange(domain.shape[0])[None, :]).astype(f32)
        * seq_weights[None, :],
        axis=1,
    )[:, None]
    core = upper_bit("rows", 0)
    side = core if direct else jnp.zeros_like(core)
    feed_out, grad_normed_mlp, feed_kept, feed_sent = feed_forward_both(
        side.astype(jnp.int32).reshape(1), normed_mlp, cotangent, token_weight, large, units
    )
    if not direct:
        grad_feed = jnp.concatenate([feed_kept[0], feed_sent[0]], axis=2)
        grad_feed = grad_feed.reshape(n_heads, 3 * units, n_rows // 2, 2, cut)
        grad_feed = grad_feed.transpose(3, 2, 0, 1, 4)
        feed_kept = lax.dynamic_index_in_dim(grad_feed, core, 0, keepdims=False)
        feed_sent = lax.dynamic_index_in_dim(grad_feed, 1 - core, 0, keepdims=False)
    feed_got = lax.ppermute(feed_sent, "rows", bit_pairs(n_rows, 0))
    half_way = 3 * units // 2
    scatter_feed = [
        Scatter(shape, 0, feed_kept, feed_got),
        Scatter(shape, 1, feed_kept, feed_got),
    ]
    block_output, grad_hidden, grad_out, grad_gain_two, *grad_mixed = middle(
        hidden, feed_out, grad_normed_mlp, cotangent, token_weight, gain_two, mixed, out, base
    )
    if not direct:
        grad_out = grad_out.reshape(n_heads, here * HD, n_rows, cut).transpose(2, 0, 1, 3)

    by_part = GROUP % n_heads == 0
    scatter_near, pieces, before = [], [], None
    scatter_out = Scatter(shape, 0, grad_out)
    for p, groups in enumerate(parts):
        under_way = scatter_feed + ([scatter_out] + scatter_near if p else [])
        blocks = [(0, half_way), (0 if p else 1, half_way)]
        grad_mixed[p] = step_all(under_way, grad_mixed[p], 2, blocks)
        *before, grad_near = attend_backward(
            p, groups, places, forward, normed, near, cos, sin, window, grad_mixed[p], before,
            block, own, halo,
        )
        if by_part:
            scatter_near.append(Scatter(shape, 1, grad_near))
        else:
            pieces.append(grad_near)
    if not by_part:
        scatter_near.append(Scatter(shape, 1, jnp.concatenate(pieces, axis=1)))
    grad_window, grad_normed = before
    got = [
        lax.ppermute(
            grad_window[(halo - k) * block : (halo - k + 1) * block],
            "heads",
            [(b, a) for a, b in halo_pairs(k)],
        )
        for k in range(1, halo + 1)
    ]
    early = scatter_near[:-1] if by_part else scatter_near
    grad_normed = step_all(scatter_feed + [scatter_out] + early, grad_normed)
    grad_tokens, grad_latent, grad_gain_one = finish(
        grad_window, got, tokens, normed, grad_normed, grad_hidden, gain_one, w_latent, w_key_rope.T, cos, sin,
        block, own, halo,
    )
    gains = jnp.concatenate([grad_gain_one, grad_gain_two], axis=0).astype(bf16)
    gains = gains.reshape(2, n_rows, n_heads, -1).transpose(1, 2, 0, 3)
    gains = jnp.pad(gains, ((0, 0), (0, 0), (0, 14), (0, LANES - gains.shape[3])))
    grad_latent = grad_latent.reshape(n_rows, n_heads, D // (n_rows * n_heads), -1)
    own_first, own_second, own_out, own_latent, own_gain, *own_near = scatter_rest(
        shape,
        scatter_feed
        + [scatter_out, Scatter(shape, 0, grad_latent), Scatter(shape, 1, gains)]
        + scatter_near,
    )
    own_feed = jnp.concatenate([own_first, own_second], axis=0)
    own_near = jnp.concatenate(own_near, axis=1)
    own_query = own_near[:cut].reshape(cut, here, LANES)
    own_up = own_near[cut:].reshape(LAT // n_rows, here, LANES)
    at, gain_cut = LGROUPS * LAT, D // (n_rows * n_heads)
    return (
        block_output,
        grad_tokens,
        own_gain[0, :gain_cut],
        own_query[:, :, :HD].reshape(cut, here * HD),
        own_query[:, :, HD : HD + RD].reshape(cut, here * RD),
        own_latent[:, :at],
        own_latent[:, at + HD : at + HD + RD],
        own_up[:, :, :HD].reshape(LAT // n_rows, here * HD),
        own_up[:, :, HD:].reshape(LAT // n_rows, here * HD),
        own_out,
        own_gain[1, :gain_cut],
        own_feed[:units].T,
        own_feed[units : 2 * units].T,
        own_feed[2 * units :],
    )


def solution(mesh):
    in_specs = (
        P(("rows", "heads"), None),
        P(("rows", "heads"), None),
        P("rows"),
        P(),
        P(),
        P(None, "heads"),
        P(None, "heads"),
        P(),
        P(),
        P(None, "heads"),
        P(None, "heads"),
        P("heads", None),
        P(),
        P(None, "heads"),
        P(None, "heads"),
        P("heads", None),
    )
    out_specs = (
        P(("rows", "heads"), None),
        P(("rows", "heads"), None),
        P(("rows", "heads")),
        P("rows", "heads"),
        P("rows", "heads"),
        P(("rows", "heads"), None),
        P(("rows", "heads"), None),
        P("rows", "heads"),
        P("rows", "heads"),
        P("heads", "rows"),
        P(("rows", "heads")),
        P("rows", "heads"),
        P("rows", "heads"),
        P("heads", "rows"),
    )
    return jax.shard_map(
        functools.partial(on_device, dict(mesh.shape)),
        mesh=mesh,
        in_specs=in_specs,
        out_specs=out_specs,
        check_vma=False,
    )
```
